256 devices in a mesh: row: 16 (over y, x), col: 16 (over z, core).
Axes of the slice: x: 4, y: 4, z: 8, core: 2. Of those that a mesh axis runs over, the one named last changes fastest.
Arguments:
- external_field: float32 [3, 36, 8192], P(None, None, ('row', 'col')), may hold values from -6 to 6
- jitter: float32 [3, 8192], P(None, ('row', 'col')), may hold values from -0.3 to 0.3
- species: int32 [8192], P(('row', 'col')), may hold values from 0 to 3
- alpha_table: float32 [12, 4], replicated, may hold values from 0.1667 to 0.6667
- block_cell: int32 [256], replicated, may hold values from 0 to 255, as said below
- tile_map: int32 [256, 256], replicated, may hold values from 0 to 2, as said below
Outputs:
- dipoles: float32 [3, 36, 8192], P(None, None, ('row', 'col'))
- residual: float32 [3, 36, 8192], P(None, None, ('row', 'col'))
The draws below stay inside these ranges and needn't reach their ends.
Inputs may be any that keep to these rules, and one draw needn't show every extreme that they name: block_cell holds each cell number of the block grid exactly once. tile_map[a, b] is 0 where the cells of blocks a and b differ by more than 2 along some grid dimension; otherwise it is 1 where a <= b and 2 where a > b.
All inputs are finite; a program needn't handle non-finite values.
Results may differ from the reference program's by a relative error of at most 0.0003.
Values sent between devices are 32-bit elements; how exact they have to be, the bound alone decides.
No kernel may reach another device: no remote copies, remote signals or barrier semaphores. Data moves between devices by JAX's collectives and lax.ppermute only.
A program may use at most 64 MiB of HBM per device.

```python
import math
import jax
import jax.numpy as jnp
from jax import lax

ATOM_DEV = 32
FREQ = 12
FIELDS = 3
SPECIES = 4
ITERS = 2
REACH = 2
NRHS = 36
NBLK = 256
ATOMS = 8192


def grid_shape_drawn(number):
    exponent = number.bit_length() - 1
    along_x = (exponent + 2) // 3
    remaining = exponent - along_x
    along_y = (remaining + 1) // 2
    return (2 ** along_y, 2 ** (remaining - along_y))


def cell_order(key):
    return jax.random.permutation(key, jnp.arange(NBLK, dtype=jnp.int32)).astype(jnp.int32)


def draw_block_cell(key, part):
    return cell_order(key)


def draw_tile_map(key, part):
    cell_ids = cell_order(key)
    grid_y, grid_z = grid_shape_drawn(NBLK)
    coords = [cell_ids // (grid_y * grid_z), cell_ids // grid_z % grid_y, cell_ids % grid_z]
    distant = jnp.zeros((NBLK, NBLK), dtype=bool)
    for coord in coords:
        distant = distant | (jnp.abs(coord[:, None] - coord[None, :]) > REACH)
    block_ids = jnp.arange(NBLK, dtype=jnp.int32)
    upper = block_ids[:, None] <= block_ids[None, :]
    return jnp.where(distant, 0, jnp.where(upper, 1, 2)).astype(jnp.int32)


def place_ends(entries, key, smallest, largest):
    longest = entries.shape.index(max(entries.shape))
    spots = []
    for shift in (0, 1):
        where = [jax.random.randint(jax.random.fold_in(key, axis), (), 0, length) for axis, length in enumerate(entries.shape)]
        where[longest] = (where[longest] + shift) % entries.shape[longest]
        spots.append(tuple(where))
    return entries.at[spots[0]].set(smallest).at[spots[1]].set(largest)


def shard_levels(key, dims, cuts, smallest, top_value):
    loudness = 1.0
    for position, shards_of in cuts:
        heights = jax.random.uniform(jax.random.fold_in(jax.random.fold_in(key, 6), position), (shards_of,), jnp.float32, smallest / len(cuts), top_value / len(cuts))
        loudness = loudness * jnp.repeat(jnp.exp(heights), dims[position] // shards_of).reshape((-1,) + (1,) * (len(dims) - 1 - position))
    return loudness


def gaussian(own_key, dims, scale, most, cuts=(), kind=jnp.bfloat16):
    drawn = scale * jax.random.normal(own_key, dims, jnp.float32)
    if cuts:
        drawn = drawn * shard_levels(own_key, dims, cuts, -0.22, 0.18)
    return jnp.clip(drawn, -most, most).astype(kind)


def setup_inputs(seed: int = 0) -> dict:
    arg_keys = jax.random.split(jax.random.key(seed), 7)
    return {
        "external_field": gaussian(arg_keys[0], (3, NRHS, ATOMS), 1.0, 6.0, ((2, 256),), jnp.float32),
        "jitter": jnp.clip(jax.random.uniform(arg_keys[1], (3, ATOMS), jnp.float32, -0.3, 0.3) * shard_levels(arg_keys[1], (3, ATOMS), ((1, 256),), -0.4, 0.0), -0.3, 0.3),
        "species": place_ends(jax.random.randint(arg_keys[2], (ATOMS,), 0, SPECIES), jax.random.fold_in(arg_keys[2], 1), 0, SPECIES - 1).astype(jnp.int32),
        "alpha_table": jnp.clip(jnp.exp(jax.random.uniform(arg_keys[3], (FREQ, SPECIES), jnp.float32, math.log(0.1667), math.log(0.6667))), 0.1667, 0.6667),
        "block_cell": draw_block_cell(jax.random.fold_in(arg_keys[6], 71), 0),
        "tile_map": draw_tile_map(jax.random.fold_in(arg_keys[6], 71), 0),
    }


spacing = 2.0
radius = 2.4
steepness = 6.0

def grid_shape(number):
    exponent = number.bit_length() - 1
    along_x = (exponent + 2) // 3
    remaining = exponent - along_x
    along_y = (remaining + 1) // 2
    return (2 ** along_x, 2 ** along_y, 2 ** (remaining - along_y))

def lattice(cell_ids, atom_total, block_total):
    grid_x, grid_y, grid_z = grid_shape(block_total)
    sub_x, sub_y, sub_z = grid_shape(atom_total)
    local_ids = jnp.arange(atom_total, dtype=jnp.int32)[None, :]
    column = cell_ids[:, None]
    coord_x = column // (grid_y * grid_z) * sub_x + local_ids // (sub_y * sub_z)
    coord_y = column // grid_z % grid_y * sub_y + local_ids // sub_z % sub_y
    coord_z = column % grid_z * sub_z + local_ids % sub_z
    return jnp.stack([coord_x, coord_y, coord_z]).astype(jnp.float32) * spacing

def coupling(row_place, col_place, diagonal_flag):
    offset = row_place[:, :, None] - col_place[:, None, :]
    atom_total = row_place.shape[1]
    rows_iota = lax.broadcasted_iota(jnp.int32, (atom_total, atom_total), 0)
    cols_iota = lax.broadcasted_iota(jnp.int32, (atom_total, atom_total), 1)
    self_mask = (rows_iota == cols_iota).astype(jnp.float32) * diagonal_flag
    distance2 = lax.optimization_barrier(jnp.sum(offset * offset, axis=0)) + self_mask
    inverse = lax.rsqrt(distance2)
    damping = 1.0 / (1.0 + jnp.exp(-steepness * (distance2 * inverse / radius - 1.0)))
    weight = damping * inverse ** 5 * (1.0 - self_mask)
    products = offset[:, None] * offset[None, :]
    identity = jnp.eye(3, dtype=jnp.float32)[:, :, None, None]
    return weight * (identity * distance2 - 3.0 * products)

def reference(external_field, jitter, species, alpha_table, block_cell, tile_map):
    atom_sites = lattice(block_cell, ATOM_DEV, NBLK).reshape(3, ATOMS) + jitter
    site_blocks = atom_sites.reshape(3, NBLK, ATOM_DEV).transpose(1, 0, 2)
    inv_table = 1.0 / alpha_table
    inv_diag = jnp.repeat(inv_table[:, species], FIELDS, axis=0)
    block_ids = jnp.arange(NBLK, dtype=jnp.int32)

    def apply_matrix(vector):
        vec_blocks = vector.reshape(3, NRHS, NBLK, ATOM_DEV).transpose(2, 0, 1, 3)

        def row_pass(row_block):

            def visit(running, col_block):

                def accumulate(running):
                    diagonal_flag = (row_block == col_block).astype(jnp.float32)
                    tile = coupling(site_blocks[row_block], site_blocks[col_block], diagonal_flag)
                    return running + jnp.einsum('kluv,lrv->kru', tile, vec_blocks[col_block], precision=lax.Precision.HIGHEST)

                def keep(running):
                    return running
                return (lax.cond(tile_map[row_block, col_block] != 0, accumulate, keep, running), None)
            running, unused = lax.scan(visit, jnp.zeros((3, NRHS, ATOM_DEV), jnp.float32), block_ids)
            return running
        coupled = lax.map(row_pass, block_ids)
        return inv_diag[None] * vector + coupled.transpose(1, 2, 0, 3).reshape(3, NRHS, ATOMS)
    dipoles = jnp.zeros_like(external_field)
    residual = external_field
    direction = external_field
    squares = lax.optimization_barrier(jnp.sum(residual * residual, axis=(0, 2)))
    for iteration in range(ITERS):
        mapped = apply_matrix(direction)
        step_size = squares / lax.optimization_barrier(jnp.sum(direction * mapped, axis=(0, 2)))
        dipoles = dipoles + step_size[None, :, None] * direction
        residual = residual - step_size[None, :, None] * mapped
        squares_next = lax.optimization_barrier(jnp.sum(residual * residual, axis=(0, 2)))
        direction = residual + (squares_next / squares)[None, :, None] * direction
        squares = squares_next
    return (dipoles, residual)
```

```python
import jax
import jax.numpy as jnp
from jax import lax
from jax.experimental import pallas as pl
from jax.experimental.pallas import tpu as pltpu
from jax.sharding import PartitionSpec as P

COMPS = 3
RHS = 36
ATOMS = 32
GROUP = 16
LANES = 128
SUMS = 8
SITE = 120
WIDE = GROUP * ATOMS
PAIRS = 5
SPACING = 2.0
F32 = jnp.float32
BF16 = jnp.bfloat16

VMEM = pl.BlockSpec(memory_space=pltpu.VMEM)
SMEM = pl.BlockSpec(memory_space=pltpu.SMEM)
PARAMS = pltpu.CompilerParams(vmem_limit_bytes=40 * 1024 * 1024)


def lane_ids(rows):
    return lax.broadcasted_iota(jnp.int32, (rows, LANES), 1)


def component_lanes(rows):
    lanes = lane_ids(rows)
    first = lanes < RHS
    second = (lanes >= RHS) & (lanes < 2 * RHS)
    third = (lanes >= 2 * RHS) & (lanes < COMPS * RHS)
    return first, second, third


def sum_components(value):
    first, second, third = component_lanes(SUMS)
    up = pltpu.roll(value, RHS, 1)
    up2 = pltpu.roll(value, 2 * RHS, 1)
    down = pltpu.roll(value, LANES - RHS, 1)
    down2 = pltpu.roll(value, LANES - 2 * RHS, 1)
    of_first = value + down + down2
    of_second = up + value + down
    of_third = up2 + up + value
    return jnp.where(first, of_first, jnp.where(second, of_second, jnp.where(third, of_third, 1.0)))


def prepare_kernel(ids, block_cell, species, alpha, field, jitter, vec_out, site_out, aux_out, work):
    lane = lax.broadcasted_iota(jnp.int32, (1, LANES), 1)
    rhs_lane = jnp.where(lane >= 2 * RHS, lane - 2 * RHS, jnp.where(lane >= RHS, lane - RHS, lane))
    inverse = []
    for kind in range(4):
        row = jnp.ones((1, LANES), F32)
        for freq in range(12):
            row = jnp.where((rhs_lane >= 3 * freq) & (rhs_lane < 3 * freq + 3), alpha[freq, kind], row)
        inverse.append(1.0 / row)
    shift = 0.25 * ((inverse[0] + inverse[1]) + (inverse[2] + inverse[3]))
    row_iota = lax.broadcasted_iota(jnp.int32, (ATOMS, LANES), 0)
    kinds = jnp.zeros((ATOMS, LANES), jnp.int32)
    for atom in range(ATOMS):
        kinds = jnp.where(row_iota == atom, species[atom], kinds)
    diag = jnp.zeros((ATOMS, LANES), F32)
    for kind in range(4):
        diag = jnp.where(kinds == kind, inverse[kind] - shift, diag)
    aux_out[0:ATOMS, :] = diag
    aux_out[ATOMS : ATOMS + SUMS, :] = jnp.broadcast_to(shift, (SUMS, LANES))

    cell = block_cell[ids[0] * GROUP + ids[1]]
    cell_x = cell // 32
    cell_y = (cell // 4) % 8
    cell_z = cell % 4
    atom = lax.broadcasted_iota(jnp.int32, (1, ATOMS), 1)
    place_x = cell_x * 4 + atom // 8
    place_y = cell_y * 4 + (atom // 2) % 4
    place_z = cell_z * 2 + atom % 2
    work[...] = jnp.zeros_like(work)
    for comp in range(COMPS):
        work[comp * RHS : (comp + 1) * RHS, 0:ATOMS] = field[comp]
    for comp, place in enumerate((place_x, place_y, place_z)):
        work[SITE + comp : SITE + comp + 1, 0:ATOMS] = (
            place.astype(F32) * SPACING + jitter[comp : comp + 1, :]
        )
    turned = work[...].T[0:ATOMS, :]
    sites = work[SITE : SITE + SUMS, :]
    for slot in range(GROUP):
        vec_out[slot] = turned
        site_out[slot] = sites


def right_side(vectors, side):
    first, second, third = component_lanes(WIDE)
    zero = jnp.zeros_like(vectors)
    up = pltpu.roll(vectors, RHS, 1)
    up2 = pltpu.roll(vectors, 2 * RHS, 1)
    down = pltpu.roll(vectors, LANES - RHS, 1)
    down2 = pltpu.roll(vectors, LANES - 2 * RHS, 1)
    parts = (
        jnp.where(first, vectors, jnp.where(third, -vectors, zero)),
        jnp.where(second, vectors, jnp.where(third, -vectors, zero)),
        jnp.where(first, down, jnp.where(second, up, zero)),
        jnp.where(first, down2, jnp.where(third, up2, zero)),
        jnp.where(second, down, jnp.where(third, up, zero)),
    )
    for slot, part in enumerate(parts):
        high = part.astype(BF16)
        low = (part - high.astype(F32)).astype(BF16)
        side[slot * WIDE : (slot + 1) * WIDE, 0:LANES] = high
        side[slot * WIDE : (slot + 1) * WIDE, LANES : 2 * LANES] = low


def product(high, low, side):
    both = jnp.dot(high[...], side[...], preferred_element_type=F32)
    rest = jnp.dot(low[...], side[:, 0:LANES], preferred_element_type=F32)
    return both[:, 0:LANES] + (both[:, LANES:] + rest)


def first_kernel(ids, tile_map, vectors, sites, part_out, high, low, side, column, mask):
    wide = vectors[...].reshape(WIDE, LANES)
    right_side(wide, side)
    across = wide.T[SITE : SITE + SUMS, :]
    across_x, across_y, across_z = across[0:1, :], across[1:2, :], across[2:3, :]
    down = sites[...].reshape(GROUP * SUMS, LANES).T[0:ATOMS, :]
    for block in range(GROUP):
        for comp in range(COMPS):
            lane = block * SUMS + comp
            column[comp, block * ATOMS : (block + 1) * ATOMS, :] = jnp.broadcast_to(
                down[:, lane : lane + 1], (ATOMS, LANES)
            )
    active = jnp.where(tile_map[pl.ds(pl.multiple_of(ids[0] * GROUP, GROUP), GROUP), :] != 0, 1.0, 0.0)
    block_row = lax.broadcasted_iota(jnp.int32, (GROUP * GROUP, WIDE), 0)
    block_col = lax.broadcasted_iota(jnp.int32, (GROUP * GROUP, WIDE), 1) // ATOMS * GROUP + ids[1]
    select = jnp.where(block_row == block_col, 1.0, 0.0).astype(BF16)
    mask[...] = jnp.dot(active.astype(BF16), select, preferred_element_type=F32)

    def build(step, carry):
        rows = pl.ds(pl.multiple_of(step * 16, 16), 16)
        here_x, here_y, here_z = column[0, rows, :], column[1, rows, :], column[2, rows, :]
        keep = mask[pl.ds(step // 2, 1), :]
        for tile in range(WIDE // LANES):
            lanes = slice(tile * LANES, (tile + 1) * LANES)
            dx = here_x - across_x[:, lanes]
            dy = here_y - across_y[:, lanes]
            dz = here_z - across_z[:, lanes]
            xx = dx * dx
            yy = dy * dy
            distance2 = xx + yy + dz * dz
            square = jnp.maximum(distance2, 1.0)
            inverse = lax.rsqrt(square)
            damping = 1.0 / (1.0 + jnp.exp(6.0 - 2.5 * (square * inverse)))
            inverse2 = inverse * inverse
            weight = damping * (inverse2 * inverse2 * inverse) * keep[:, lanes]
            weight = jnp.where(distance2 > 0.5, weight, 0.0)
            radial = weight * square
            minus3 = -3.0 * weight
            along_x = minus3 * dx
            along_y = minus3 * dy
            entries = (
                radial + minus3 * xx,
                radial + minus3 * yy,
                along_x * dy,
                along_x * dz,
                along_y * dz,
            )
            for slot, entry in enumerate(entries):
                top = entry.astype(BF16)
                at = slice(slot * WIDE + tile * LANES, slot * WIDE + (tile + 1) * LANES)
                high[rows, at] = top
                low[rows, at] = (entry - top.astype(F32)).astype(BF16)
        return carry

    lax.fori_loop(0, WIDE // 16, build, 0)
    part_out[...] = product(high, low, side).reshape(GROUP, ATOMS, LANES)


def shifted_kernel(parts, own, aux, out):
    coupled = jnp.sum(parts[...], axis=0)
    vector = jnp.where(lane_ids(ATOMS) < COMPS * RHS, own[0], 0.0)
    mapped = aux[0:ATOMS, :] * vector + coupled
    out_rows = jnp.zeros((SUMS, LANES), F32)
    row = lax.broadcasted_iota(jnp.int32, (SUMS, LANES), 0)
    for slot, terms in enumerate((vector * vector, vector * mapped, mapped * mapped)):
        out_rows = jnp.where(row == slot, jnp.sum(terms, axis=0, keepdims=True), out_rows)
    for slot in range(GROUP):
        out[slot, 0:ATOMS, :] = mapped
        out[slot, ATOMS:, :] = out_rows


def second_kernel(gathered, high, low, part_out, side):
    right_side(gathered[:, 0:ATOMS, :].reshape(WIDE, LANES), side)
    part_out[:, 0:ATOMS, :] = product(high, low, side).reshape(GROUP, ATOMS, LANES)
    sums = jnp.sum(gathered[:, ATOMS:, :], axis=0)
    for slot in range(GROUP):
        part_out[slot, ATOMS:, :] = sums


def step_kernel(parts, own, shifted, aux, sums_out, state):
    total = jnp.sum(parts[...], axis=0)
    inside = lane_ids(ATOMS) < COMPS * RHS
    vector = jnp.where(inside, own[0], 0.0)
    mapped = shifted[0, 0:ATOMS, :]
    twice = aux[0:ATOMS, :] * mapped + total[0:ATOMS, :]
    sums = sum_components(total[ATOMS:, :])
    bb, be, ee = sums[0:1, :], sums[1:2, :], sums[2:3, :]
    shift = aux[ATOMS : ATOMS + 1, :]
    bm = shift * bb + be
    step = bb / bm
    kept = be / bm
    beta = (bb * ee - be * be) / (bm * bm)
    residual = kept * vector - step * mapped
    direction = residual + beta * vector
    image = shift * direction + ((kept + beta) * mapped - step * twice)
    row = lax.broadcasted_iota(jnp.int32, (SUMS, LANES), 0)
    squares = jnp.sum(residual * residual, axis=0, keepdims=True)
    curvature = jnp.sum(direction * image, axis=0, keepdims=True)
    both = sum_components(jnp.where(row == 0, squares, jnp.where(row == 1, curvature, 0.0)))
    lane = lax.broadcasted_iota(jnp.int32, (1, LANES), 1)
    packed = jnp.where(lane < RHS, both[0:1, :], jnp.where(lane < 2 * RHS, both[1:2, :], 0.0))
    sums_out[...] = jnp.broadcast_to(packed.reshape(1, 1, LANES), sums_out.shape)
    state[0] = step * vector
    state[1] = direction
    state[2] = residual
    state[3] = image


def finish_kernel(gathered, state, dipoles, residual, work):
    total = jnp.broadcast_to(jnp.sum(gathered[...], axis=0), (SUMS, LANES))
    first, second, third = component_lanes(SUMS)
    up = pltpu.roll(total, RHS, 1)
    up2 = pltpu.roll(total, 2 * RHS, 1)
    down = pltpu.roll(total, LANES - RHS, 1)
    squares = jnp.where(first, total, jnp.where(second, up, up2))
    curvature = jnp.where(first, down, jnp.where(second, total, jnp.where(third, up, 1.0)))
    step = (squares / curvature)[0:1, :]
    for out, value in (
        (dipoles, state[0] + step * state[1]),
        (residual, state[2] - step * state[3]),
    ):
        work[0:ATOMS, :] = value
        turned = work[...].T
        for comp in range(COMPS):
            out[comp] = turned[comp * RHS : (comp + 1) * RHS, 0:ATOMS]


def shape(*dims, dtype=F32):
    return jax.ShapeDtypeStruct(dims, dtype)


def local(external_field, jitter, species, alpha_table, block_cell, tile_map):
    ids = jnp.stack([lax.axis_index("row"), lax.axis_index("col")]).astype(jnp.int32)
    vec, site, aux = pl.pallas_call(
        prepare_kernel,
        out_shape=(shape(GROUP, ATOMS, LANES), shape(GROUP, SUMS, LANES), shape(ATOMS + SUMS, LANES)),
        in_specs=[SMEM, SMEM, SMEM, SMEM, VMEM, VMEM],
        out_specs=(VMEM, VMEM, VMEM),
        scratch_shapes=[pltpu.VMEM((LANES, LANES), F32)],
        compiler_params=PARAMS,
        name="prepare",
    )(ids, block_cell, species, alpha_table, external_field, jitter)
    sites = lax.all_to_all(site, "col", 0, 0)
    vectors = lax.all_to_all(vec, "row", 0, 0)
    own_spec = pl.BlockSpec((1, ATOMS, LANES), lambda i: (0, 0, 0))

    def whole(*dims):
        return pl.BlockSpec(dims, lambda i: (0,) * len(dims))

    part, high, low = pl.pallas_call(
        first_kernel,
        out_shape=(
            shape(GROUP, ATOMS, LANES),
            shape(WIDE, PAIRS * WIDE, dtype=BF16),
            shape(WIDE, PAIRS * WIDE, dtype=BF16),
        ),
        in_specs=[SMEM, VMEM, VMEM, VMEM],
        out_specs=(VMEM, VMEM, VMEM),
        scratch_shapes=[
            pltpu.VMEM((PAIRS * WIDE, 2 * LANES), BF16),
            pltpu.VMEM((COMPS, WIDE, LANES), F32),
            pltpu.VMEM((GROUP, WIDE), F32),
        ],
        compiler_params=PARAMS,
        name="first",
    )(ids, tile_map, vectors, sites)
    parts = lax.all_to_all(part, "col", 0, 0)
    shifted = pl.pallas_call(
        shifted_kernel,
        grid=(1,),
        out_shape=shape(GROUP, ATOMS + SUMS, LANES),
        in_specs=[whole(GROUP, ATOMS, LANES), own_spec, whole(ATOMS + SUMS, LANES)],
        out_specs=whole(GROUP, ATOMS + SUMS, LANES),
        compiler_params=PARAMS,
        name="shifted",
    )(parts, vec, aux)
    gathered = lax.all_to_all(shifted, "row", 0, 0)
    part2 = pl.pallas_call(
        second_kernel,
        out_shape=shape(GROUP, ATOMS + SUMS, LANES),
        in_specs=[VMEM, VMEM, VMEM],
        out_specs=VMEM,
        scratch_shapes=[pltpu.VMEM((PAIRS * WIDE, 2 * LANES), BF16)],
        compiler_params=PARAMS,
        name="second",
    )(gathered, high, low)
    parts2 = lax.all_to_all(part2, "col", 0, 0)
    sums, state = pl.pallas_call(
        step_kernel,
        grid=(1,),
        out_shape=(shape(GROUP * GROUP, 1, LANES), shape(4, ATOMS, LANES)),
        in_specs=[
            whole(GROUP, ATOMS + SUMS, LANES),
            own_spec,
            pl.BlockSpec((1, ATOMS + SUMS, LANES), lambda i: (0, 0, 0)),
            whole(ATOMS + SUMS, LANES),
        ],
        out_specs=(whole(GROUP * GROUP, 1, LANES), whole(4, ATOMS, LANES)),
        compiler_params=PARAMS,
        name="step",
    )(parts2, vec, shifted, aux)
    all_sums = lax.all_to_all(sums, ("row", "col"), 0, 0)
    return pl.pallas_call(
        finish_kernel,
        out_shape=(shape(COMPS, RHS, ATOMS), shape(COMPS, RHS, ATOMS)),
        in_specs=[VMEM, VMEM],
        out_specs=(VMEM, VMEM),
        scratch_shapes=[pltpu.VMEM((LANES, LANES), F32)],
        compiler_params=PARAMS,
        name="finish",
    )(all_sums, state)


def solution(mesh):
    return jax.shard_map(
        local,
        mesh=mesh,
        in_specs=(
            P(None, None, ("row", "col")),
            P(None, ("row", "col")),
            P(("row", "col")),
            P(),
            P(),
            P(),
        ),
        out_specs=(P(None, None, ("row", "col")), P(None, None, ("row", "col"))),
        check_vma=False,
    )
```

```python
import jax
import jax.numpy as jnp
from jax import lax
from jax.experimental import pallas as pl
from jax.experimental.pallas import tpu as pltpu
from jax.sharding import PartitionSpec as P

COMPS = 3
RHS = 36
ATOMS = 32
GROUP = 16
HALF = 8
LANES = 128
SUMS = 8
SITE = 120
SUM_ROW = 104
WIDE = GROUP * ATOMS
NARROW = HALF * ATOMS
PAIRS = 5
SPACING = 2.0
F32 = jnp.float32
BF16 = jnp.bfloat16

VMEM = pl.BlockSpec(memory_space=pltpu.VMEM)
SMEM = pl.BlockSpec(memory_space=pltpu.SMEM)
HBM = pl.BlockSpec(memory_space=pltpu.HBM)
SQUARE = pltpu.VMEM((LANES, LANES), F32)
PARAMS = pltpu.CompilerParams(vmem_limit_bytes=40 * 1024 * 1024)


def lane_ids(rows):
    return lax.broadcasted_iota(jnp.int32, (rows, LANES), 1)


def component_lanes(rows):
    lanes = lane_ids(rows)
    first = lanes < RHS
    second = (lanes >= RHS) & (lanes < 2 * RHS)
    third = (lanes >= 2 * RHS) & (lanes < COMPS * RHS)
    return first, second, third


def sum_components(value):
    first, second, third = component_lanes(SUMS)
    up = pltpu.roll(value, RHS, 1)
    up2 = pltpu.roll(value, 2 * RHS, 1)
    down = pltpu.roll(value, LANES - RHS, 1)
    down2 = pltpu.roll(value, LANES - 2 * RHS, 1)
    of_first = value + down + down2
    of_second = up + value + down
    of_third = up2 + up + value
    return jnp.where(first, of_first, jnp.where(second, of_second, jnp.where(third, of_third, 1.0)))


def fetch(pairs, sems):
    copies = [pltpu.make_async_copy(source, target, sems.at[i]) for i, (source, target) in enumerate(pairs)]
    for copy in copies:
        copy.start()
    for copy in copies:
        copy.wait()


def prepare_kernel(ids, cells_hbm, field_hbm, jitter_hbm, vec_out, cells, field, jitter, work, wide, sems):
    fetch(((cells_hbm, cells), (field_hbm, field), (jitter_hbm, jitter)), sems)
    cell = cells[ids[0] * GROUP + ids[1]]
    work[...] = jnp.zeros_like(work)
    work[SITE : SITE + COMPS, 0:ATOMS] = block_sites(cell, jitter[...])
    wide[...] = work[...].T[0:ATOMS, :]
    for comp in range(COMPS):
        wide[:, comp * RHS : (comp + 1) * RHS] = field[comp]
    turned = wide[...]
    for slot in range(HALF):
        vec_out[slot] = turned


def block_sites(cell, jitter):
    comp = lax.broadcasted_iota(jnp.int32, (COMPS, ATOMS), 0)
    atom = lax.broadcasted_iota(jnp.int32, (COMPS, ATOMS), 1)
    inner = jnp.where(comp == 0, atom // 8, jnp.where(comp == 1, (atom // 2) % 4, atom % 2))
    corner = jnp.where(comp == 0, cell // 32 * 4, jnp.where(comp == 1, (cell // 4) % 8 * 4, cell % 4 * 2))
    return (corner + inner).astype(F32) * SPACING + jitter


def side_kernel(
    ids, species_hbm, alpha_hbm, tile_map_hbm, cells_hbm, jitters,
    aux_out, mask_out, column, species, alpha, tile_map, cells, work, sems
):
    fetch(
        ((species_hbm, species), (alpha_hbm, alpha), (tile_map_hbm, tile_map), (cells_hbm, cells)), sems
    )
    lane = lax.broadcasted_iota(jnp.int32, (4, LANES), 1)
    rhs_lane = jnp.where(lane >= 2 * RHS, lane - 2 * RHS, jnp.where(lane >= RHS, lane - RHS, lane))
    table = jnp.ones((4, LANES), F32)
    for freq in range(12):
        table = jnp.where(
            (rhs_lane >= 3 * freq) & (rhs_lane < 3 * freq + 3),
            jnp.broadcast_to(alpha[:, freq : freq + 1], (4, LANES)),
            table,
        )
    inverse = 1.0 / table
    shift = 0.25 * ((inverse[0:1] + inverse[1:2]) + (inverse[2:3] + inverse[3:4]))
    work[...] = jnp.zeros_like(work)
    work[0:1, 0:ATOMS] = species[...].astype(F32).reshape(1, ATOMS)
    kinds = jnp.broadcast_to(work[...].T[0:ATOMS, 0:1], (ATOMS, LANES))
    diag = jnp.zeros((ATOMS, LANES), F32)
    for kind in range(4):
        diag = jnp.where(kinds == float(kind), inverse[kind : kind + 1] - shift, diag)
    aux_out[0:ATOMS, :] = diag
    aux_out[ATOMS : ATOMS + SUMS, :] = jnp.broadcast_to(shift, (SUMS, LANES))

    blocks = GROUP * GROUP
    active = jnp.where(tile_map[...] != 0, 1.0, 0.0).astype(BF16)
    place = lax.broadcasted_iota(jnp.int32, (GROUP, blocks), 1)
    wanted = lax.broadcasted_iota(jnp.int32, (GROUP, blocks), 0) * GROUP + ids[1]
    pick = jnp.where(place == wanted, 1.0, 0.0).astype(BF16)
    lines = jnp.dot(pick, active, preferred_element_type=F32).astype(BF16)
    slot = lax.broadcasted_iota(jnp.int32, (blocks, WIDE), 1) // ATOMS
    wanted = ids[0] * GROUP + (slot % HALF) * 2 + ((ids[1] % 2) ^ (slot // HALF))
    place = lax.broadcasted_iota(jnp.int32, (blocks, WIDE), 0)
    spread = jnp.where(place == wanted, 1.0, 0.0).astype(BF16)
    mask_out[...] = 0.5 * jnp.dot(lines, spread, preferred_element_type=F32)

    work[...] = jnp.zeros_like(work)
    for slot in range(GROUP):
        cell = cells[slot * GROUP + ids[1]]
        work[slot * SUMS : slot * SUMS + COMPS, 0:ATOMS] = block_sites(cell, jitters[slot])
    down = work[...].T[0:ATOMS, :]
    for slot in range(GROUP):
        rows = slice(slot * ATOMS, (slot + 1) * ATOMS)
        for comp in range(COMPS):
            lane = slot * SUMS + comp
            column[comp, rows, :] = jnp.broadcast_to(down[:, lane : lane + 1], (ATOMS, LANES))


def right_side(vectors, side):
    first, second, third = component_lanes(NARROW)
    zero = jnp.zeros_like(vectors)
    up = pltpu.roll(vectors, RHS, 1)
    up2 = pltpu.roll(vectors, 2 * RHS, 1)
    down = pltpu.roll(vectors, LANES - RHS, 1)
    down2 = pltpu.roll(vectors, LANES - 2 * RHS, 1)
    parts = (
        jnp.where(first, vectors, jnp.where(third, -vectors, zero)),
        jnp.where(second, vectors, jnp.where(third, -vectors, zero)),
        jnp.where(first, down, jnp.where(second, up, zero)),
        jnp.where(first, down2, jnp.where(third, up2, zero)),
        jnp.where(second, down, jnp.where(third, up, zero)),
    )
    for slot, part in enumerate(parts):
        high = part.astype(BF16)
        low = (part - high.astype(F32)).astype(BF16)
        side[slot * NARROW : (slot + 1) * NARROW, 0:LANES] = high
        side[slot * NARROW : (slot + 1) * NARROW, LANES : 2 * LANES] = low


def product(high, low, side):
    both = jnp.dot(high[...], side[...], preferred_element_type=F32)
    rest = jnp.dot(low[...], side[:, 0:LANES], preferred_element_type=F32)
    return both[:, 0:LANES] + (both[:, LANES:] + rest)


def build(mask, vectors, column, high, low, first_lane):
    across = vectors.T[SITE : SITE + SUMS, :]
    across_x, across_y, across_z = across[0:1, :], across[1:2, :], across[2:3, :]

    def rows16(step, carry):
        rows = pl.ds(pl.multiple_of(step * 16, 16), 16)
        here_x, here_y, here_z = column[0, rows, :], column[1, rows, :], column[2, rows, :]
        keep = mask[pl.ds(step // 2, 1), :]
        for tile in range(NARROW // LANES):
            lanes = slice(tile * LANES, (tile + 1) * LANES)
            dx = here_x - across_x[:, lanes]
            dy = here_y - across_y[:, lanes]
            dz = here_z - across_z[:, lanes]
            xx = dx * dx
            yy = dy * dy
            distance2 = xx + yy + dz * dz
            square = jnp.maximum(distance2, 1.0)
            inverse = lax.rsqrt(square)
            damping = 1.0 + jnp.tanh(1.25 * (square * inverse) - 3.0)
            inverse2 = inverse * inverse
            kept = keep[:, first_lane + tile * LANES : first_lane + (tile + 1) * LANES]
            weight = damping * (inverse2 * inverse2 * inverse) * kept
            radial = weight * distance2
            minus3 = -3.0 * weight
            along_x = minus3 * dx
            along_y = minus3 * dy
            entries = (
                radial + minus3 * xx,
                radial + minus3 * yy,
                along_x * dy,
                along_x * dz,
                along_y * dz,
            )
            for slot, entry in enumerate(entries):
                top = entry.astype(BF16)
                at = slice(slot * NARROW + tile * LANES, slot * NARROW + (tile + 1) * LANES)
                high[rows, at] = top
                low[rows, at] = (entry - top.astype(F32)).astype(BF16)
        return carry

    lax.fori_loop(0, WIDE // 16, rows16, 0, unroll=4)


def first_own_kernel(mask, column, gathered, total, high, low, side):
    vectors = gathered[...].reshape(NARROW, LANES)
    right_side(vectors, side)
    build(mask, vectors, column, high, low, 0)
    total[...] = product(high, low, side)


def first_other_kernel(mask, column, gathered, total, part_out, high, low, side):
    vectors = gathered[...].reshape(NARROW, LANES)
    right_side(vectors, side)
    build(mask, vectors, column, high, low, NARROW)
    part_out[...] = (total[...] + product(high, low, side)).reshape(GROUP, ATOMS, LANES)


def spare_sums(vectors):
    return jnp.where(lane_ids(ATOMS) < COMPS * RHS, 0.0, jnp.sum(vectors, axis=0))


def second_own_kernel(gathered, high, low, total, side):
    vectors = gathered[...]
    right_side(vectors.reshape(NARROW, LANES), side)
    out = product(high, low, side).reshape(GROUP, ATOMS, LANES) + spare_sums(vectors)[None]
    total[...] = out


def second_other_kernel(gathered, high, low, total, part_out, side):
    vectors = gathered[...]
    right_side(vectors.reshape(NARROW, LANES), side)
    out = product(high, low, side).reshape(GROUP, ATOMS, LANES) + spare_sums(vectors)[None]
    part_out[...] = total[...] + out


def shifted_kernel(parts, own, aux, out, work):
    coupled = jnp.sum(parts[...], axis=0)
    inside = lane_ids(ATOMS) < COMPS * RHS
    vector = jnp.where(inside, own[0], 0.0)
    mapped = aux[0:ATOMS, :] * vector + coupled
    sums = jnp.zeros((SUMS, LANES), F32)
    row = lax.broadcasted_iota(jnp.int32, (SUMS, LANES), 0)
    for slot, terms in enumerate((vector * vector, vector * mapped, mapped * mapped)):
        sums = jnp.where(row == slot, jnp.sum(terms, axis=0, keepdims=True), sums)
    sums = sum_components(sums)
    work[...] = jnp.zeros_like(work)
    work[SUM_ROW : SUM_ROW + SUMS, :] = pltpu.roll(sums, 4, 0)
    work[SUM_ROW + SUMS : SUM_ROW + 2 * SUMS, :] = pltpu.roll(sums, LANES - ATOMS, 1)
    payload = jnp.where(inside, mapped, work[...].T[0:ATOMS, :])
    for slot in range(HALF):
        out[slot] = payload


def second_kernel(gathered, high, low, part_out, side):
    vectors = gathered[...]
    right_side(vectors.reshape(WIDE, LANES), side)
    sums = jnp.where(lane_ids(ATOMS) < COMPS * RHS, 0.0, jnp.sum(vectors, axis=0))
    part_out[...] = product(high, low, side).reshape(GROUP, ATOMS, LANES) + sums[None]


def step_kernel(parts, own, shifted, aux, sums_out, state, work):
    total = jnp.sum(parts[...], axis=0)
    vector = own[0]
    mapped = shifted[0]
    twice = aux[0:ATOMS, :] * mapped + total
    work[...] = jnp.zeros_like(work)
    work[0:ATOMS, :] = total
    turned = work[...].T
    lane8 = lane_ids(SUMS)
    head = pltpu.roll(turned[SUM_ROW : SUM_ROW + SUMS, :], 4, 0)
    tail = pltpu.roll(turned[SUM_ROW + SUMS : SUM_ROW + 2 * SUMS, :], ATOMS, 1)
    sums = jnp.where(lane8 < ATOMS, head, jnp.where(lane8 < RHS, tail, 0.0))
    sums = sums + pltpu.roll(sums, RHS, 1) + pltpu.roll(sums, 2 * RHS, 1)
    bb, be, ee = sums[0:1, :], sums[1:2, :], sums[2:3, :]
    shift = aux[ATOMS : ATOMS + 1, :]
    bm = shift * bb + be
    step = bb / bm
    kept = be / bm
    beta = (bb * ee - be * be) / (bm * bm)
    residual = kept * vector - step * mapped
    direction = residual + beta * vector
    image = shift * direction + ((kept + beta) * mapped - step * twice)
    row = lax.broadcasted_iota(jnp.int32, (SUMS, LANES), 0)
    squares = jnp.sum(residual * residual, axis=0, keepdims=True)
    curvature = jnp.sum(direction * image, axis=0, keepdims=True)
    both = sum_components(jnp.where(row == 0, squares, jnp.where(row == 1, curvature, 0.0)))
    lane = lax.broadcasted_iota(jnp.int32, (1, LANES), 1)
    packed = jnp.where(lane < RHS, both[0:1, :], jnp.where(lane < 2 * RHS, both[1:2, :], 0.0))
    sums_out[...] = jnp.broadcast_to(packed.reshape(1, 1, LANES), sums_out.shape)
    state[0] = step * vector
    state[1] = direction
    state[2] = residual
    state[3] = image


def finish_kernel(gathered, state, dipoles, residual):
    total = jnp.broadcast_to(jnp.sum(gathered[...], axis=0), (SUMS, LANES))
    first, second, third = component_lanes(SUMS)
    up = pltpu.roll(total, RHS, 1)
    up2 = pltpu.roll(total, 2 * RHS, 1)
    down = pltpu.roll(total, LANES - RHS, 1)
    squares = jnp.where(first, total, jnp.where(second, up, up2))
    curvature = jnp.where(first, down, jnp.where(second, total, jnp.where(third, up, 1.0)))
    step = (squares / curvature)[0:1, :]
    for out, value in (
        (dipoles, state[0] + step * state[1]),
        (residual, state[2] - step * state[3]),
    ):
        for comp in range(COMPS):
            out[comp] = value[:, comp * RHS : (comp + 1) * RHS]


def shape(*dims, dtype=F32):
    return jax.ShapeDtypeStruct(dims, dtype)


def whole(*dims):
    return pl.BlockSpec(dims, lambda i: (0,) * len(dims))


def core_swap(value):
    return lax.ppermute(value, "col", [(slot, slot ^ 1) for slot in range(GROUP)])


def gather_own(value):
    groups = [list(range(core, GROUP, 2)) for core in range(2)]
    return lax.all_to_all(value, "col", 0, 0, axis_index_groups=groups)


def local(external_field, jitter, species, alpha_table, block_cell, tile_map):
    ids = jnp.stack([lax.axis_index("row"), lax.axis_index("col")]).astype(jnp.int32)
    jitters = lax.all_to_all(jnp.broadcast_to(jitter, (GROUP, COMPS, ATOMS)), "row", 0, 0)
    vec = pl.pallas_call(
        prepare_kernel,
        out_shape=shape(HALF, ATOMS, LANES),
        in_specs=[SMEM, HBM, HBM, HBM],
        out_specs=VMEM,
        scratch_shapes=[
            pltpu.SMEM((GROUP * GROUP,), jnp.int32),
            pltpu.VMEM((COMPS, ATOMS, RHS), F32),
            pltpu.VMEM((COMPS, ATOMS), F32),
            SQUARE,
            pltpu.VMEM((ATOMS, LANES), F32),
            pltpu.SemaphoreType.DMA((3,)),
        ],
        compiler_params=PARAMS,
        name="prepare",
    )(ids, block_cell, external_field.transpose(0, 2, 1), jitter)
    ready, jitters = lax.optimization_barrier((vec, jitters))
    aux, mask, column = pl.pallas_call(
        side_kernel,
        out_shape=(shape(ATOMS + SUMS, LANES), shape(GROUP, WIDE), shape(COMPS, WIDE, LANES)),
        in_specs=[SMEM, HBM, HBM, HBM, HBM, VMEM],
        out_specs=(VMEM, VMEM, VMEM),
        scratch_shapes=[
            pltpu.VMEM((ATOMS,), jnp.int32),
            pltpu.VMEM((4, 12), F32),
            pltpu.VMEM((GROUP * GROUP, GROUP * GROUP), jnp.int32),
            pltpu.SMEM((GROUP * GROUP,), jnp.int32),
            SQUARE,
            pltpu.SemaphoreType.DMA((4,)),
        ],
        compiler_params=PARAMS,
        name="side",
    )(ids, species, alpha_table.T, tile_map, block_cell, jitters)
    own = gather_own(ready)
    own, aux, mask, column = lax.optimization_barrier((own, aux, mask, column))
    other = core_swap(own)
    side = pltpu.VMEM((PAIRS * NARROW, 2 * LANES), BF16)
    tile = shape(WIDE, PAIRS * NARROW, dtype=BF16)
    total, high0, low0 = pl.pallas_call(
        first_own_kernel,
        out_shape=(shape(WIDE, LANES), tile, tile),
        in_specs=[VMEM] * 3,
        out_specs=(VMEM, VMEM, VMEM),
        scratch_shapes=[side],
        compiler_params=PARAMS,
        name="first_own",
    )(mask, column, own)
    part, high1, low1 = pl.pallas_call(
        first_other_kernel,
        out_shape=(shape(GROUP, ATOMS, LANES), tile, tile),
        in_specs=[VMEM] * 4,
        out_specs=(VMEM, VMEM, VMEM),
        scratch_shapes=[side],
        compiler_params=PARAMS,
        name="first_other",
    )(mask, column, other, total)
    parts = lax.all_to_all(part, "row", 0, 0)
    blocks = whole(GROUP, ATOMS, LANES)
    block = whole(1, ATOMS, LANES)
    shifted = pl.pallas_call(
        shifted_kernel,
        grid=(1,),
        out_shape=shape(HALF, ATOMS, LANES),
        in_specs=[blocks, block, whole(ATOMS + SUMS, LANES)],
        out_specs=whole(HALF, ATOMS, LANES),
        scratch_shapes=[SQUARE],
        compiler_params=PARAMS,
        name="shifted",
    )(parts, vec, aux)
    own2 = gather_own(shifted)
    other2 = core_swap(own2)
    total2 = pl.pallas_call(
        second_own_kernel,
        out_shape=shape(GROUP, ATOMS, LANES),
        in_specs=[VMEM] * 3,
        out_specs=VMEM,
        scratch_shapes=[side],
        compiler_params=PARAMS,
        name="second_own",
    )(own2, high0, low0)
    part2 = pl.pallas_call(
        second_other_kernel,
        out_shape=shape(GROUP, ATOMS, LANES),
        in_specs=[VMEM] * 4,
        out_specs=VMEM,
        scratch_shapes=[side],
        compiler_params=PARAMS,
        name="second_other",
    )(other2, high1, low1, total2)
    parts2 = lax.all_to_all(part2, "row", 0, 0)
    sums, state = pl.pallas_call(
        step_kernel,
        grid=(1,),
        out_shape=(shape(GROUP * GROUP, 1, LANES), shape(4, ATOMS, LANES)),
        in_specs=[blocks, block, block, whole(ATOMS + SUMS, LANES)],
        out_specs=(whole(GROUP * GROUP, 1, LANES), whole(4, ATOMS, LANES)),
        scratch_shapes=[SQUARE],
        compiler_params=PARAMS,
        name="step",
    )(parts2, vec, shifted, aux)
    all_sums = lax.all_to_all(sums, ("row", "col"), 0, 0)
    dipoles, residual = pl.pallas_call(
        finish_kernel,
        out_shape=(shape(COMPS, ATOMS, RHS), shape(COMPS, ATOMS, RHS)),
        in_specs=[VMEM, VMEM],
        out_specs=(VMEM, VMEM),
        compiler_params=PARAMS,
        name="finish",
    )(all_sums, state)
    return dipoles.transpose(0, 2, 1), residual.transpose(0, 2, 1)


def solution(mesh):
    return jax.shard_map(
        local,
        mesh=mesh,
        in_specs=(
            P(None, None, ("row", "col")),
            P(None, ("row", "col")),
            P(("row", "col")),
            P(),
            P(),
            P(),
        ),
        out_specs=(P(None, None, ("row", "col")), P(None, None, ("row", "col"))),
        check_vma=False,
    )
```

```python
import jax
import jax.numpy as jnp
from jax import lax
from jax.experimental import pallas as pl
from jax.experimental.pallas import tpu as pltpu
from jax.sharding import Mesh, PartitionSpec as P

COMPS = 3
RHS = 36
ATOMS = 32
GROUP = 16
HALF = 8
LANES = 128
SUMS = 8
SITE = 120
SUM_ROW = 104
WIDE = GROUP * ATOMS
NARROW = HALF * ATOMS
CHUNK = 256
PAIRS = 5
SPACING = 2.0
F32 = jnp.float32
BF16 = jnp.bfloat16

VMEM = pl.BlockSpec(memory_space=pltpu.VMEM)
SMEM = pl.BlockSpec(memory_space=pltpu.SMEM)
HBM = pl.BlockSpec(memory_space=pltpu.HBM)
SQUARE = pltpu.VMEM((LANES, LANES), F32)
PARAMS = pltpu.CompilerParams(vmem_limit_bytes=16 * 1024 * 1024)


def lane_ids(rows):
    return lax.broadcasted_iota(jnp.int32, (rows, LANES), 1)


def component_lanes(rows):
    lanes = lane_ids(rows)
    first = lanes < RHS
    second = (lanes >= RHS) & (lanes < 2 * RHS)
    third = (lanes >= 2 * RHS) & (lanes < COMPS * RHS)
    return first, second, third


def sum_components(value):
    first, second, third = component_lanes(SUMS)
    up = pltpu.roll(value, RHS, 1)
    up2 = pltpu.roll(value, 2 * RHS, 1)
    down = pltpu.roll(value, LANES - RHS, 1)
    down2 = pltpu.roll(value, LANES - 2 * RHS, 1)
    of_first = value + down + down2
    of_second = up + value + down
    of_third = up2 + up + value
    return jnp.where(first, of_first, jnp.where(second, of_second, jnp.where(third, of_third, 1.0)))


def fetch(pairs, sems):
    copies = [pltpu.make_async_copy(source, target, sems.at[i]) for i, (source, target) in enumerate(pairs)]
    for copy in copies:
        copy.start()
    for copy in copies:
        copy.wait()


def prepare_kernel(ids, cells_hbm, field_hbm, jitter_hbm, vec_out, own_out, cells, field, jitter, work, wide, sems):
    fetch(((cells_hbm, cells), (field_hbm, field), (jitter_hbm, jitter)), sems)
    cell = cells[ids[0] * GROUP + ids[1]]
    work[...] = jnp.zeros_like(work)
    work[SITE : SITE + COMPS, 0:ATOMS] = block_sites(cell, jitter[...])
    wide[...] = work[...].T[0:ATOMS, :]
    for comp in range(COMPS):
        wide[:, comp * RHS : (comp + 1) * RHS] = field[comp]
    turned = wide[...]
    own_out[...] = turned
    for slot in range(HALF):
        vec_out[slot] = turned


def block_sites(cell, jitter):
    comp = lax.broadcasted_iota(jnp.int32, (COMPS, ATOMS), 0)
    atom = lax.broadcasted_iota(jnp.int32, (COMPS, ATOMS), 1)
    inner = jnp.where(comp == 0, atom // 8, jnp.where(comp == 1, (atom // 2) % 4, atom % 2))
    corner = jnp.where(comp == 0, cell // 32 * 4, jnp.where(comp == 1, (cell // 4) % 8 * 4, cell % 4 * 2))
    return (corner + inner).astype(F32) * SPACING + jitter


def side_kernel(
    ids, species_hbm, alpha_hbm, tile_map_hbm, cells_hbm, jitters,
    aux_out, mask_out, column, species, alpha, tile_map, cells, work, sems
):
    fetch(
        ((species_hbm, species), (alpha_hbm, alpha), (tile_map_hbm, tile_map), (cells_hbm, cells)), sems
    )
    lane = lax.broadcasted_iota(jnp.int32, (4, LANES), 1)
    rhs_lane = jnp.where(lane >= 2 * RHS, lane - 2 * RHS, jnp.where(lane >= RHS, lane - RHS, lane))
    table = jnp.ones((4, LANES), F32)
    for freq in range(12):
        table = jnp.where(
            (rhs_lane >= 3 * freq) & (rhs_lane < 3 * freq + 3),
            jnp.broadcast_to(alpha[:, freq : freq + 1], (4, LANES)),
            table,
        )
    inverse = 1.0 / table
    shift = 0.25 * ((inverse[0:1] + inverse[1:2]) + (inverse[2:3] + inverse[3:4]))
    work[...] = jnp.zeros_like(work)
    work[0:1, 0:ATOMS] = species[...].astype(F32).reshape(1, ATOMS)
    kinds = jnp.broadcast_to(work[...].T[0:ATOMS, 0:1], (ATOMS, LANES))
    diag = jnp.zeros((ATOMS, LANES), F32)
    for kind in range(4):
        diag = jnp.where(kinds == float(kind), inverse[kind : kind + 1] - shift, diag)
    aux_out[0:ATOMS, :] = diag
    aux_out[ATOMS : ATOMS + SUMS, :] = jnp.broadcast_to(shift, (SUMS, LANES))

    blocks = GROUP * GROUP
    active = jnp.where(tile_map[...] != 0, 1.0, 0.0).astype(BF16)
    place = lax.broadcasted_iota(jnp.int32, (GROUP, blocks), 1)
    wanted = lax.broadcasted_iota(jnp.int32, (GROUP, blocks), 0) * GROUP + ids[1]
    pick = jnp.where(place == wanted, 1.0, 0.0).astype(BF16)
    lines = jnp.dot(pick, active, preferred_element_type=F32).astype(BF16)
    slot = lax.broadcasted_iota(jnp.int32, (blocks, WIDE), 1) // ATOMS
    wanted = ids[0] * GROUP + (slot % HALF) * 2 + ((ids[1] % 2) ^ (slot // HALF))
    place = lax.broadcasted_iota(jnp.int32, (blocks, WIDE), 0)
    spread = jnp.where(place == wanted, 1.0, 0.0).astype(BF16)
    mask_out[...] = 0.5 * jnp.dot(lines, spread, preferred_element_type=F32)

    work[...] = jnp.zeros_like(work)
    for slot in range(GROUP):
        cell = cells[slot * GROUP + ids[1]]
        work[slot * SUMS : slot * SUMS + COMPS, 0:ATOMS] = block_sites(cell, jitters[slot])
    down = work[...].T[0:ATOMS, :]
    for slot in range(GROUP):
        rows = slice(slot * ATOMS, (slot + 1) * ATOMS)
        for comp in range(COMPS):
            lane = slot * SUMS + comp
            column[comp, rows, :] = jnp.broadcast_to(down[:, lane : lane + 1], (ATOMS, LANES))


def right_side(vectors, side):
    first, second, third = component_lanes(NARROW)
    zero = jnp.zeros_like(vectors)
    up = pltpu.roll(vectors, RHS, 1)
    up2 = pltpu.roll(vectors, 2 * RHS, 1)
    down = pltpu.roll(vectors, LANES - RHS, 1)
    down2 = pltpu.roll(vectors, LANES - 2 * RHS, 1)
    parts = (
        jnp.where(first, vectors, jnp.where(third, -vectors, zero)),
        jnp.where(second, vectors, jnp.where(third, -vectors, zero)),
        jnp.where(first, down, jnp.where(second, up, zero)),
        jnp.where(first, down2, jnp.where(third, up2, zero)),
        jnp.where(second, down, jnp.where(third, up, zero)),
    )
    for slot, part in enumerate(parts):
        high = part.astype(BF16)
        low = (part - high.astype(F32)).astype(BF16)
        side[slot * NARROW : (slot + 1) * NARROW, 0:LANES] = high
        side[slot * NARROW : (slot + 1) * NARROW, LANES : 2 * LANES] = low


def product(high, low, side):
    both = jnp.dot(high, side[...], preferred_element_type=F32)
    rest = jnp.dot(low, side[:, 0:LANES], preferred_element_type=F32)
    return both[:, 0:LANES] + (both[:, LANES:] + rest)


def build_and_apply(mask, vectors, column, high, low, side, first_lane):
    across = vectors.T[SITE : SITE + SUMS, :]
    across_x, across_y, across_z = across[0:1, :], across[1:2, :], across[2:3, :]

    def rows16(step):
        rows = slice(step * 16, (step + 1) * 16)
        here_x, here_y, here_z = column[0, rows, :], column[1, rows, :], column[2, rows, :]
        keep = mask[step // 2 : step // 2 + 1, :]
        for tile in range(NARROW // LANES):
            lanes = slice(tile * LANES, (tile + 1) * LANES)
            dx = here_x - across_x[:, lanes]
            dy = here_y - across_y[:, lanes]
            dz = here_z - across_z[:, lanes]
            xx = dx * dx
            yy = dy * dy
            distance2 = xx + yy + dz * dz
            square = jnp.maximum(distance2, 1.0)
            inverse = lax.rsqrt(square)
            damping = 1.0 + jnp.tanh(1.25 * (square * inverse) - 3.0)
            inverse2 = inverse * inverse
            kept = keep[:, first_lane + tile * LANES : first_lane + (tile + 1) * LANES]
            weight = damping * (inverse2 * inverse2 * inverse) * kept
            radial = weight * distance2
            minus3 = -3.0 * weight
            along_x = minus3 * dx
            along_y = minus3 * dy
            entries = (
                radial + minus3 * xx,
                radial + minus3 * yy,
                along_x * dy,
                along_x * dz,
                along_y * dz,
            )
            for slot, entry in enumerate(entries):
                top = entry.astype(BF16)
                at = slice(slot * NARROW + tile * LANES, slot * NARROW + (tile + 1) * LANES)
                high[rows, at] = top
                low[rows, at] = (entry - top.astype(F32)).astype(BF16)

    outs = []
    for chunk in range(0, WIDE, CHUNK):
        for step in range(chunk // 16, (chunk + CHUNK) // 16):
            rows16(step)
        rows = slice(chunk, chunk + CHUNK)
        outs.append(product(high[rows, :], low[rows, :], side))
    return jnp.concatenate(outs, axis=0)


def first_own_kernel(mask, column, gathered, total, high, low, side):
    vectors = gathered[...].reshape(NARROW, LANES)
    right_side(vectors, side)
    total[...] = build_and_apply(mask, vectors, column, high, low, side, 0)


def first_other_kernel(mask, column, gathered, total, part_out, high, low, side):
    vectors = gathered[...].reshape(NARROW, LANES)
    right_side(vectors, side)
    out = build_and_apply(mask, vectors, column, high, low, side, NARROW)
    part_out[...] = (total[...] + out).reshape(GROUP, ATOMS, LANES)


def spare_sums(vectors):
    return jnp.where(lane_ids(ATOMS) < COMPS * RHS, 0.0, jnp.sum(vectors, axis=0))


def second_own_kernel(gathered, high, low, total, side):
    vectors = gathered[...]
    right_side(vectors.reshape(NARROW, LANES), side)
    out = product(high[...], low[...], side).reshape(GROUP, ATOMS, LANES) + spare_sums(vectors)[None]
    total[...] = out


def second_other_kernel(gathered, high, low, total, part_out, side):
    vectors = gathered[...]
    right_side(vectors.reshape(NARROW, LANES), side)
    out = product(high[...], low[...], side).reshape(GROUP, ATOMS, LANES) + spare_sums(vectors)[None]
    part_out[...] = total[...] + out


def shifted_kernel(parts, own, aux, out, work):
    coupled = jnp.sum(parts[...], axis=0)
    inside = lane_ids(ATOMS) < COMPS * RHS
    vector = jnp.where(inside, own[...], 0.0)
    mapped = aux[0:ATOMS, :] * vector + coupled
    sums = jnp.zeros((SUMS, LANES), F32)
    row = lax.broadcasted_iota(jnp.int32, (SUMS, LANES), 0)
    for slot, terms in enumerate((vector * vector, vector * mapped, mapped * mapped)):
        sums = jnp.where(row == slot, jnp.sum(terms, axis=0, keepdims=True), sums)
    sums = sum_components(sums)
    work[...] = jnp.zeros_like(work)
    work[SUM_ROW : SUM_ROW + SUMS, :] = pltpu.roll(sums, 4, 0)
    work[SUM_ROW + SUMS : SUM_ROW + 2 * SUMS, :] = pltpu.roll(sums, LANES - ATOMS, 1)
    payload = jnp.where(inside, mapped, work[...].T[0:ATOMS, :])
    for slot in range(HALF):
        out[slot] = payload


def second_kernel(gathered, high, low, part_out, side):
    vectors = gathered[...]
    right_side(vectors.reshape(WIDE, LANES), side)
    sums = jnp.where(lane_ids(ATOMS) < COMPS * RHS, 0.0, jnp.sum(vectors, axis=0))
    part_out[...] = product(high[...], low[...], side).reshape(GROUP, ATOMS, LANES) + sums[None]


def step_kernel(parts, own, shifted, aux, sums_out, state, work):
    total = jnp.sum(parts[...], axis=0)
    vector = own[...]
    mapped = shifted[0]
    twice = aux[0:ATOMS, :] * mapped + total
    work[...] = jnp.zeros_like(work)
    work[0:ATOMS, :] = total
    turned = work[...].T
    lane8 = lane_ids(SUMS)
    head = pltpu.roll(turned[SUM_ROW : SUM_ROW + SUMS, :], 4, 0)
    tail = pltpu.roll(turned[SUM_ROW + SUMS : SUM_ROW + 2 * SUMS, :], ATOMS, 1)
    sums = jnp.where(lane8 < ATOMS, head, jnp.where(lane8 < RHS, tail, 0.0))
    sums = sums + pltpu.roll(sums, RHS, 1) + pltpu.roll(sums, 2 * RHS, 1)
    bb, be, ee = sums[0:1, :], sums[1:2, :], sums[2:3, :]
    shift = aux[ATOMS : ATOMS + 1, :]
    bm = shift * bb + be
    step = bb / bm
    kept = be / bm
    beta = (bb * ee - be * be) / (bm * bm)
    residual = kept * vector - step * mapped
    direction = residual + beta * vector
    image = shift * direction + ((kept + beta) * mapped - step * twice)
    row = lax.broadcasted_iota(jnp.int32, (SUMS, LANES), 0)
    squares = jnp.sum(residual * residual, axis=0, keepdims=True)
    curvature = jnp.sum(direction * image, axis=0, keepdims=True)
    both = sum_components(jnp.where(row == 0, squares, jnp.where(row == 1, curvature, 0.0)))
    lane = lax.broadcasted_iota(jnp.int32, (1, LANES), 1)
    packed = jnp.where(lane < RHS, both[0:1, :], jnp.where(lane < 2 * RHS, both[1:2, :], 0.0))
    sums_out[...] = jnp.broadcast_to(packed, sums_out.shape)
    state[0] = step * vector
    state[1] = direction
    state[2] = residual
    state[3] = image


def pair_kernel(sums, swapped, out):
    out[...] = jnp.broadcast_to((sums[...] + swapped[...])[None], out.shape)


def finish_kernel(gathered, state, dipoles, residual):
    total = jnp.sum(gathered[...], axis=0)
    total = jnp.broadcast_to(jnp.sum(total, axis=0, keepdims=True), (SUMS, LANES))
    first, second, third = component_lanes(SUMS)
    up = pltpu.roll(total, RHS, 1)
    up2 = pltpu.roll(total, 2 * RHS, 1)
    down = pltpu.roll(total, LANES - RHS, 1)
    squares = jnp.where(first, total, jnp.where(second, up, up2))
    curvature = jnp.where(first, down, jnp.where(second, total, jnp.where(third, up, 1.0)))
    step = (squares / curvature)[0:1, :]
    for out, value in (
        (dipoles, state[0] + step * state[1]),
        (residual, state[2] - step * state[3]),
    ):
        for comp in range(COMPS):
            out[comp] = value[:, comp * RHS : (comp + 1) * RHS]


def shape(*dims, dtype=F32):
    return jax.ShapeDtypeStruct(dims, dtype)


def whole(*dims):
    return pl.BlockSpec(dims, lambda i: (0,) * len(dims))


def core_swap(value):
    return lax.ppermute(value, "core", [(0, 1), (1, 0)])


def gather_own(value):
    return lax.all_to_all(value, "z", 0, 0)


def local(external_field, jitter, species, alpha_table, block_cell, tile_map):
    ids = jnp.stack([lax.axis_index("row"), lax.axis_index(("z", "core"))]).astype(jnp.int32)
    jitters = lax.all_to_all(jnp.broadcast_to(jitter, (GROUP, COMPS, ATOMS)), "row", 0, 0)
    vec, vector = pl.pallas_call(
        prepare_kernel,
        out_shape=(shape(HALF, ATOMS, LANES), shape(ATOMS, LANES)),
        in_specs=[SMEM, HBM, HBM, HBM],
        out_specs=(VMEM, VMEM),
        scratch_shapes=[
            pltpu.SMEM((GROUP * GROUP,), jnp.int32),
            pltpu.VMEM((COMPS, ATOMS, RHS), F32),
            pltpu.VMEM((COMPS, ATOMS), F32),
            SQUARE,
            pltpu.VMEM((ATOMS, LANES), F32),
            pltpu.SemaphoreType.DMA((3,)),
        ],
        compiler_params=PARAMS,
        name="prepare",
    )(ids, block_cell, external_field.transpose(0, 2, 1), jitter)
    aux, mask, column = pl.pallas_call(
        side_kernel,
        out_shape=(shape(ATOMS + SUMS, LANES), shape(GROUP, WIDE), shape(COMPS, WIDE, LANES)),
        in_specs=[SMEM, HBM, HBM, HBM, HBM, VMEM],
        out_specs=(VMEM, VMEM, VMEM),
        scratch_shapes=[
            pltpu.VMEM((ATOMS,), jnp.int32),
            pltpu.VMEM((4, 12), F32),
            pltpu.VMEM((GROUP * GROUP, GROUP * GROUP), jnp.int32),
            pltpu.SMEM((GROUP * GROUP,), jnp.int32),
            SQUARE,
            pltpu.SemaphoreType.DMA((4,)),
        ],
        compiler_params=PARAMS,
        name="side",
    )(ids, species, alpha_table.T, tile_map, block_cell, jitters)
    own = gather_own(vec)
    own, aux, mask, column = lax.optimization_barrier((own, aux, mask, column))
    other = core_swap(own)
    side = pltpu.VMEM((PAIRS * NARROW, 2 * LANES), BF16)
    tile = shape(WIDE, PAIRS * NARROW, dtype=BF16)
    total, high0, low0 = pl.pallas_call(
        first_own_kernel,
        out_shape=(shape(WIDE, LANES), tile, tile),
        in_specs=[VMEM] * 3,
        out_specs=(VMEM, VMEM, VMEM),
        scratch_shapes=[side],
        compiler_params=PARAMS,
        name="first_own",
    )(mask, column, own)
    part, high1, low1 = pl.pallas_call(
        first_other_kernel,
        out_shape=(shape(GROUP, ATOMS, LANES), tile, tile),
        in_specs=[VMEM] * 4,
        out_specs=(VMEM, VMEM, VMEM),
        scratch_shapes=[side],
        compiler_params=PARAMS,
        name="first_other",
    )(mask, column, other, total)
    parts = lax.all_to_all(part, "row", 0, 0)
    blocks = whole(GROUP, ATOMS, LANES)
    block = whole(1, ATOMS, LANES)
    shifted = pl.pallas_call(
        shifted_kernel,
        grid=(1,),
        out_shape=shape(HALF, ATOMS, LANES),
        in_specs=[blocks, whole(ATOMS, LANES), whole(ATOMS + SUMS, LANES)],
        out_specs=whole(HALF, ATOMS, LANES),
        scratch_shapes=[SQUARE],
        compiler_params=PARAMS,
        name="shifted",
    )(parts, vector, aux)
    own2 = gather_own(shifted)
    other2 = core_swap(own2)
    total2 = pl.pallas_call(
        second_own_kernel,
        out_shape=shape(GROUP, ATOMS, LANES),
        in_specs=[VMEM] * 3,
        out_specs=VMEM,
        scratch_shapes=[side],
        compiler_params=PARAMS,
        name="second_own",
    )(own2, high0, low0)
    part2 = pl.pallas_call(
        second_other_kernel,
        out_shape=shape(GROUP, ATOMS, LANES),
        in_specs=[VMEM] * 4,
        out_specs=VMEM,
        scratch_shapes=[side],
        compiler_params=PARAMS,
        name="second_other",
    )(other2, high1, low1, total2)
    parts2 = lax.all_to_all(part2, "row", 0, 0)
    sums, state = pl.pallas_call(
        step_kernel,
        grid=(1,),
        out_shape=(shape(SUMS, LANES), shape(4, ATOMS, LANES)),
        in_specs=[blocks, whole(ATOMS, LANES), block, whole(ATOMS + SUMS, LANES)],
        out_specs=(whole(SUMS, LANES), whole(4, ATOMS, LANES)),
        scratch_shapes=[SQUARE],
        compiler_params=PARAMS,
        name="step",
    )(parts2, vector, shifted, aux)
    pair = pl.pallas_call(
        pair_kernel,
        out_shape=shape(GROUP, SUMS, LANES),
        in_specs=[VMEM, VMEM],
        out_specs=VMEM,
        compiler_params=PARAMS,
        name="pair",
    )(sums, core_swap(sums))
    pair = pair.reshape(GROUP * HALF, 1, LANES)
    all_sums = lax.all_to_all(pair, ("row", "z"), 0, 0).reshape(GROUP, SUMS, LANES)
    dipoles, residual = pl.pallas_call(
        finish_kernel,
        out_shape=(shape(COMPS, ATOMS, RHS), shape(COMPS, ATOMS, RHS)),
        in_specs=[VMEM, VMEM],
        out_specs=(VMEM, VMEM),
        compiler_params=PARAMS,
        name="finish",
    )(all_sums, state)
    return dipoles.transpose(0, 2, 1), residual.transpose(0, 2, 1)


def solution(mesh):
    split = Mesh(mesh.devices.reshape(GROUP, HALF, 2), ("row", "z", "core"))
    every = ("row", "z", "core")
    return jax.shard_map(
        local,
        mesh=split,
        in_specs=(P(None, None, every), P(None, every), P(every), P(), P(), P()),
        out_specs=(P(None, None, every), P(None, None, every)),
        check_vma=False,
    )
```

```python
import jax
import jax.numpy as jnp
from jax import lax
from jax.experimental import pallas as pl
from jax.experimental.pallas import tpu as pltpu
from jax.sharding import Mesh, PartitionSpec as P

COMPS = 3
RHS = 36
ATOMS = 32
GROUP = 16
HALF = 8
LANES = 128
SUMS = 8
SITE = 120
SUM_ROW = 104
WIDE = GROUP * ATOMS
NARROW = HALF * ATOMS
CHUNK = 256
PAIRS = 5
SPACING = 2.0
F32 = jnp.float32
BF16 = jnp.bfloat16

VMEM = pl.BlockSpec(memory_space=pltpu.VMEM)
SMEM = pl.BlockSpec(memory_space=pltpu.SMEM)
HBM = pl.BlockSpec(memory_space=pltpu.HBM)
SQUARE = pltpu.VMEM((LANES, LANES), F32)
PARAMS = pltpu.CompilerParams(vmem_limit_bytes=16 * 1024 * 1024)


def lane_ids(rows):
    return lax.broadcasted_iota(jnp.int32, (rows, LANES), 1)


def component_lanes(rows):
    lanes = lane_ids(rows)
    first = lanes < RHS
    second = (lanes >= RHS) & (lanes < 2 * RHS)
    third = (lanes >= 2 * RHS) & (lanes < COMPS * RHS)
    return first, second, third


def sum_components(value):
    first, second, third = component_lanes(SUMS)
    up = pltpu.roll(value, RHS, 1)
    up2 = pltpu.roll(value, 2 * RHS, 1)
    down = pltpu.roll(value, LANES - RHS, 1)
    down2 = pltpu.roll(value, LANES - 2 * RHS, 1)
    of_first = value + down + down2
    of_second = up + value + down
    of_third = up2 + up + value
    return jnp.where(first, of_first, jnp.where(second, of_second, jnp.where(third, of_third, 1.0)))


def fetch(pairs, sems):
    copies = [pltpu.make_async_copy(source, target, sems.at[i]) for i, (source, target) in enumerate(pairs)]
    for copy in copies:
        copy.start()
    for copy in copies:
        copy.wait()


def prepare_kernel(ids, cells_hbm, field_hbm, jitter_hbm, vec_out, own_out, cells_out, cells, field, jitter, work, wide, sems):
    fetch(((cells_hbm, cells), (field_hbm, field), (jitter_hbm, jitter)), sems)
    cell = cells[ids[0] * GROUP + ids[1]]
    work[...] = jnp.zeros_like(work)
    work[SITE : SITE + COMPS, 0:ATOMS] = block_sites(cell, jitter[...])
    wide[...] = work[...].T[0:ATOMS, :]
    for comp in range(COMPS):
        wide[:, comp * RHS : (comp + 1) * RHS] = field[comp]
    turned = wide[...]
    own_out[...] = turned
    cells_out[...] = cells_hbm[...]
    for slot in range(HALF):
        vec_out[slot] = turned


def block_sites(cell, jitter):
    comp = lax.broadcasted_iota(jnp.int32, (COMPS, ATOMS), 0)
    atom = lax.broadcasted_iota(jnp.int32, (COMPS, ATOMS), 1)
    inner = jnp.where(comp == 0, atom // 8, jnp.where(comp == 1, (atom // 2) % 4, atom % 2))
    corner = jnp.where(comp == 0, cell // 32 * 4, jnp.where(comp == 1, (cell // 4) % 8 * 4, cell % 4 * 2))
    return (corner + inner).astype(F32) * SPACING + jitter


def side_kernel(
    ids, species_hbm, alpha_hbm, tile_map_hbm, cells_hbm, jitters,
    aux_out, mask_out, column, species, alpha, tile_map, cells, work, sems
):
    fetch(
        ((species_hbm, species), (alpha_hbm, alpha), (tile_map_hbm, tile_map), (cells_hbm, cells)), sems
    )
    lane = lax.broadcasted_iota(jnp.int32, (4, LANES), 1)
    rhs_lane = jnp.where(lane >= 2 * RHS, lane - 2 * RHS, jnp.where(lane >= RHS, lane - RHS, lane))
    table = jnp.ones((4, LANES), F32)
    for freq in range(12):
        table = jnp.where(
            (rhs_lane >= 3 * freq) & (rhs_lane < 3 * freq + 3),
            jnp.broadcast_to(alpha[:, freq : freq + 1], (4, LANES)),
            table,
        )
    inverse = 1.0 / table
    shift = 0.25 * ((inverse[0:1] + inverse[1:2]) + (inverse[2:3] + inverse[3:4]))
    work[...] = jnp.zeros_like(work)
    work[0:1, 0:ATOMS] = species[...].astype(F32).reshape(1, ATOMS)
    kinds = jnp.broadcast_to(work[...].T[0:ATOMS, 0:1], (ATOMS, LANES))
    diag = jnp.zeros((ATOMS, LANES), F32)
    for kind in range(4):
        diag = jnp.where(kinds == float(kind), inverse[kind : kind + 1] - shift, diag)
    aux_out[0:ATOMS, :] = diag
    aux_out[ATOMS : ATOMS + SUMS, :] = jnp.broadcast_to(shift, (SUMS, LANES))

    blocks = GROUP * GROUP
    active = jnp.where(tile_map[...] != 0, 1.0, 0.0).astype(BF16)
    place = lax.broadcasted_iota(jnp.int32, (GROUP, blocks), 1)
    wanted = lax.broadcasted_iota(jnp.int32, (GROUP, blocks), 0) * GROUP + ids[1]
    pick = jnp.where(place == wanted, 1.0, 0.0).astype(BF16)
    lines = jnp.dot(pick, active, preferred_element_type=F32).astype(BF16)
    slot = lax.broadcasted_iota(jnp.int32, (blocks, WIDE), 1) // ATOMS
    wanted = ids[0] * GROUP + (slot % HALF) * 2 + ((ids[1] % 2) ^ (slot // HALF))
    place = lax.broadcasted_iota(jnp.int32, (blocks, WIDE), 0)
    spread = jnp.where(place == wanted, 1.0, 0.0).astype(BF16)
    mask_out[...] = 0.5 * jnp.dot(lines, spread, preferred_element_type=F32)

    work[...] = jnp.zeros_like(work)
    for slot in range(GROUP):
        cell = cells[slot * GROUP + ids[1]]
        work[slot * SUMS : slot * SUMS + COMPS, 0:ATOMS] = block_sites(cell, jitters[slot])
    down = work[...].T[0:ATOMS, :]
    for slot in range(GROUP):
        rows = slice(slot * ATOMS, (slot + 1) * ATOMS)
        for comp in range(COMPS):
            lane = slot * SUMS + comp
            column[comp, rows, :] = jnp.broadcast_to(down[:, lane : lane + 1], (ATOMS, LANES))


def right_side(vectors, side):
    first, second, third = component_lanes(NARROW)
    zero = jnp.zeros_like(vectors)
    up = pltpu.roll(vectors, RHS, 1)
    up2 = pltpu.roll(vectors, 2 * RHS, 1)
    down = pltpu.roll(vectors, LANES - RHS, 1)
    down2 = pltpu.roll(vectors, LANES - 2 * RHS, 1)
    parts = (
        jnp.where(first, vectors, jnp.where(third, -vectors, zero)),
        jnp.where(second, vectors, jnp.where(third, -vectors, zero)),
        jnp.where(first, down, jnp.where(second, up, zero)),
        jnp.where(first, down2, jnp.where(third, up2, zero)),
        jnp.where(second, down, jnp.where(third, up, zero)),
    )
    for slot, part in enumerate(parts):
        high = part.astype(BF16)
        low = (part - high.astype(F32)).astype(BF16)
        side[slot * NARROW : (slot + 1) * NARROW, 0:LANES] = high
        side[slot * NARROW : (slot + 1) * NARROW, LANES : 2 * LANES] = low


def product(high, low, side):
    both = jnp.dot(high, side[...], preferred_element_type=F32)
    rest = jnp.dot(low, side[:, 0:LANES], preferred_element_type=F32)
    return both[:, 0:LANES] + (both[:, LANES:] + rest)


def build_and_apply(mask, vectors, column, high, low, side, first_lane):
    across = vectors.T[SITE : SITE + SUMS, :]
    across_x, across_y, across_z = across[0:1, :], across[1:2, :], across[2:3, :]

    def rows16(step):
        rows = slice(step * 16, (step + 1) * 16)
        here_x, here_y, here_z = column[0, rows, :], column[1, rows, :], column[2, rows, :]
        keep = mask[step // 2 : step // 2 + 1, :]
        for tile in range(NARROW // LANES):
            lanes = slice(tile * LANES, (tile + 1) * LANES)
            dx = here_x - across_x[:, lanes]
            dy = here_y - across_y[:, lanes]
            dz = here_z - across_z[:, lanes]
            xx = dx * dx
            yy = dy * dy
            distance2 = xx + yy + dz * dz
            square = jnp.maximum(distance2, 1.0)
            inverse = lax.rsqrt(square)
            damping = 1.0 + jnp.tanh(1.25 * (square * inverse) - 3.0)
            inverse2 = inverse * inverse
            kept = keep[:, first_lane + tile * LANES : first_lane + (tile + 1) * LANES]
            weight = damping * (inverse2 * inverse2 * inverse) * kept
            radial = weight * distance2
            minus3 = -3.0 * weight
            along_x = minus3 * dx
            along_y = minus3 * dy
            entries = (
                radial + minus3 * xx,
                radial + minus3 * yy,
                along_x * dy,
                along_x * dz,
                along_y * dz,
            )
            for slot, entry in enumerate(entries):
                top = entry.astype(BF16)
                at = slice(slot * NARROW + tile * LANES, slot * NARROW + (tile + 1) * LANES)
                high[rows, at] = top
                low[rows, at] = (entry - top.astype(F32)).astype(BF16)

    outs = []
    for chunk in range(0, WIDE, CHUNK):
        for step in range(chunk // 16, (chunk + CHUNK) // 16):
            rows16(step)
        rows = slice(chunk, chunk + CHUNK)
        outs.append(product(high[rows, :], low[rows, :], side))
    return jnp.concatenate(outs, axis=0)


def first_own_kernel(mask, column, gathered, total, high, low, side):
    vectors = gathered[...].reshape(NARROW, LANES)
    right_side(vectors, side)
    total[...] = build_and_apply(mask, vectors, column, high, low, side, 0)


def first_other_kernel(mask, column, gathered, total, part_out, high, low, side):
    vectors = gathered[...].reshape(NARROW, LANES)
    right_side(vectors, side)
    out = build_and_apply(mask, vectors, column, high, low, side, NARROW)
    part_out[...] = (total[...] + out).reshape(GROUP, ATOMS, LANES)


def spare_sums(vectors):
    return jnp.where(lane_ids(ATOMS) < COMPS * RHS, 0.0, jnp.sum(vectors, axis=0))


def second_own_kernel(gathered, high, low, total, side):
    vectors = gathered[...]
    right_side(vectors.reshape(NARROW, LANES), side)
    out = product(high[...], low[...], side).reshape(GROUP, ATOMS, LANES) + spare_sums(vectors)[None]
    total[...] = out


def second_other_kernel(gathered, high, low, total, part_out, side):
    vectors = gathered[...]
    right_side(vectors.reshape(NARROW, LANES), side)
    out = product(high[...], low[...], side).reshape(GROUP, ATOMS, LANES) + spare_sums(vectors)[None]
    part_out[...] = total[...] + out


def shifted_kernel(parts, own, aux, out, work):
    coupled = jnp.sum(parts[...], axis=0)
    inside = lane_ids(ATOMS) < COMPS * RHS
    vector = jnp.where(inside, own[...], 0.0)
    mapped = aux[0:ATOMS, :] * vector + coupled
    sums = jnp.zeros((SUMS, LANES), F32)
    row = lax.broadcasted_iota(jnp.int32, (SUMS, LANES), 0)
    for slot, terms in enumerate((vector * vector, vector * mapped, mapped * mapped)):
        sums = jnp.where(row == slot, jnp.sum(terms, axis=0, keepdims=True), sums)
    sums = sum_components(sums)
    work[...] = jnp.zeros_like(work)
    work[SUM_ROW : SUM_ROW + SUMS, :] = pltpu.roll(sums, 4, 0)
    work[SUM_ROW + SUMS : SUM_ROW + 2 * SUMS, :] = pltpu.roll(sums, LANES - ATOMS, 1)
    payload = jnp.where(inside, mapped, work[...].T[0:ATOMS, :])
    for slot in range(HALF):
        out[slot] = payload


def second_kernel(gathered, high, low, part_out, side):
    vectors = gathered[...]
    right_side(vectors.reshape(WIDE, LANES), side)
    sums = jnp.where(lane_ids(ATOMS) < COMPS * RHS, 0.0, jnp.sum(vectors, axis=0))
    part_out[...] = product(high[...], low[...], side).reshape(GROUP, ATOMS, LANES) + sums[None]


def step_kernel(parts, own, shifted, aux, sums_out, state, work):
    total = jnp.sum(parts[...], axis=0)
    vector = own[...]
    mapped = shifted[0]
    twice = aux[0:ATOMS, :] * mapped + total
    work[...] = jnp.zeros_like(work)
    work[0:ATOMS, :] = total
    turned = work[...].T
    lane8 = lane_ids(SUMS)
    head = pltpu.roll(turned[SUM_ROW : SUM_ROW + SUMS, :], 4, 0)
    tail = pltpu.roll(turned[SUM_ROW + SUMS : SUM_ROW + 2 * SUMS, :], ATOMS, 1)
    sums = jnp.where(lane8 < ATOMS, head, jnp.where(lane8 < RHS, tail, 0.0))
    sums = sums + pltpu.roll(sums, RHS, 1) + pltpu.roll(sums, 2 * RHS, 1)
    bb, be, ee = sums[0:1, :], sums[1:2, :], sums[2:3, :]
    shift = aux[ATOMS : ATOMS + 1, :]
    bm = shift * bb + be
    step = bb / bm
    kept = be / bm
    beta = (bb * ee - be * be) / (bm * bm)
    residual = kept * vector - step * mapped
    direction = residual + beta * vector
    image = shift * direction + ((kept + beta) * mapped - step * twice)
    row = lax.broadcasted_iota(jnp.int32, (SUMS, LANES), 0)
    squares = jnp.sum(residual * residual, axis=0, keepdims=True)
    curvature = jnp.sum(direction * image, axis=0, keepdims=True)
    both = sum_components(jnp.where(row == 0, squares, jnp.where(row == 1, curvature, 0.0)))
    lane = lax.broadcasted_iota(jnp.int32, (1, LANES), 1)
    packed = jnp.where(lane < RHS, both[0:1, :], jnp.where(lane < 2 * RHS, both[1:2, :], 0.0))
    sums_out[...] = jnp.broadcast_to(packed, sums_out.shape)
    state[0] = step * vector
    state[1] = direction
    state[2] = residual
    state[3] = image


def pair_kernel(sums, swapped, out):
    out[...] = jnp.broadcast_to((sums[...] + swapped[...])[None], out.shape)


def finish_kernel(gathered, state, dipoles, residual):
    total = jnp.sum(gathered[...], axis=0)
    total = jnp.broadcast_to(jnp.sum(total, axis=0, keepdims=True), (SUMS, LANES))
    first, second, third = component_lanes(SUMS)
    up = pltpu.roll(total, RHS, 1)
    up2 = pltpu.roll(total, 2 * RHS, 1)
    down = pltpu.roll(total, LANES - RHS, 1)
    squares = jnp.where(first, total, jnp.where(second, up, up2))
    curvature = jnp.where(first, down, jnp.where(second, total, jnp.where(third, up, 1.0)))
    step = (squares / curvature)[0:1, :]
    for out, value in (
        (dipoles, state[0] + step * state[1]),
        (residual, state[2] - step * state[3]),
    ):
        for comp in range(COMPS):
            out[comp] = value[:, comp * RHS : (comp + 1) * RHS]


def shape(*dims, dtype=F32):
    return jax.ShapeDtypeStruct(dims, dtype)


def whole(*dims):
    return pl.BlockSpec(dims, lambda i: (0,) * len(dims))


def core_swap(value):
    return lax.ppermute(value, "core", [(0, 1), (1, 0)])


def gather_own(value):
    return lax.all_to_all(value, "z", 0, 0)


def local(external_field, jitter, species, alpha_table, block_cell, tile_map):
    ids = jnp.stack([lax.axis_index("row"), lax.axis_index(("z", "core"))]).astype(jnp.int32)
    jitters = lax.all_to_all(jnp.broadcast_to(jitter, (GROUP, COMPS, ATOMS)), "row", 0, 0)
    vec, vector, cells = pl.pallas_call(
        prepare_kernel,
        out_shape=(
            shape(HALF, ATOMS, LANES),
            shape(ATOMS, LANES),
            shape(GROUP * GROUP, dtype=jnp.int32),
        ),
        in_specs=[SMEM, VMEM, HBM, HBM],
        out_specs=(VMEM, VMEM, VMEM),
        scratch_shapes=[
            pltpu.SMEM((GROUP * GROUP,), jnp.int32),
            pltpu.VMEM((COMPS, ATOMS, RHS), F32),
            pltpu.VMEM((COMPS, ATOMS), F32),
            SQUARE,
            pltpu.VMEM((ATOMS, LANES), F32),
            pltpu.SemaphoreType.DMA((3,)),
        ],
        compiler_params=PARAMS,
        name="prepare",
    )(ids, block_cell, external_field.transpose(0, 2, 1), jitter)
    aux, mask, column = pl.pallas_call(
        side_kernel,
        out_shape=(shape(ATOMS + SUMS, LANES), shape(GROUP, WIDE), shape(COMPS, WIDE, LANES)),
        in_specs=[SMEM, HBM, HBM, HBM, VMEM, VMEM],
        out_specs=(VMEM, VMEM, VMEM),
        scratch_shapes=[
            pltpu.VMEM((ATOMS,), jnp.int32),
            pltpu.VMEM((4, 12), F32),
            pltpu.VMEM((GROUP * GROUP, GROUP * GROUP), jnp.int32),
            pltpu.SMEM((GROUP * GROUP,), jnp.int32),
            SQUARE,
            pltpu.SemaphoreType.DMA((4,)),
        ],
        compiler_params=PARAMS,
        name="side",
    )(ids, species, alpha_table.T, tile_map, cells, jitters)
    own = gather_own(vec)
    own, aux, mask, column = lax.optimization_barrier((own, aux, mask, column))
    other = core_swap(own)
    side = pltpu.VMEM((PAIRS * NARROW, 2 * LANES), BF16)
    tile = shape(WIDE, PAIRS * NARROW, dtype=BF16)
    total, high0, low0 = pl.pallas_call(
        first_own_kernel,
        out_shape=(shape(WIDE, LANES), tile, tile),
        in_specs=[VMEM] * 3,
        out_specs=(VMEM, VMEM, VMEM),
        scratch_shapes=[side],
        compiler_params=PARAMS,
        name="first_own",
    )(mask, column, own)
    part, high1, low1 = pl.pallas_call(
        first_other_kernel,
        out_shape=(shape(GROUP, ATOMS, LANES), tile, tile),
        in_specs=[VMEM] * 4,
        out_specs=(VMEM, VMEM, VMEM),
        scratch_shapes=[side],
        compiler_params=PARAMS,
        name="first_other",
    )(mask, column, other, total)
    parts = lax.all_to_all(part, "row", 0, 0)
    blocks = whole(GROUP, ATOMS, LANES)
    block = whole(1, ATOMS, LANES)
    shifted = pl.pallas_call(
        shifted_kernel,
        grid=(1,),
        out_shape=shape(HALF, ATOMS, LANES),
        in_specs=[blocks, whole(ATOMS, LANES), whole(ATOMS + SUMS, LANES)],
        out_specs=whole(HALF, ATOMS, LANES),
        scratch_shapes=[SQUARE],
        compiler_params=PARAMS,
        name="shifted",
    )(parts, vector, aux)
    own2 = gather_own(shifted)
    other2 = core_swap(own2)
    total2 = pl.pallas_call(
        second_own_kernel,
        out_shape=shape(GROUP, ATOMS, LANES),
        in_specs=[VMEM] * 3,
        out_specs=VMEM,
        scratch_shapes=[side],
        compiler_params=PARAMS,
        name="second_own",
    )(own2, high0, low0)
    part2 = pl.pallas_call(
        second_other_kernel,
        out_shape=shape(GROUP, ATOMS, LANES),
        in_specs=[VMEM] * 4,
        out_specs=VMEM,
        scratch_shapes=[side],
        compiler_params=PARAMS,
        name="second_other",
    )(other2, high1, low1, total2)
    parts2 = lax.all_to_all(part2, "row", 0, 0)
    sums, state = pl.pallas_call(
        step_kernel,
        grid=(1,),
        out_shape=(shape(SUMS, LANES), shape(4, ATOMS, LANES)),
        in_specs=[blocks, whole(ATOMS, LANES), block, whole(ATOMS + SUMS, LANES)],
        out_specs=(whole(SUMS, LANES), whole(4, ATOMS, LANES)),
        scratch_shapes=[SQUARE],
        compiler_params=PARAMS,
        name="step",
    )(parts2, vector, shifted, aux)
    pair = pl.pallas_call(
        pair_kernel,
        out_shape=shape(GROUP, SUMS, LANES),
        in_specs=[VMEM, VMEM],
        out_specs=VMEM,
        compiler_params=PARAMS,
        name="pair",
    )(sums, core_swap(sums))
    pair = pair.reshape(GROUP * HALF, 1, LANES)
    all_sums = lax.all_to_all(pair, ("row", "z"), 0, 0).reshape(GROUP, SUMS, LANES)
    dipoles, residual = pl.pallas_call(
        finish_kernel,
        out_shape=(shape(COMPS, ATOMS, RHS), shape(COMPS, ATOMS, RHS)),
        in_specs=[VMEM, VMEM],
        out_specs=(VMEM, VMEM),
        compiler_params=PARAMS,
        name="finish",
    )(all_sums, state)
    return dipoles.transpose(0, 2, 1), residual.transpose(0, 2, 1)


def solution(mesh):
    split = Mesh(mesh.devices.reshape(GROUP, HALF, 2), ("row", "z", "core"))
    every = ("row", "z", "core")
    return jax.shard_map(
        local,
        mesh=split,
        in_specs=(P(None, None, every), P(None, every), P(every), P(), P(), P()),
        out_specs=(P(None, None, every), P(None, None, every)),
        check_vma=False,
    )
```

```python
import jax
import jax.numpy as jnp
from jax import lax
from jax.experimental import pallas as pl
from jax.experimental.pallas import tpu as pltpu
from jax.sharding import Mesh, PartitionSpec as P

COMPS = 3
RHS = 36
ATOMS = 32
GROUP = 16
HALF = 8
LANES = 128
SUMS = 8
SITE = 120
SUM_ROW = 104
CELL_ROW = 8
WIDE = GROUP * ATOMS
NARROW = HALF * ATOMS
CHUNK = 256
PAIRS = 5
SPACING = 2.0
F32 = jnp.float32
BF16 = jnp.bfloat16

VMEM = pl.BlockSpec(memory_space=pltpu.VMEM)
SMEM = pl.BlockSpec(memory_space=pltpu.SMEM)
SQUARE = pltpu.VMEM((LANES, LANES), F32)
PARAMS = pltpu.CompilerParams(vmem_limit_bytes=16 * 1024 * 1024)


def lane_ids(rows):
    return lax.broadcasted_iota(jnp.int32, (rows, LANES), 1)


def component_lanes(rows):
    lanes = lane_ids(rows)
    first = lanes < RHS
    second = (lanes >= RHS) & (lanes < 2 * RHS)
    third = (lanes >= 2 * RHS) & (lanes < COMPS * RHS)
    return first, second, third


def sum_components(value):
    first, second, third = component_lanes(SUMS)
    up = pltpu.roll(value, RHS, 1)
    up2 = pltpu.roll(value, 2 * RHS, 1)
    down = pltpu.roll(value, LANES - RHS, 1)
    down2 = pltpu.roll(value, LANES - 2 * RHS, 1)
    of_first = value + down + down2
    of_second = up + value + down
    of_third = up2 + up + value
    return jnp.where(first, of_first, jnp.where(second, of_second, jnp.where(third, of_third, 1.0)))


def prepare_kernel(ids, pack, field, vec_out, own_out, work, wide):
    own = ids[0] * GROUP + ids[1]
    index = lax.broadcasted_iota(jnp.int32, (SUMS, LANES), 0) * LANES + lane_ids(SUMS)
    found = jnp.where(index == own, pack[CELL_ROW : CELL_ROW + SUMS, :], 0.0)
    cell = jnp.sum(jnp.sum(found, axis=0, keepdims=True), axis=1, keepdims=True).astype(jnp.int32)
    comp = lax.broadcasted_iota(jnp.int32, (SUMS, LANES), 0)
    work[...] = jnp.zeros_like(work)
    work[SITE : SITE + SUMS, :] = lattice(comp, lane_ids(SUMS), cell) + pack[0:SUMS, :]
    wide[...] = work[...].T[0:ATOMS, :]
    for comp in range(COMPS):
        wide[:, comp * RHS : (comp + 1) * RHS] = field[comp]
    turned = wide[...]
    own_out[...] = turned
    for slot in range(HALF):
        vec_out[slot] = turned


def lattice(comp, atom, cell):
    inner = jnp.where(comp == 0, atom >> 3, jnp.where(comp == 1, (atom >> 1) & 3, atom & 1))
    corner = jnp.where(comp == 0, (cell >> 5) * 4, jnp.where(comp == 1, ((cell >> 2) & 7) * 4, (cell & 3) * 2))
    return (corner + inner).astype(F32) * SPACING


def side_kernel(ids, pack, species, tile_map, jitters, aux_out, mask_out, column, work):
    alpha = species[4:SUMS, :]
    lane = lax.broadcasted_iota(jnp.int32, (4, LANES), 1)
    rhs_lane = jnp.where(lane >= 2 * RHS, lane - 2 * RHS, jnp.where(lane >= RHS, lane - RHS, lane))
    table = jnp.ones((4, LANES), F32)
    for freq in range(12):
        table = jnp.where(
            (rhs_lane >= 3 * freq) & (rhs_lane < 3 * freq + 3),
            jnp.broadcast_to(alpha[:, freq : freq + 1], (4, LANES)),
            table,
        )
    inverse = 1.0 / table
    shift = 0.25 * ((inverse[0:1] + inverse[1:2]) + (inverse[2:3] + inverse[3:4]))
    work[0:SUMS, :] = species[...]
    kinds = jnp.broadcast_to(work[...].T[0:ATOMS, 0:1], (ATOMS, LANES))
    diag = jnp.zeros((ATOMS, LANES), F32)
    for kind in range(4):
        diag = jnp.where(kinds == float(kind), inverse[kind : kind + 1] - shift, diag)
    aux_out[0:ATOMS, :] = diag
    aux_out[ATOMS : ATOMS + SUMS, :] = jnp.broadcast_to(shift, (SUMS, LANES))

    blocks = GROUP * GROUP
    active = jnp.where(tile_map[...] != 0, 1.0, 0.0).astype(BF16)
    place = lax.broadcasted_iota(jnp.int32, (GROUP, blocks), 1)
    wanted = lax.broadcasted_iota(jnp.int32, (GROUP, blocks), 0) * GROUP + ids[1]
    pick = jnp.where(place == wanted, 1.0, 0.0).astype(BF16)
    lines = jnp.dot(pick, active, preferred_element_type=F32).astype(BF16)
    slot = lax.broadcasted_iota(jnp.int32, (blocks, WIDE), 1) // ATOMS
    wanted = ids[0] * GROUP + (slot % HALF) * 2 + ((ids[1] % 2) ^ (slot // HALF))
    place = lax.broadcasted_iota(jnp.int32, (blocks, WIDE), 0)
    spread = jnp.where(place == wanted, 1.0, 0.0).astype(BF16)
    mask_out[...] = 0.5 * jnp.dot(lines, spread, preferred_element_type=F32)

    cells = jnp.concatenate([pack[CELL_ROW : CELL_ROW + 1, :], pack[CELL_ROW + 1 : CELL_ROW + 2, :]], axis=1)
    place = lax.broadcasted_iota(jnp.int32, (LANES, blocks), 1)
    wanted = (lax.broadcasted_iota(jnp.int32, (LANES, blocks), 0) >> 3) * GROUP + ids[1]
    cell = jnp.sum(jnp.where(place == wanted, cells, 0.0), axis=1, keepdims=True).astype(jnp.int32)
    comp = lax.broadcasted_iota(jnp.int32, (LANES, LANES), 0) & 7
    work[...] = jnp.zeros_like(work)
    for slot in range(GROUP):
        work[slot * SUMS : slot * SUMS + COMPS, 0:ATOMS] = jitters[slot]
    down = (lattice(comp, lane_ids(LANES), cell) + work[...]).T[0:ATOMS, :]
    for slot in range(GROUP):
        rows = slice(slot * ATOMS, (slot + 1) * ATOMS)
        for comp in range(COMPS):
            lane = slot * SUMS + comp
            column[comp, rows, :] = jnp.broadcast_to(down[:, lane : lane + 1], (ATOMS, LANES))


def right_side(vectors, side):
    first, second, third = component_lanes(NARROW)
    zero = jnp.zeros_like(vectors)
    up = pltpu.roll(vectors, RHS, 1)
    up2 = pltpu.roll(vectors, 2 * RHS, 1)
    down = pltpu.roll(vectors, LANES - RHS, 1)
    down2 = pltpu.roll(vectors, LANES - 2 * RHS, 1)
    parts = (
        jnp.where(first, vectors, jnp.where(third, -vectors, zero)),
        jnp.where(second, vectors, jnp.where(third, -vectors, zero)),
        jnp.where(first, down, jnp.where(second, up, zero)),
        jnp.where(first, down2, jnp.where(third, up2, zero)),
        jnp.where(second, down, jnp.where(third, up, zero)),
    )
    for slot, part in enumerate(parts):
        high = part.astype(BF16)
        low = (part - high.astype(F32)).astype(BF16)
        side[slot * NARROW : (slot + 1) * NARROW, 0:LANES] = high
        side[slot * NARROW : (slot + 1) * NARROW, LANES : 2 * LANES] = low


def product(high, low, side):
    both = jnp.dot(high, side[...], preferred_element_type=F32)
    rest = jnp.dot(low, side[:, 0:LANES], preferred_element_type=F32)
    return both[:, 0:LANES] + (both[:, LANES:] + rest)


def build_and_apply(mask, vectors, column, high, low, side, first_lane):
    across = vectors.T[SITE : SITE + SUMS, :]
    across_x, across_y, across_z = across[0:1, :], across[1:2, :], across[2:3, :]

    def rows16(step):
        rows = slice(step * 16, (step + 1) * 16)
        here_x, here_y, here_z = column[0, rows, :], column[1, rows, :], column[2, rows, :]
        keep = mask[step // 2 : step // 2 + 1, :]
        for tile in range(NARROW // LANES):
            lanes = slice(tile * LANES, (tile + 1) * LANES)
            dx = here_x - across_x[:, lanes]
            dy = here_y - across_y[:, lanes]
            dz = here_z - across_z[:, lanes]
            xx = dx * dx
            yy = dy * dy
            distance2 = xx + yy + dz * dz
            square = jnp.maximum(distance2, 1.0)
            inverse = lax.rsqrt(square)
            damping = 1.0 + jnp.tanh(1.25 * (square * inverse) - 3.0)
            inverse2 = inverse * inverse
            kept = keep[:, first_lane + tile * LANES : first_lane + (tile + 1) * LANES]
            weight = damping * (inverse2 * inverse2 * inverse) * kept
            radial = weight * distance2
            minus3 = -3.0 * weight
            along_x = minus3 * dx
            along_y = minus3 * dy
            entries = (
                radial + minus3 * xx,
                radial + minus3 * yy,
                along_x * dy,
                along_x * dz,
                along_y * dz,
            )
            for slot, entry in enumerate(entries):
                top = entry.astype(BF16)
                at = slice(slot * NARROW + tile * LANES, slot * NARROW + (tile + 1) * LANES)
                high[rows, at] = top
                low[rows, at] = (entry - top.astype(F32)).astype(BF16)

    outs = []
    for chunk in range(0, WIDE, CHUNK):
        for step in range(chunk // 16, (chunk + CHUNK) // 16):
            rows16(step)
        rows = slice(chunk, chunk + CHUNK)
        outs.append(product(high[rows, :], low[rows, :], side))
    return jnp.concatenate(outs, axis=0)


def first_own_kernel(mask, column, gathered, total, high, low, side):
    vectors = gathered[...].reshape(NARROW, LANES)
    right_side(vectors, side)
    total[...] = build_and_apply(mask, vectors, column, high, low, side, 0)


def first_other_kernel(mask, column, gathered, total, part_out, high, low, side):
    vectors = gathered[...].reshape(NARROW, LANES)
    right_side(vectors, side)
    out = build_and_apply(mask, vectors, column, high, low, side, NARROW)
    part_out[...] = (total[...] + out).reshape(GROUP, ATOMS, LANES)


def spare_sums(vectors):
    return jnp.where(lane_ids(ATOMS) < COMPS * RHS, 0.0, jnp.sum(vectors, axis=0))


def second_own_kernel(gathered, high, low, total, side):
    vectors = gathered[...]
    right_side(vectors.reshape(NARROW, LANES), side)
    out = product(high[...], low[...], side).reshape(GROUP, ATOMS, LANES) + spare_sums(vectors)[None]
    total[...] = out


def second_other_kernel(gathered, high, low, total, part_out, side):
    vectors = gathered[...]
    right_side(vectors.reshape(NARROW, LANES), side)
    out = product(high[...], low[...], side).reshape(GROUP, ATOMS, LANES) + spare_sums(vectors)[None]
    part_out[...] = total[...] + out


def shifted_kernel(parts, own, aux, out, work):
    coupled = jnp.sum(parts[...], axis=0)
    inside = lane_ids(ATOMS) < COMPS * RHS
    vector = jnp.where(inside, own[...], 0.0)
    mapped = aux[0:ATOMS, :] * vector + coupled
    sums = jnp.zeros((SUMS, LANES), F32)
    row = lax.broadcasted_iota(jnp.int32, (SUMS, LANES), 0)
    for slot, terms in enumerate((vector * vector, vector * mapped, mapped * mapped)):
        sums = jnp.where(row == slot, jnp.sum(terms, axis=0, keepdims=True), sums)
    sums = sum_components(sums)
    work[...] = jnp.zeros_like(work)
    work[SUM_ROW : SUM_ROW + SUMS, :] = pltpu.roll(sums, 4, 0)
    work[SUM_ROW + SUMS : SUM_ROW + 2 * SUMS, :] = pltpu.roll(sums, LANES - ATOMS, 1)
    payload = jnp.where(inside, mapped, work[...].T[0:ATOMS, :])
    for slot in range(HALF):
        out[slot] = payload


def second_kernel(gathered, high, low, part_out, side):
    vectors = gathered[...]
    right_side(vectors.reshape(WIDE, LANES), side)
    sums = jnp.where(lane_ids(ATOMS) < COMPS * RHS, 0.0, jnp.sum(vectors, axis=0))
    part_out[...] = product(high[...], low[...], side).reshape(GROUP, ATOMS, LANES) + sums[None]


def step_kernel(parts, own, shifted, aux, sums_out, state, work):
    total = jnp.sum(parts[...], axis=0)
    vector = own[...]
    mapped = shifted[0]
    twice = aux[0:ATOMS, :] * mapped + total
    work[...] = jnp.zeros_like(work)
    work[0:ATOMS, :] = total
    turned = work[...].T
    lane8 = lane_ids(SUMS)
    head = pltpu.roll(turned[SUM_ROW : SUM_ROW + SUMS, :], 4, 0)
    tail = pltpu.roll(turned[SUM_ROW + SUMS : SUM_ROW + 2 * SUMS, :], ATOMS, 1)
    sums = jnp.where(lane8 < ATOMS, head, jnp.where(lane8 < RHS, tail, 0.0))
    sums = sums + pltpu.roll(sums, RHS, 1) + pltpu.roll(sums, 2 * RHS, 1)
    bb, be, ee = sums[0:1, :], sums[1:2, :], sums[2:3, :]
    shift = aux[ATOMS : ATOMS + 1, :]
    bm = shift * bb + be
    step = bb / bm
    kept = be / bm
    beta = (bb * ee - be * be) / (bm * bm)
    residual = kept * vector - step * mapped
    direction = residual + beta * vector
    image = shift * direction + ((kept + beta) * mapped - step * twice)
    row = lax.broadcasted_iota(jnp.int32, (SUMS, LANES), 0)
    squares = jnp.sum(residual * residual, axis=0, keepdims=True)
    curvature = jnp.sum(direction * image, axis=0, keepdims=True)
    both = sum_components(jnp.where(row == 0, squares, jnp.where(row == 1, curvature, 0.0)))
    lane = lax.broadcasted_iota(jnp.int32, (1, LANES), 1)
    packed = jnp.where(lane < RHS, both[0:1, :], jnp.where(lane < 2 * RHS, both[1:2, :], 0.0))
    sums_out[...] = jnp.broadcast_to(packed, sums_out.shape)
    state[0] = step * vector
    state[1] = direction
    state[2] = residual
    state[3] = image


def pair_kernel(sums, swapped, out):
    out[...] = jnp.broadcast_to((sums[...] + swapped[...])[None], out.shape)


def finish_kernel(gathered, state, dipoles, residual):
    total = jnp.sum(gathered[...], axis=0)
    total = jnp.broadcast_to(jnp.sum(total, axis=0, keepdims=True), (SUMS, LANES))
    first, second, third = component_lanes(SUMS)
    up = pltpu.roll(total, RHS, 1)
    up2 = pltpu.roll(total, 2 * RHS, 1)
    down = pltpu.roll(total, LANES - RHS, 1)
    squares = jnp.where(first, total, jnp.where(second, up, up2))
    curvature = jnp.where(first, down, jnp.where(second, total, jnp.where(third, up, 1.0)))
    step = (squares / curvature)[0:1, :]
    for out, value in (
        (dipoles, state[0] + step * state[1]),
        (residual, state[2] - step * state[3]),
    ):
        for comp in range(COMPS):
            out[comp] = value[:, comp * RHS : (comp + 1) * RHS]


def shape(*dims, dtype=F32):
    return jax.ShapeDtypeStruct(dims, dtype)


def whole(*dims):
    return pl.BlockSpec(dims, lambda i: (0,) * len(dims))


def core_swap(value):
    return lax.ppermute(value, "core", [(0, 1), (1, 0)])


def gather_own(value):
    return lax.all_to_all(value, "z", 0, 0)


def local(external_field, jitter, species, alpha_table, block_cell, tile_map):
    ids = jnp.stack([lax.axis_index("row"), lax.axis_index(("z", "core"))]).astype(jnp.int32)
    jitters = lax.all_to_all(jnp.broadcast_to(jitter, (GROUP, COMPS, ATOMS)), "row", 0, 0)
    pack = jnp.concatenate(
        [
            jnp.pad(jitter, ((0, CELL_ROW - COMPS), (0, LANES - ATOMS))),
            jnp.pad(block_cell.astype(F32).reshape(2, LANES), ((0, 6), (0, 0))),
        ]
    )
    kinds = jnp.concatenate(
        [
            jnp.pad(species.astype(F32)[None], ((0, 3), (0, LANES - ATOMS))),
            jnp.pad(alpha_table.T, ((0, 0), (0, LANES - 12))),
        ]
    )
    vec, vector = pl.pallas_call(
        prepare_kernel,
        out_shape=(shape(HALF, ATOMS, LANES), shape(ATOMS, LANES)),
        in_specs=[SMEM, VMEM, VMEM],
        out_specs=(VMEM, VMEM),
        scratch_shapes=[SQUARE, pltpu.VMEM((ATOMS, LANES), F32)],
        compiler_params=PARAMS,
        name="prepare",
    )(ids, pack, external_field.transpose(0, 2, 1))
    aux, mask, column = pl.pallas_call(
        side_kernel,
        out_shape=(shape(ATOMS + SUMS, LANES), shape(GROUP, WIDE), shape(COMPS, WIDE, LANES)),
        in_specs=[SMEM, VMEM, VMEM, VMEM, VMEM],
        out_specs=(VMEM, VMEM, VMEM),
        scratch_shapes=[SQUARE],
        compiler_params=PARAMS,
        name="side",
    )(ids, pack, kinds, tile_map, jitters)
    own = gather_own(vec)
    own, aux, mask, column = lax.optimization_barrier((own, aux, mask, column))
    other = core_swap(own)
    side = pltpu.VMEM((PAIRS * NARROW, 2 * LANES), BF16)
    tile = shape(WIDE, PAIRS * NARROW, dtype=BF16)
    total, high0, low0 = pl.pallas_call(
        first_own_kernel,
        out_shape=(shape(WIDE, LANES), tile, tile),
        in_specs=[VMEM] * 3,
        out_specs=(VMEM, VMEM, VMEM),
        scratch_shapes=[side],
        compiler_params=PARAMS,
        name="first_own",
    )(mask, column, own)
    part, high1, low1 = pl.pallas_call(
        first_other_kernel,
        out_shape=(shape(GROUP, ATOMS, LANES), tile, tile),
        in_specs=[VMEM] * 4,
        out_specs=(VMEM, VMEM, VMEM),
        scratch_shapes=[side],
        compiler_params=PARAMS,
        name="first_other",
    )(mask, column, other, total)
    parts = lax.all_to_all(part, "row", 0, 0)
    blocks = whole(GROUP, ATOMS, LANES)
    block = whole(1, ATOMS, LANES)
    shifted = pl.pallas_call(
        shifted_kernel,
        grid=(1,),
        out_shape=shape(HALF, ATOMS, LANES),
        in_specs=[blocks, whole(ATOMS, LANES), whole(ATOMS + SUMS, LANES)],
        out_specs=whole(HALF, ATOMS, LANES),
        scratch_shapes=[SQUARE],
        compiler_params=PARAMS,
        name="shifted",
    )(parts, vector, aux)
    own2 = gather_own(shifted)
    other2 = core_swap(own2)
    total2 = pl.pallas_call(
        second_own_kernel,
        out_shape=shape(GROUP, ATOMS, LANES),
        in_specs=[VMEM] * 3,
        out_specs=VMEM,
        scratch_shapes=[side],
        compiler_params=PARAMS,
        name="second_own",
    )(own2, high0, low0)
    part2 = pl.pallas_call(
        second_other_kernel,
        out_shape=shape(GROUP, ATOMS, LANES),
        in_specs=[VMEM] * 4,
        out_specs=VMEM,
        scratch_shapes=[side],
        compiler_params=PARAMS,
        name="second_other",
    )(other2, high1, low1, total2)
    parts2 = lax.all_to_all(part2, "row", 0, 0)
    sums, state = pl.pallas_call(
        step_kernel,
        grid=(1,),
        out_shape=(shape(SUMS, LANES), shape(4, ATOMS, LANES)),
        in_specs=[blocks, whole(ATOMS, LANES), block, whole(ATOMS + SUMS, LANES)],
        out_specs=(whole(SUMS, LANES), whole(4, ATOMS, LANES)),
        scratch_shapes=[SQUARE],
        compiler_params=PARAMS,
        name="step",
    )(parts2, vector, shifted, aux)
    pair = pl.pallas_call(
        pair_kernel,
        out_shape=shape(GROUP, SUMS, LANES),
        in_specs=[VMEM, VMEM],
        out_specs=VMEM,
        compiler_params=PARAMS,
        name="pair",
    )(sums, core_swap(sums))
    pair = pair.reshape(GROUP * HALF, 1, LANES)
    all_sums = lax.all_to_all(pair, ("row", "z"), 0, 0).reshape(GROUP, SUMS, LANES)
    dipoles, residual = pl.pallas_call(
        finish_kernel,
        out_shape=(shape(COMPS, ATOMS, RHS), shape(COMPS, ATOMS, RHS)),
        in_specs=[VMEM, VMEM],
        out_specs=(VMEM, VMEM),
        compiler_params=PARAMS,
        name="finish",
    )(all_sums, state)
    return dipoles.transpose(0, 2, 1), residual.transpose(0, 2, 1)


def solution(mesh):
    split = Mesh(mesh.devices.reshape(GROUP, HALF, 2), ("row", "z", "core"))
    every = ("row", "z", "core")
    return jax.shard_map(
        local,
        mesh=split,
        in_specs=(P(None, None, every), P(None, every), P(every), P(), P(), P()),
        out_specs=(P(None, None, every), P(None, None, every)),
        check_vma=False,
    )
```

```python
import jax
import jax.numpy as jnp
from jax import lax
from jax.experimental import pallas as pl
from jax.experimental.pallas import tpu as pltpu
from jax.sharding import Mesh, PartitionSpec as P

COMPS = 3
RHS = 36
ATOMS = 32
GROUP = 16
HALF = 8
LANES = 128
SUMS = 8
SITE = 120
SUM_ROW = 104
CELL_ROW = 16
WIDE = GROUP * ATOMS
NARROW = HALF * ATOMS
CHUNK = 256
PAIRS = 5
SPACING = 2.0
F32 = jnp.float32
BF16 = jnp.bfloat16

VMEM = pl.BlockSpec(memory_space=pltpu.VMEM)
SMEM = pl.BlockSpec(memory_space=pltpu.SMEM)
SQUARE = pltpu.VMEM((LANES, LANES), F32)
PARAMS = pltpu.CompilerParams(vmem_limit_bytes=16 * 1024 * 1024)


def lane_ids(rows):
    return lax.broadcasted_iota(jnp.int32, (rows, LANES), 1)


def component_lanes(rows):
    lanes = lane_ids(rows)
    first = lanes < RHS
    second = (lanes >= RHS) & (lanes < 2 * RHS)
    third = (lanes >= 2 * RHS) & (lanes < COMPS * RHS)
    return first, second, third


def sum_components(value):
    first, second, third = component_lanes(SUMS)
    up = pltpu.roll(value, RHS, 1)
    up2 = pltpu.roll(value, 2 * RHS, 1)
    down = pltpu.roll(value, LANES - RHS, 1)
    down2 = pltpu.roll(value, LANES - 2 * RHS, 1)
    of_first = value + down + down2
    of_second = up + value + down
    of_third = up2 + up + value
    return jnp.where(first, of_first, jnp.where(second, of_second, jnp.where(third, of_third, 1.0)))


def block_rows(own, pack, jitter_row, field, work, wide):
    index = lax.broadcasted_iota(jnp.int32, (SUMS, LANES), 0) * LANES + lane_ids(SUMS)
    found = jnp.where(index == own, pack[CELL_ROW : CELL_ROW + SUMS, :], 0.0)
    cell = jnp.sum(jnp.sum(found, axis=0, keepdims=True), axis=1, keepdims=True).astype(jnp.int32)
    comp = lax.broadcasted_iota(jnp.int32, (SUMS, LANES), 0)
    work[SITE : SITE + SUMS, :] = lattice(comp, lane_ids(SUMS), cell) + pack[jitter_row : jitter_row + SUMS, :]
    wide[...] = work[...].T[0:ATOMS, :]
    for comp in range(COMPS):
        wide[:, comp * RHS : (comp + 1) * RHS] = field[comp]
    return wide[...]


def prepare_kernel(ids, pack, field, partner, vec_out, own_out, work, wide):
    work[...] = jnp.zeros_like(work)
    block = ids[0] * GROUP + ids[1]
    core = ids[1] % 2
    mine = block_rows(block, pack, 0, field, work, wide)
    own_out[...] = mine
    here = pl.ds(pl.multiple_of(core * ATOMS, ATOMS), ATOMS)
    for slot in range(GROUP):
        vec_out[slot, here, :] = mine
    theirs = block_rows(block ^ 1, pack, SUMS, partner, work, wide)
    there = pl.ds(pl.multiple_of((1 - core) * ATOMS, ATOMS), ATOMS)
    for slot in range(GROUP):
        vec_out[slot, there, :] = theirs


def pick_kernel(ids, mine, theirs, own, other, column):
    core = ids[1] % 2
    line = pl.ds(pl.multiple_of((ids[0] % 2) * HALF, HALF), HALF)
    here = pl.ds(pl.multiple_of(core * ATOMS, ATOMS), ATOMS)
    there = pl.ds(pl.multiple_of((1 - core) * ATOMS, ATOMS), ATOMS)

    def take(along_z, along_row):
        own[...] = along_z[line, here, :]
        other[...] = along_z[line, there, :]
        rows = along_row[:, here, :].reshape(WIDE, LANES)
        for comp in range(COMPS):
            column[comp] = jnp.broadcast_to(rows[:, SITE + comp : SITE + comp + 1], (WIDE, LANES))

    @pl.when(core == 0)
    def _():
        take(theirs, mine)

    @pl.when(core == 1)
    def _():
        take(mine, theirs)


def lattice(comp, atom, cell):
    inner = jnp.where(comp == 0, atom >> 3, jnp.where(comp == 1, (atom >> 1) & 3, atom & 1))
    corner = jnp.where(comp == 0, (cell >> 5) * 4, jnp.where(comp == 1, ((cell >> 2) & 7) * 4, (cell & 3) * 2))
    return (corner + inner).astype(F32) * SPACING


def side_kernel(ids, species, tile_map, aux_out, mask_out, work):
    alpha = species[4:SUMS, :]
    lane = lax.broadcasted_iota(jnp.int32, (4, LANES), 1)
    rhs_lane = jnp.where(lane >= 2 * RHS, lane - 2 * RHS, jnp.where(lane >= RHS, lane - RHS, lane))
    table = jnp.ones((4, LANES), F32)
    for freq in range(12):
        table = jnp.where(
            (rhs_lane >= 3 * freq) & (rhs_lane < 3 * freq + 3),
            jnp.broadcast_to(alpha[:, freq : freq + 1], (4, LANES)),
            table,
        )
    inverse = 1.0 / table
    shift = 0.25 * ((inverse[0:1] + inverse[1:2]) + (inverse[2:3] + inverse[3:4]))
    work[0:SUMS, :] = species[...]
    kinds = jnp.broadcast_to(work[...].T[0:ATOMS, 0:1], (ATOMS, LANES))
    diag = jnp.zeros((ATOMS, LANES), F32)
    for kind in range(4):
        diag = jnp.where(kinds == float(kind), inverse[kind : kind + 1] - shift, diag)
    aux_out[0:ATOMS, :] = diag
    aux_out[ATOMS : ATOMS + SUMS, :] = jnp.broadcast_to(shift, (SUMS, LANES))

    blocks = GROUP * GROUP
    active = jnp.where(tile_map[...] != 0, 1.0, 0.0).astype(BF16)
    place = lax.broadcasted_iota(jnp.int32, (GROUP, blocks), 1)
    wanted = lax.broadcasted_iota(jnp.int32, (GROUP, blocks), 0) * GROUP + ids[1]
    pick = jnp.where(place == wanted, 1.0, 0.0).astype(BF16)
    lines = jnp.dot(pick, active, preferred_element_type=F32).astype(BF16)
    slot = lax.broadcasted_iota(jnp.int32, (blocks, WIDE), 1) // ATOMS
    wanted = ids[0] * GROUP + (slot % HALF) * 2 + ((ids[1] % 2) ^ (slot // HALF))
    place = lax.broadcasted_iota(jnp.int32, (blocks, WIDE), 0)
    spread = jnp.where(place == wanted, 1.0, 0.0).astype(BF16)
    mask_out[...] = 0.5 * jnp.dot(lines, spread, preferred_element_type=F32)


def right_side(vectors, side):
    first, second, third = component_lanes(NARROW)
    zero = jnp.zeros_like(vectors)
    up = pltpu.roll(vectors, RHS, 1)
    up2 = pltpu.roll(vectors, 2 * RHS, 1)
    down = pltpu.roll(vectors, LANES - RHS, 1)
    down2 = pltpu.roll(vectors, LANES - 2 * RHS, 1)
    parts = (
        jnp.where(first, vectors, jnp.where(third, -vectors, zero)),
        jnp.where(second, vectors, jnp.where(third, -vectors, zero)),
        jnp.where(first, down, jnp.where(second, up, zero)),
        jnp.where(first, down2, jnp.where(third, up2, zero)),
        jnp.where(second, down, jnp.where(third, up, zero)),
    )
    for slot, part in enumerate(parts):
        high = part.astype(BF16)
        low = (part - high.astype(F32)).astype(BF16)
        side[slot * NARROW : (slot + 1) * NARROW, 0:LANES] = high
        side[slot * NARROW : (slot + 1) * NARROW, LANES : 2 * LANES] = low


def product(high, low, side):
    both = jnp.dot(high, side[...], preferred_element_type=F32)
    rest = jnp.dot(low, side[:, 0:LANES], preferred_element_type=F32)
    return both[:, 0:LANES] + (both[:, LANES:] + rest)


def build_and_apply(mask, vectors, column, high, low, side, first_lane):
    across = vectors.T[SITE : SITE + SUMS, :]
    across_x, across_y, across_z = across[0:1, :], across[1:2, :], across[2:3, :]

    def rows16(step):
        rows = slice(step * 16, (step + 1) * 16)
        here_x, here_y, here_z = column[0, rows, :], column[1, rows, :], column[2, rows, :]
        keep = mask[step // 2 : step // 2 + 1, :]
        for tile in range(NARROW // LANES):
            lanes = slice(tile * LANES, (tile + 1) * LANES)
            dx = here_x - across_x[:, lanes]
            dy = here_y - across_y[:, lanes]
            dz = here_z - across_z[:, lanes]
            xx = dx * dx
            yy = dy * dy
            distance2 = xx + yy + dz * dz
            square = jnp.maximum(distance2, 1.0)
            inverse = lax.rsqrt(square)
            damping = 1.0 + jnp.tanh(1.25 * (square * inverse) - 3.0)
            inverse2 = inverse * inverse
            kept = keep[:, first_lane + tile * LANES : first_lane + (tile + 1) * LANES]
            weight = damping * (inverse2 * inverse2 * inverse) * kept
            radial = weight * distance2
            minus3 = -3.0 * weight
            along_x = minus3 * dx
            along_y = minus3 * dy
            entries = (
                radial + minus3 * xx,
                radial + minus3 * yy,
                along_x * dy,
                along_x * dz,
                along_y * dz,
            )
            for slot, entry in enumerate(entries):
                top = entry.astype(BF16)
                at = slice(slot * NARROW + tile * LANES, slot * NARROW + (tile + 1) * LANES)
                high[rows, at] = top
                low[rows, at] = (entry - top.astype(F32)).astype(BF16)

    outs = []
    for chunk in range(0, WIDE, CHUNK):
        for step in range(chunk // 16, (chunk + CHUNK) // 16):
            rows16(step)
        rows = slice(chunk, chunk + CHUNK)
        outs.append(product(high[rows, :], low[rows, :], side))
    return jnp.concatenate(outs, axis=0)


def first_own_kernel(mask, column, gathered, total, high, low, side):
    vectors = gathered[...].reshape(NARROW, LANES)
    right_side(vectors, side)
    total[...] = build_and_apply(mask, vectors, column, high, low, side, 0)


def first_other_kernel(mask, column, gathered, total, part_out, high, low, side):
    vectors = gathered[...].reshape(NARROW, LANES)
    right_side(vectors, side)
    out = build_and_apply(mask, vectors, column, high, low, side, NARROW)
    part_out[...] = (total[...] + out).reshape(GROUP, ATOMS, LANES)


def spare_sums(vectors):
    return jnp.where(lane_ids(ATOMS) < COMPS * RHS, 0.0, jnp.sum(vectors, axis=0))


def second_own_kernel(gathered, high, low, total, side):
    vectors = gathered[...]
    right_side(vectors.reshape(NARROW, LANES), side)
    out = product(high[...], low[...], side).reshape(GROUP, ATOMS, LANES) + spare_sums(vectors)[None]
    total[...] = out


def second_other_kernel(gathered, high, low, total, part_out, side):
    vectors = gathered[...]
    right_side(vectors.reshape(NARROW, LANES), side)
    out = product(high[...], low[...], side).reshape(GROUP, ATOMS, LANES) + spare_sums(vectors)[None]
    part_out[...] = total[...] + out


def shifted_kernel(parts, own, aux, out, work):
    coupled = jnp.sum(parts[...], axis=0)
    inside = lane_ids(ATOMS) < COMPS * RHS
    vector = jnp.where(inside, own[...], 0.0)
    mapped = aux[0:ATOMS, :] * vector + coupled
    sums = jnp.zeros((SUMS, LANES), F32)
    row = lax.broadcasted_iota(jnp.int32, (SUMS, LANES), 0)
    for slot, terms in enumerate((vector * vector, vector * mapped, mapped * mapped)):
        sums = jnp.where(row == slot, jnp.sum(terms, axis=0, keepdims=True), sums)
    sums = sum_components(sums)
    work[...] = jnp.zeros_like(work)
    work[SUM_ROW : SUM_ROW + SUMS, :] = pltpu.roll(sums, 4, 0)
    work[SUM_ROW + SUMS : SUM_ROW + 2 * SUMS, :] = pltpu.roll(sums, LANES - ATOMS, 1)
    payload = jnp.where(inside, mapped, work[...].T[0:ATOMS, :])
    for slot in range(HALF):
        out[slot] = payload


def second_kernel(gathered, high, low, part_out, side):
    vectors = gathered[...]
    right_side(vectors.reshape(WIDE, LANES), side)
    sums = jnp.where(lane_ids(ATOMS) < COMPS * RHS, 0.0, jnp.sum(vectors, axis=0))
    part_out[...] = product(high[...], low[...], side).reshape(GROUP, ATOMS, LANES) + sums[None]


def step_kernel(parts, own, shifted, aux, sums_out, state, work):
    total = jnp.sum(parts[...], axis=0)
    vector = own[...]
    mapped = shifted[0]
    twice = aux[0:ATOMS, :] * mapped + total
    work[...] = jnp.zeros_like(work)
    work[0:ATOMS, :] = total
    turned = work[...].T
    lane8 = lane_ids(SUMS)
    head = pltpu.roll(turned[SUM_ROW : SUM_ROW + SUMS, :], 4, 0)
    tail = pltpu.roll(turned[SUM_ROW + SUMS : SUM_ROW + 2 * SUMS, :], ATOMS, 1)
    sums = jnp.where(lane8 < ATOMS, head, jnp.where(lane8 < RHS, tail, 0.0))
    sums = sums + pltpu.roll(sums, RHS, 1) + pltpu.roll(sums, 2 * RHS, 1)
    bb, be, ee = sums[0:1, :], sums[1:2, :], sums[2:3, :]
    shift = aux[ATOMS : ATOMS + 1, :]
    bm = shift * bb + be
    step = bb / bm
    kept = be / bm
    beta = (bb * ee - be * be) / (bm * bm)
    residual = kept * vector - step * mapped
    direction = residual + beta * vector
    image = shift * direction + ((kept + beta) * mapped - step * twice)
    row = lax.broadcasted_iota(jnp.int32, (SUMS, LANES), 0)
    squares = jnp.sum(residual * residual, axis=0, keepdims=True)
    curvature = jnp.sum(direction * image, axis=0, keepdims=True)
    both = sum_components(jnp.where(row == 0, squares, jnp.where(row == 1, curvature, 0.0)))
    lane = lax.broadcasted_iota(jnp.int32, (1, LANES), 1)
    packed = jnp.where(lane < RHS, both[0:1, :], jnp.where(lane < 2 * RHS, both[1:2, :], 0.0))
    sums_out[...] = jnp.broadcast_to(packed, sums_out.shape)
    state[0] = step * vector
    state[1] = direction
    state[2] = residual
    state[3] = image


def pair_kernel(sums, swapped, out):
    out[...] = jnp.broadcast_to((sums[...] + swapped[...])[None], out.shape)


def finish_kernel(gathered, state, dipoles, residual):
    total = jnp.sum(gathered[...], axis=0)
    total = jnp.broadcast_to(jnp.sum(total, axis=0, keepdims=True), (SUMS, LANES))
    first, second, third = component_lanes(SUMS)
    up = pltpu.roll(total, RHS, 1)
    up2 = pltpu.roll(total, 2 * RHS, 1)
    down = pltpu.roll(total, LANES - RHS, 1)
    squares = jnp.where(first, total, jnp.where(second, up, up2))
    curvature = jnp.where(first, down, jnp.where(second, total, jnp.where(third, up, 1.0)))
    step = (squares / curvature)[0:1, :]
    for out, value in (
        (dipoles, state[0] + step * state[1]),
        (residual, state[2] - step * state[3]),
    ):
        for comp in range(COMPS):
            out[comp] = value[:, comp * RHS : (comp + 1) * RHS]


def shape(*dims, dtype=F32):
    return jax.ShapeDtypeStruct(dims, dtype)


def whole(*dims):
    return pl.BlockSpec(dims, lambda i: (0,) * len(dims))


def number(row, z, core):
    return row * GROUP + z * 2 + core


def core_swap(value):
    return lax.ppermute(value, "device", [(here, here ^ 1) for here in range(GROUP * GROUP)])


def exchange(value, groups):
    return lax.all_to_all(value, "device", 0, 0, axis_index_groups=groups)


ROWS = [[number(row, z, core) for row in range(GROUP)] for z in range(HALF) for core in range(2)]
LINES = [[number(row, z, core) for z in range(HALF)] for row in range(GROUP) for core in range(2)]
CHIPS = [[number(row, z, core) for row in range(GROUP) for z in range(HALF)] for core in range(2)]
MIXED = [[number(row, z, 1) for row in (pair, pair + 1) for z in range(HALF)] for pair in range(0, GROUP, 2)] + [
    [number(row, z, 0) for row in range(GROUP)] for z in range(HALF)
]


def local(external_field, jitter, species, alpha_table, block_cell, tile_map):
    me = lax.axis_index("device")
    ids = jnp.stack([me // GROUP, me % GROUP]).astype(jnp.int32)
    field = external_field.transpose(0, 2, 1)
    across_jitter = core_swap(jitter)
    across_field = core_swap(field)
    pack = jnp.concatenate(
        [
            jnp.pad(jitter, ((0, SUMS - COMPS), (0, LANES - ATOMS))),
            jnp.pad(across_jitter, ((0, SUMS - COMPS), (0, LANES - ATOMS))),
            jnp.pad(block_cell.astype(F32).reshape(2, LANES), ((0, 6), (0, 0))),
        ]
    )
    kinds = jnp.concatenate(
        [
            jnp.pad(species.astype(F32)[None], ((0, 3), (0, LANES - ATOMS))),
            jnp.pad(alpha_table.T, ((0, 0), (0, LANES - 12))),
        ]
    )
    vec, vector = pl.pallas_call(
        prepare_kernel,
        out_shape=(shape(GROUP, 2 * ATOMS, LANES), shape(ATOMS, LANES)),
        in_specs=[SMEM, VMEM, VMEM, VMEM],
        out_specs=(VMEM, VMEM),
        scratch_shapes=[SQUARE, pltpu.VMEM((ATOMS, LANES), F32)],
        compiler_params=PARAMS,
        name="prepare",
    )(ids, pack, field, across_field)
    aux, mask = pl.pallas_call(
        side_kernel,
        out_shape=(shape(ATOMS + SUMS, LANES), shape(GROUP, WIDE)),
        in_specs=[SMEM, VMEM, VMEM],
        out_specs=(VMEM, VMEM),
        scratch_shapes=[SQUARE],
        compiler_params=PARAMS,
        name="side",
    )(ids, kinds, tile_map)
    mine, aux, mask = lax.optimization_barrier((exchange(vec, MIXED), aux, mask))
    half = shape(HALF, ATOMS, LANES)
    own, other, column = pl.pallas_call(
        pick_kernel,
        out_shape=(half, half, shape(COMPS, WIDE, LANES)),
        in_specs=[SMEM, VMEM, VMEM],
        out_specs=(VMEM, VMEM, VMEM),
        compiler_params=PARAMS,
        name="pick",
    )(ids, mine, core_swap(mine))
    side = pltpu.VMEM((PAIRS * NARROW, 2 * LANES), BF16)
    tile = shape(WIDE, PAIRS * NARROW, dtype=BF16)
    total, high0, low0 = pl.pallas_call(
        first_own_kernel,
        out_shape=(shape(WIDE, LANES), tile, tile),
        in_specs=[VMEM] * 3,
        out_specs=(VMEM, VMEM, VMEM),
        scratch_shapes=[side],
        compiler_params=PARAMS,
        name="first_own",
    )(mask, column, own)
    part, high1, low1 = pl.pallas_call(
        first_other_kernel,
        out_shape=(shape(GROUP, ATOMS, LANES), tile, tile),
        in_specs=[VMEM] * 4,
        out_specs=(VMEM, VMEM, VMEM),
        scratch_shapes=[side],
        compiler_params=PARAMS,
        name="first_other",
    )(mask, column, other, total)
    parts = exchange(part, ROWS)
    blocks = whole(GROUP, ATOMS, LANES)
    block = whole(1, ATOMS, LANES)
    shifted = pl.pallas_call(
        shifted_kernel,
        grid=(1,),
        out_shape=shape(HALF, ATOMS, LANES),
        in_specs=[blocks, whole(ATOMS, LANES), whole(ATOMS + SUMS, LANES)],
        out_specs=whole(HALF, ATOMS, LANES),
        scratch_shapes=[SQUARE],
        compiler_params=PARAMS,
        name="shifted",
    )(parts, vector, aux)
    own2 = exchange(shifted, LINES)
    other2 = core_swap(own2)
    total2 = pl.pallas_call(
        second_own_kernel,
        out_shape=shape(GROUP, ATOMS, LANES),
        in_specs=[VMEM] * 3,
        out_specs=VMEM,
        scratch_shapes=[side],
        compiler_params=PARAMS,
        name="second_own",
    )(own2, high0, low0)
    part2 = pl.pallas_call(
        second_other_kernel,
        out_shape=shape(GROUP, ATOMS, LANES),
        in_specs=[VMEM] * 4,
        out_specs=VMEM,
        scratch_shapes=[side],
        compiler_params=PARAMS,
        name="second_other",
    )(other2, high1, low1, total2)
    parts2 = exchange(part2, ROWS)
    sums, state = pl.pallas_call(
        step_kernel,
        grid=(1,),
        out_shape=(shape(SUMS, LANES), shape(4, ATOMS, LANES)),
        in_specs=[blocks, whole(ATOMS, LANES), block, whole(ATOMS + SUMS, LANES)],
        out_specs=(whole(SUMS, LANES), whole(4, ATOMS, LANES)),
        scratch_shapes=[SQUARE],
        compiler_params=PARAMS,
        name="step",
    )(parts2, vector, shifted, aux)
    pair = pl.pallas_call(
        pair_kernel,
        out_shape=shape(GROUP, SUMS, LANES),
        in_specs=[VMEM, VMEM],
        out_specs=VMEM,
        compiler_params=PARAMS,
        name="pair",
    )(sums, core_swap(sums))
    pair = pair.reshape(GROUP * HALF, 1, LANES)
    all_sums = exchange(pair, CHIPS).reshape(GROUP, SUMS, LANES)
    dipoles, residual = pl.pallas_call(
        finish_kernel,
        out_shape=(shape(COMPS, ATOMS, RHS), shape(COMPS, ATOMS, RHS)),
        in_specs=[VMEM, VMEM],
        out_specs=(VMEM, VMEM),
        compiler_params=PARAMS,
        name="finish",
    )(all_sums, state)
    return dipoles.transpose(0, 2, 1), residual.transpose(0, 2, 1)


def solution(mesh):
    flat = Mesh(mesh.devices.reshape(GROUP * GROUP), ("device",))
    every = "device"
    return jax.shard_map(
        local,
        mesh=flat,
        in_specs=(P(None, None, every), P(None, every), P(every), P(), P(), P()),
        out_specs=(P(None, None, every), P(None, None, every)),
        check_vma=False,
    )
```

```python
import jax
import jax.numpy as jnp
from jax import lax
from jax.experimental import pallas as pl
from jax.experimental.pallas import tpu as pltpu
from jax.sharding import Mesh, PartitionSpec as P

COMPS = 3
RHS = 36
ATOMS = 32
GROUP = 16
HALF = 8
LANES = 128
SUMS = 8
SITE = 120
SUM_ROW = 104
CELL_ROW = 16
WIDE = GROUP * ATOMS
NARROW = HALF * ATOMS
CHUNK = 256
PAIRS = 5
SPACING = 2.0
F32 = jnp.float32
BF16 = jnp.bfloat16

VMEM = pl.BlockSpec(memory_space=pltpu.VMEM)
SMEM = pl.BlockSpec(memory_space=pltpu.SMEM)
SQUARE = pltpu.VMEM((LANES, LANES), F32)
PARAMS = pltpu.CompilerParams(vmem_limit_bytes=16 * 1024 * 1024)


def lane_ids(rows):
    return lax.broadcasted_iota(jnp.int32, (rows, LANES), 1)


def component_lanes(rows):
    lanes = lane_ids(rows)
    first = lanes < RHS
    second = (lanes >= RHS) & (lanes < 2 * RHS)
    third = (lanes >= 2 * RHS) & (lanes < COMPS * RHS)
    return first, second, third


def sum_components(value):
    first, second, third = component_lanes(SUMS)
    up = pltpu.roll(value, RHS, 1)
    up2 = pltpu.roll(value, 2 * RHS, 1)
    down = pltpu.roll(value, LANES - RHS, 1)
    down2 = pltpu.roll(value, LANES - 2 * RHS, 1)
    of_first = value + down + down2
    of_second = up + value + down
    of_third = up2 + up + value
    return jnp.where(first, of_first, jnp.where(second, of_second, jnp.where(third, of_third, 1.0)))


def block_sites(block, pack, jitter_row):
    index = lax.broadcasted_iota(jnp.int32, (SUMS, LANES), 0) * LANES + lane_ids(SUMS)
    found = jnp.where(index == block, pack[CELL_ROW : CELL_ROW + SUMS, :], 0.0)
    cell = jnp.sum(jnp.sum(found, axis=0, keepdims=True), axis=1, keepdims=True).astype(jnp.int32)
    comp = lax.broadcasted_iota(jnp.int32, (SUMS, LANES), 0)
    return lattice(comp, lane_ids(SUMS), cell) + pack[jitter_row : jitter_row + SUMS, :]


def prepare_kernel(ids, pack, field, partner, vec_out, own_out, work, wide):
    work[...] = jnp.zeros_like(work)
    block = ids[0] * GROUP + ids[1]
    core = ids[1] % 2
    comp = lax.broadcasted_iota(jnp.int32, (SUMS, LANES), 0)
    for flip, vectors in ((0, field), (1, partner)):
        near = block_sites(block ^ flip, pack, flip * SUMS)
        beside = block_sites(block ^ flip ^ GROUP, pack, (3 + flip) * SUMS)
        work[SITE : SITE + SUMS, :] = jnp.where(comp < 4, near, pltpu.roll(beside, 4, 0))
        wide[...] = work[...].T[0:ATOMS, :]
        for part in range(COMPS):
            wide[:, part * RHS : (part + 1) * RHS] = vectors[part]
        turned = wide[...]
        if flip == 0:
            own_out[...] = turned
        rows = pl.ds(pl.multiple_of((core ^ flip) * ATOMS, ATOMS), ATOMS)
        for slot in range(HALF):
            vec_out[slot, rows, :] = turned


def pick_kernel(ids, mine, theirs, own, other, column):
    core = ids[1] % 2
    side = ids[0] % 2
    here = pl.ds(pl.multiple_of(core * ATOMS, ATOMS), ATOMS)
    there = pl.ds(pl.multiple_of((1 - core) * ATOMS, ATOMS), ATOMS)

    def take(along_z, along_row):
        own[...] = along_z[:, here, :]
        other[...] = along_z[:, there, :]
        for slot in range(HALF):
            rows = along_row[slot, here, :]
            for flip in range(2):
                place = pl.ds(pl.multiple_of((2 * slot + (side ^ flip)) * ATOMS, ATOMS), ATOMS)
                for comp in range(COMPS):
                    lane = SITE + 4 * flip + comp
                    column[comp, place, :] = jnp.broadcast_to(rows[:, lane : lane + 1], (ATOMS, LANES))

    @pl.when(core == 0)
    def _():
        take(theirs, mine)

    @pl.when(core == 1)
    def _():
        take(mine, theirs)


def lattice(comp, atom, cell):
    inner = jnp.where(comp == 0, atom >> 3, jnp.where(comp == 1, (atom >> 1) & 3, atom & 1))
    corner = jnp.where(comp == 0, (cell >> 5) * 4, jnp.where(comp == 1, ((cell >> 2) & 7) * 4, (cell & 3) * 2))
    return (corner + inner).astype(F32) * SPACING


def side_kernel(ids, species, tile_map, aux_out, mask_out, work):
    alpha = species[4:SUMS, :]
    lane = lax.broadcasted_iota(jnp.int32, (4, LANES), 1)
    rhs_lane = jnp.where(lane >= 2 * RHS, lane - 2 * RHS, jnp.where(lane >= RHS, lane - RHS, lane))
    table = jnp.ones((4, LANES), F32)
    for freq in range(12):
        table = jnp.where(
            (rhs_lane >= 3 * freq) & (rhs_lane < 3 * freq + 3),
            jnp.broadcast_to(alpha[:, freq : freq + 1], (4, LANES)),
            table,
        )
    inverse = 1.0 / table
    shift = 0.25 * ((inverse[0:1] + inverse[1:2]) + (inverse[2:3] + inverse[3:4]))
    work[0:SUMS, :] = species[...]
    kinds = jnp.broadcast_to(work[...].T[0:ATOMS, 0:1], (ATOMS, LANES))
    diag = jnp.zeros((ATOMS, LANES), F32)
    for kind in range(4):
        diag = jnp.where(kinds == float(kind), inverse[kind : kind + 1] - shift, diag)
    aux_out[0:ATOMS, :] = diag
    aux_out[ATOMS : ATOMS + SUMS, :] = jnp.broadcast_to(shift, (SUMS, LANES))

    blocks = GROUP * GROUP
    active = jnp.where(tile_map[...] != 0, 1.0, 0.0).astype(BF16)
    place = lax.broadcasted_iota(jnp.int32, (GROUP, blocks), 1)
    wanted = lax.broadcasted_iota(jnp.int32, (GROUP, blocks), 0) * GROUP + ids[1]
    pick = jnp.where(place == wanted, 1.0, 0.0).astype(BF16)
    lines = jnp.dot(pick, active, preferred_element_type=F32).astype(BF16)
    slot = lax.broadcasted_iota(jnp.int32, (blocks, WIDE), 1) // ATOMS
    wanted = ids[0] * GROUP + (slot % HALF) * 2 + ((ids[1] % 2) ^ (slot // HALF))
    place = lax.broadcasted_iota(jnp.int32, (blocks, WIDE), 0)
    spread = jnp.where(place == wanted, 1.0, 0.0).astype(BF16)
    mask_out[...] = 0.5 * jnp.dot(lines, spread, preferred_element_type=F32)


def right_side(vectors, side):
    first, second, third = component_lanes(NARROW)
    zero = jnp.zeros_like(vectors)
    up = pltpu.roll(vectors, RHS, 1)
    up2 = pltpu.roll(vectors, 2 * RHS, 1)
    down = pltpu.roll(vectors, LANES - RHS, 1)
    down2 = pltpu.roll(vectors, LANES - 2 * RHS, 1)
    parts = (
        jnp.where(first, vectors, jnp.where(third, -vectors, zero)),
        jnp.where(second, vectors, jnp.where(third, -vectors, zero)),
        jnp.where(first, down, jnp.where(second, up, zero)),
        jnp.where(first, down2, jnp.where(third, up2, zero)),
        jnp.where(second, down, jnp.where(third, up, zero)),
    )
    for slot, part in enumerate(parts):
        high = part.astype(BF16)
        low = (part - high.astype(F32)).astype(BF16)
        side[slot * NARROW : (slot + 1) * NARROW, 0:LANES] = high
        side[slot * NARROW : (slot + 1) * NARROW, LANES : 2 * LANES] = low


def product(high, low, side):
    both = jnp.dot(high, side[...], preferred_element_type=F32)
    rest = jnp.dot(low, side[:, 0:LANES], preferred_element_type=F32)
    return both[:, 0:LANES] + (both[:, LANES:] + rest)


def build_and_apply(mask, vectors, column, high, low, side, first_lane):
    across = vectors.T[SITE : SITE + SUMS, :]
    across_x, across_y, across_z = across[0:1, :], across[1:2, :], across[2:3, :]

    def rows16(step):
        rows = slice(step * 16, (step + 1) * 16)
        here_x, here_y, here_z = column[0, rows, :], column[1, rows, :], column[2, rows, :]
        keep = mask[step // 2 : step // 2 + 1, :]
        for tile in range(NARROW // LANES):
            lanes = slice(tile * LANES, (tile + 1) * LANES)
            dx = here_x - across_x[:, lanes]
            dy = here_y - across_y[:, lanes]
            dz = here_z - across_z[:, lanes]
            xx = dx * dx
            yy = dy * dy
            distance2 = xx + yy + dz * dz
            square = jnp.maximum(distance2, 1.0)
            inverse = lax.rsqrt(square)
            damping = 1.0 + jnp.tanh(1.25 * (square * inverse) - 3.0)
            inverse2 = inverse * inverse
            kept = keep[:, first_lane + tile * LANES : first_lane + (tile + 1) * LANES]
            weight = damping * (inverse2 * inverse2 * inverse) * kept
            radial = weight * distance2
            minus3 = -3.0 * weight
            along_x = minus3 * dx
            along_y = minus3 * dy
            entries = (
                radial + minus3 * xx,
                radial + minus3 * yy,
                along_x * dy,
                along_x * dz,
                along_y * dz,
            )
            for slot, entry in enumerate(entries):
                top = entry.astype(BF16)
                at = slice(slot * NARROW + tile * LANES, slot * NARROW + (tile + 1) * LANES)
                high[rows, at] = top
                low[rows, at] = (entry - top.astype(F32)).astype(BF16)

    outs = []
    for chunk in range(0, WIDE, CHUNK):
        for step in range(chunk // 16, (chunk + CHUNK) // 16):
            rows16(step)
        rows = slice(chunk, chunk + CHUNK)
        outs.append(product(high[rows, :], low[rows, :], side))
    return jnp.concatenate(outs, axis=0)


def first_own_kernel(mask, column, gathered, total, high, low, side):
    vectors = gathered[...].reshape(NARROW, LANES)
    right_side(vectors, side)
    total[...] = build_and_apply(mask, vectors, column, high, low, side, 0)


def first_other_kernel(mask, column, gathered, total, part_out, high, low, side):
    vectors = gathered[...].reshape(NARROW, LANES)
    right_side(vectors, side)
    out = build_and_apply(mask, vectors, column, high, low, side, NARROW)
    part_out[...] = (total[...] + out).reshape(GROUP, ATOMS, LANES)


def spare_sums(vectors):
    return jnp.where(lane_ids(ATOMS) < COMPS * RHS, 0.0, jnp.sum(vectors, axis=0))


def second_own_kernel(gathered, high, low, total, side):
    vectors = gathered[...]
    right_side(vectors.reshape(NARROW, LANES), side)
    out = product(high[...], low[...], side).reshape(GROUP, ATOMS, LANES) + spare_sums(vectors)[None]
    total[...] = out


def second_other_kernel(gathered, high, low, total, part_out, side):
    vectors = gathered[...]
    right_side(vectors.reshape(NARROW, LANES), side)
    out = product(high[...], low[...], side).reshape(GROUP, ATOMS, LANES) + spare_sums(vectors)[None]
    part_out[...] = total[...] + out


def shifted_kernel(parts, own, aux, out, work):
    coupled = jnp.sum(parts[...], axis=0)
    inside = lane_ids(ATOMS) < COMPS * RHS
    vector = jnp.where(inside, own[...], 0.0)
    mapped = aux[0:ATOMS, :] * vector + coupled
    sums = jnp.zeros((SUMS, LANES), F32)
    row = lax.broadcasted_iota(jnp.int32, (SUMS, LANES), 0)
    for slot, terms in enumerate((vector * vector, vector * mapped, mapped * mapped)):
        sums = jnp.where(row == slot, jnp.sum(terms, axis=0, keepdims=True), sums)
    sums = sum_components(sums)
    work[...] = jnp.zeros_like(work)
    work[SUM_ROW : SUM_ROW + SUMS, :] = pltpu.roll(sums, 4, 0)
    work[SUM_ROW + SUMS : SUM_ROW + 2 * SUMS, :] = pltpu.roll(sums, LANES - ATOMS, 1)
    payload = jnp.where(inside, mapped, work[...].T[0:ATOMS, :])
    for slot in range(HALF):
        out[slot] = payload


def second_kernel(gathered, high, low, part_out, side):
    vectors = gathered[...]
    right_side(vectors.reshape(WIDE, LANES), side)
    sums = jnp.where(lane_ids(ATOMS) < COMPS * RHS, 0.0, jnp.sum(vectors, axis=0))
    part_out[...] = product(high[...], low[...], side).reshape(GROUP, ATOMS, LANES) + sums[None]


def step_kernel(parts, own, shifted, aux, sums_out, state, work):
    total = jnp.sum(parts[...], axis=0)
    vector = own[...]
    mapped = shifted[0]
    twice = aux[0:ATOMS, :] * mapped + total
    work[...] = jnp.zeros_like(work)
    work[0:ATOMS, :] = total
    turned = work[...].T
    lane8 = lane_ids(SUMS)
    head = pltpu.roll(turned[SUM_ROW : SUM_ROW + SUMS, :], 4, 0)
    tail = pltpu.roll(turned[SUM_ROW + SUMS : SUM_ROW + 2 * SUMS, :], ATOMS, 1)
    sums = jnp.where(lane8 < ATOMS, head, jnp.where(lane8 < RHS, tail, 0.0))
    sums = sums + pltpu.roll(sums, RHS, 1) + pltpu.roll(sums, 2 * RHS, 1)
    bb, be, ee = sums[0:1, :], sums[1:2, :], sums[2:3, :]
    shift = aux[ATOMS : ATOMS + 1, :]
    bm = shift * bb + be
    step = bb / bm
    kept = be / bm
    beta = (bb * ee - be * be) / (bm * bm)
    residual = kept * vector - step * mapped
    direction = residual + beta * vector
    image = shift * direction + ((kept + beta) * mapped - step * twice)
    row = lax.broadcasted_iota(jnp.int32, (SUMS, LANES), 0)
    squares = jnp.sum(residual * residual, axis=0, keepdims=True)
    curvature = jnp.sum(direction * image, axis=0, keepdims=True)
    both = sum_components(jnp.where(row == 0, squares, jnp.where(row == 1, curvature, 0.0)))
    lane = lax.broadcasted_iota(jnp.int32, (1, LANES), 1)
    packed = jnp.where(lane < RHS, both[0:1, :], jnp.where(lane < 2 * RHS, both[1:2, :], 0.0))
    sums_out[...] = jnp.broadcast_to(packed, sums_out.shape)
    state[0] = step * vector
    state[1] = direction
    state[2] = residual
    state[3] = image


def pair_kernel(sums, swapped, out):
    out[...] = jnp.broadcast_to((sums[...] + swapped[...])[None], out.shape)


def finish_kernel(gathered, state, dipoles, residual):
    total = jnp.sum(gathered[...], axis=0)
    total = jnp.broadcast_to(jnp.sum(total, axis=0, keepdims=True), (SUMS, LANES))
    first, second, third = component_lanes(SUMS)
    up = pltpu.roll(total, RHS, 1)
    up2 = pltpu.roll(total, 2 * RHS, 1)
    down = pltpu.roll(total, LANES - RHS, 1)
    squares = jnp.where(first, total, jnp.where(second, up, up2))
    curvature = jnp.where(first, down, jnp.where(second, total, jnp.where(third, up, 1.0)))
    step = (squares / curvature)[0:1, :]
    for out, value in (
        (dipoles, state[0] + step * state[1]),
        (residual, state[2] - step * state[3]),
    ):
        for comp in range(COMPS):
            out[comp] = value[:, comp * RHS : (comp + 1) * RHS]


def shape(*dims, dtype=F32):
    return jax.ShapeDtypeStruct(dims, dtype)


def whole(*dims):
    return pl.BlockSpec(dims, lambda i: (0,) * len(dims))


def number(row, z, core):
    return row * GROUP + z * 2 + core


def trade(value, bits):
    return lax.ppermute(value, "device", [(here, here ^ bits) for here in range(GROUP * GROUP)])


def core_swap(value):
    return trade(value, 1)


def exchange(value, groups):
    return lax.all_to_all(value, "device", 0, 0, axis_index_groups=groups)


ROWS = [[number(row, z, core) for row in range(GROUP)] for z in range(HALF) for core in range(2)]
LINES = [[number(row, z, core) for z in range(HALF)] for row in range(GROUP) for core in range(2)]
CHIPS = [[number(row, z, core) for row in range(GROUP) for z in range(HALF)] for core in range(2)]
MIXED = [[number(row, z, 1) for z in range(HALF)] for row in range(GROUP)] + [
    [number(row, z, 0) for row in range(first, GROUP, 2)] for first in range(2) for z in range(HALF)
]


def local(external_field, jitter, species, alpha_table, block_cell, tile_map):
    me = lax.axis_index("device")
    ids = jnp.stack([me // GROUP, me % GROUP]).astype(jnp.int32)
    field = external_field.transpose(0, 2, 1)
    across_field = core_swap(field)
    shifts = [jitter] + [trade(jitter, bits) for bits in (1, GROUP, GROUP + 1)]
    shifts = [jnp.pad(shift, ((0, SUMS - COMPS), (0, LANES - ATOMS))) for shift in shifts]
    cells = jnp.pad(block_cell.astype(F32).reshape(2, LANES), ((0, 6), (0, 0)))
    pack = jnp.concatenate(shifts[:2] + [cells] + shifts[2:])
    kinds = jnp.concatenate(
        [
            jnp.pad(species.astype(F32)[None], ((0, 3), (0, LANES - ATOMS))),
            jnp.pad(alpha_table.T, ((0, 0), (0, LANES - 12))),
        ]
    )
    vec, vector = pl.pallas_call(
        prepare_kernel,
        out_shape=(shape(HALF, 2 * ATOMS, LANES), shape(ATOMS, LANES)),
        in_specs=[SMEM, VMEM, VMEM, VMEM],
        out_specs=(VMEM, VMEM),
        scratch_shapes=[SQUARE, pltpu.VMEM((ATOMS, LANES), F32)],
        compiler_params=PARAMS,
        name="prepare",
    )(ids, pack, field, across_field)
    aux, mask = pl.pallas_call(
        side_kernel,
        out_shape=(shape(ATOMS + SUMS, LANES), shape(GROUP, WIDE)),
        in_specs=[SMEM, VMEM, VMEM],
        out_specs=(VMEM, VMEM),
        scratch_shapes=[SQUARE],
        compiler_params=PARAMS,
        name="side",
    )(ids, kinds, tile_map)
    mine, aux, mask = lax.optimization_barrier((exchange(vec, MIXED), aux, mask))
    half = shape(HALF, ATOMS, LANES)
    own, other, column = pl.pallas_call(
        pick_kernel,
        out_shape=(half, half, shape(COMPS, WIDE, LANES)),
        in_specs=[SMEM, VMEM, VMEM],
        out_specs=(VMEM, VMEM, VMEM),
        compiler_params=PARAMS,
        name="pick",
    )(ids, mine, core_swap(mine))
    side = pltpu.VMEM((PAIRS * NARROW, 2 * LANES), BF16)
    tile = shape(WIDE, PAIRS * NARROW, dtype=BF16)
    total, high0, low0 = pl.pallas_call(
        first_own_kernel,
        out_shape=(shape(WIDE, LANES), tile, tile),
        in_specs=[VMEM] * 3,
        out_specs=(VMEM, VMEM, VMEM),
        scratch_shapes=[side],
        compiler_params=PARAMS,
        name="first_own",
    )(mask, column, own)
    part, high1, low1 = pl.pallas_call(
        first_other_kernel,
        out_shape=(shape(GROUP, ATOMS, LANES), tile, tile),
        in_specs=[VMEM] * 4,
        out_specs=(VMEM, VMEM, VMEM),
        scratch_shapes=[side],
        compiler_params=PARAMS,
        name="first_other",
    )(mask, column, other, total)
    parts = exchange(part, ROWS)
    blocks = whole(GROUP, ATOMS, LANES)
    block = whole(1, ATOMS, LANES)
    shifted = pl.pallas_call(
        shifted_kernel,
        grid=(1,),
        out_shape=shape(HALF, ATOMS, LANES),
        in_specs=[blocks, whole(ATOMS, LANES), whole(ATOMS + SUMS, LANES)],
        out_specs=whole(HALF, ATOMS, LANES),
        scratch_shapes=[SQUARE],
        compiler_params=PARAMS,
        name="shifted",
    )(parts, vector, aux)
    own2 = exchange(shifted, LINES)
    other2 = core_swap(own2)
    total2 = pl.pallas_call(
        second_own_kernel,
        out_shape=shape(GROUP, ATOMS, LANES),
        in_specs=[VMEM] * 3,
        out_specs=VMEM,
        scratch_shapes=[side],
        compiler_params=PARAMS,
        name="second_own",
    )(own2, high0, low0)
    part2 = pl.pallas_call(
        second_other_kernel,
        out_shape=shape(GROUP, ATOMS, LANES),
        in_specs=[VMEM] * 4,
        out_specs=VMEM,
        scratch_shapes=[side],
        compiler_params=PARAMS,
        name="second_other",
    )(other2, high1, low1, total2)
    parts2 = exchange(part2, ROWS)
    sums, state = pl.pallas_call(
        step_kernel,
        grid=(1,),
        out_shape=(shape(SUMS, LANES), shape(4, ATOMS, LANES)),
        in_specs=[blocks, whole(ATOMS, LANES), block, whole(ATOMS + SUMS, LANES)],
        out_specs=(whole(SUMS, LANES), whole(4, ATOMS, LANES)),
        scratch_shapes=[SQUARE],
        compiler_params=PARAMS,
        name="step",
    )(parts2, vector, shifted, aux)
    pair = pl.pallas_call(
        pair_kernel,
        out_shape=shape(GROUP, SUMS, LANES),
        in_specs=[VMEM, VMEM],
        out_specs=VMEM,
        compiler_params=PARAMS,
        name="pair",
    )(sums, core_swap(sums))
    pair = pair.reshape(GROUP * HALF, 1, LANES)
    all_sums = exchange(pair, CHIPS).reshape(GROUP, SUMS, LANES)
    dipoles, residual = pl.pallas_call(
        finish_kernel,
        out_shape=(shape(COMPS, ATOMS, RHS), shape(COMPS, ATOMS, RHS)),
        in_specs=[VMEM, VMEM],
        out_specs=(VMEM, VMEM),
        compiler_params=PARAMS,
        name="finish",
    )(all_sums, state)
    return dipoles.transpose(0, 2, 1), residual.transpose(0, 2, 1)


def solution(mesh):
    flat = Mesh(mesh.devices.reshape(GROUP * GROUP), ("device",))
    every = "device"
    return jax.shard_map(
        local,
        mesh=flat,
        in_specs=(P(None, None, every), P(None, every), P(every), P(), P(), P()),
        out_specs=(P(None, None, every), P(None, None, every)),
        check_vma=False,
    )
```

```python
import jax
import jax.numpy as jnp
from jax import lax
from jax.experimental import pallas as pl
from jax.experimental.pallas import tpu as pltpu
from jax.sharding import Mesh, PartitionSpec as P

COMPS = 3
RHS = 36
ATOMS = 32
GROUP = 16
HALF = 8
LANES = 128
SUMS = 8
SITE = 120
SUM_ROW = 104
WIDE = GROUP * ATOMS
NARROW = HALF * ATOMS
CHUNK = 256
PAIRS = 5
SPACING = 2.0
F32 = jnp.float32
BF16 = jnp.bfloat16

VMEM = pl.BlockSpec(memory_space=pltpu.VMEM)
SMEM = pl.BlockSpec(memory_space=pltpu.SMEM)
SQUARE = pltpu.VMEM((LANES, LANES), F32)
PARAMS = pltpu.CompilerParams(vmem_limit_bytes=16 * 1024 * 1024)


def lane_ids(rows):
    return lax.broadcasted_iota(jnp.int32, (rows, LANES), 1)


def component_lanes(rows):
    lanes = lane_ids(rows)
    first = lanes < RHS
    second = (lanes >= RHS) & (lanes < 2 * RHS)
    third = (lanes >= 2 * RHS) & (lanes < COMPS * RHS)
    return first, second, third


def sum_components(value):
    first, second, third = component_lanes(SUMS)
    up = pltpu.roll(value, RHS, 1)
    up2 = pltpu.roll(value, 2 * RHS, 1)
    down = pltpu.roll(value, LANES - RHS, 1)
    down2 = pltpu.roll(value, LANES - 2 * RHS, 1)
    of_first = value + down + down2
    of_second = up + value + down
    of_third = up2 + up + value
    return jnp.where(first, of_first, jnp.where(second, of_second, jnp.where(third, of_third, 1.0)))


def prepare_kernel(ids, jitter, across, beside, corner, field, partner, vec_out, own_out, work, wide):
    work[...] = jnp.zeros_like(work)
    core = ids[1] % 2
    for flip, near, far, vectors in ((0, jitter, beside, field), (1, across, corner, partner)):
        work[SITE : SITE + COMPS, 0:ATOMS] = near[:, 0:ATOMS]
        work[SITE + 4 : SITE + 4 + COMPS, 0:ATOMS] = far[...]
        wide[...] = work[...].T[0:ATOMS, :]
        for part in range(COMPS):
            wide[:, part * RHS : (part + 1) * RHS] = vectors[part, :, 0:RHS]
        turned = wide[...]
        if flip == 0:
            own_out[...] = turned
        rows = pl.ds(pl.multiple_of((core ^ flip) * ATOMS, ATOMS), ATOMS)
        for slot in range(HALF):
            vec_out[slot, rows, :] = turned


def pick_kernel(ids, points, mine, theirs, own, other, column):
    core = ids[1] % 2
    side = ids[0] % 2
    here = pl.ds(pl.multiple_of(core * ATOMS, ATOMS), ATOMS)
    there = pl.ds(pl.multiple_of((1 - core) * ATOMS, ATOMS), ATOMS)

    def take(along_z, along_row):
        own[...] = along_z[:, here, :]
        other[...] = along_z[:, there, :]
        for slot in range(HALF):
            rows = along_row[slot, here, :]
            for flip in range(2):
                place = pl.ds(pl.multiple_of((2 * slot + (side ^ flip)) * ATOMS, ATOMS), ATOMS)
                for comp in range(COMPS):
                    lane = SITE + 4 * flip + comp
                    column[comp, place, :] = points[comp, place, :] + rows[:, lane : lane + 1]

    @pl.when(core == 0)
    def _():
        take(theirs, mine)

    @pl.when(core == 1)
    def _():
        take(mine, theirs)


def lattice(comp, atom, cell):
    if isinstance(comp, int):
        inner = (atom >> 3, (atom >> 1) & 3, atom & 1)[comp]
        corner = ((cell >> 5) * 4, ((cell >> 2) & 7) * 4, (cell & 3) * 2)[comp]
        return (corner + inner).astype(F32) * SPACING
    inner = jnp.where(comp == 0, atom >> 3, jnp.where(comp == 1, (atom >> 1) & 3, atom & 1))
    corner = jnp.where(comp == 0, (cell >> 5) * 4, jnp.where(comp == 1, ((cell >> 2) & 7) * 4, (cell & 3) * 2))
    return (corner + inner).astype(F32) * SPACING


def side_kernel(ids, species, cells, tile_map, aux_out, mask_out, points, across, work):
    alpha = species[4:SUMS, :]
    lane = lax.broadcasted_iota(jnp.int32, (4, LANES), 1)
    rhs_lane = jnp.where(lane >= 2 * RHS, lane - 2 * RHS, jnp.where(lane >= RHS, lane - RHS, lane))
    table = jnp.ones((4, LANES), F32)
    for freq in range(12):
        table = jnp.where(
            (rhs_lane >= 3 * freq) & (rhs_lane < 3 * freq + 3),
            jnp.broadcast_to(alpha[:, freq : freq + 1], (4, LANES)),
            table,
        )
    inverse = 1.0 / table
    shift = 0.25 * ((inverse[0:1] + inverse[1:2]) + (inverse[2:3] + inverse[3:4]))
    work[0:SUMS, :] = species[...]
    kinds = jnp.broadcast_to(work[...].T[0:ATOMS, 0:1], (ATOMS, LANES))
    diag = jnp.zeros((ATOMS, LANES), F32)
    for kind in range(4):
        diag = jnp.where(kinds == float(kind), inverse[kind : kind + 1] - shift, diag)
    aux_out[0:ATOMS, :] = diag
    aux_out[ATOMS : ATOMS + SUMS, :] = jnp.broadcast_to(shift, (SUMS, LANES))

    blocks = GROUP * GROUP
    active = jnp.where(tile_map[...] != 0, 1.0, 0.0).astype(BF16)
    place = lax.broadcasted_iota(jnp.int32, (GROUP, blocks), 1)
    wanted = lax.broadcasted_iota(jnp.int32, (GROUP, blocks), 0) * GROUP + ids[1]
    pick = jnp.where(place == wanted, 1.0, 0.0).astype(BF16)
    lines = jnp.dot(pick, active, preferred_element_type=F32).astype(BF16)
    slot = lax.broadcasted_iota(jnp.int32, (blocks, WIDE), 1) // ATOMS
    wanted = ids[0] * GROUP + (slot % HALF) * 2 + ((ids[1] % 2) ^ (slot // HALF))
    place = lax.broadcasted_iota(jnp.int32, (blocks, WIDE), 0)
    spread = jnp.where(place == wanted, 1.0, 0.0).astype(BF16)
    mask_out[...] = 0.5 * jnp.dot(lines, spread, preferred_element_type=F32)

    cell = jnp.dot(cells[...].astype(BF16), spread, preferred_element_type=F32)[0:1, :].astype(jnp.int32)
    comp = lax.broadcasted_iota(jnp.int32, (SUMS, WIDE), 0)
    atom = lax.broadcasted_iota(jnp.int32, (SUMS, WIDE), 1) & (ATOMS - 1)
    across[...] = lattice(comp, atom, cell)
    place = lax.broadcasted_iota(jnp.int32, (WIDE, blocks), 1)
    row = lax.broadcasted_iota(jnp.int32, (WIDE, blocks), 0)
    wanted = (row // ATOMS) * GROUP + ids[1]
    cell = jnp.sum(jnp.where(place == wanted, cells[0:1, :], 0.0), axis=1, keepdims=True).astype(jnp.int32)
    atom = lax.broadcasted_iota(jnp.int32, (WIDE, LANES), 0) & (ATOMS - 1)
    for comp in range(COMPS):
        points[comp] = lattice(comp, atom, cell)


def right_side(vectors, side):
    first, second, third = component_lanes(NARROW)
    zero = jnp.zeros_like(vectors)
    up = pltpu.roll(vectors, RHS, 1)
    up2 = pltpu.roll(vectors, 2 * RHS, 1)
    down = pltpu.roll(vectors, LANES - RHS, 1)
    down2 = pltpu.roll(vectors, LANES - 2 * RHS, 1)
    parts = (
        jnp.where(first, vectors, jnp.where(third, -vectors, zero)),
        jnp.where(second, vectors, jnp.where(third, -vectors, zero)),
        jnp.where(first, down, jnp.where(second, up, zero)),
        jnp.where(first, down2, jnp.where(third, up2, zero)),
        jnp.where(second, down, jnp.where(third, up, zero)),
    )
    for slot, part in enumerate(parts):
        high = part.astype(BF16)
        low = (part - high.astype(F32)).astype(BF16)
        side[slot * NARROW : (slot + 1) * NARROW, 0:LANES] = high
        side[slot * NARROW : (slot + 1) * NARROW, LANES : 2 * LANES] = low


def product(high, low, side):
    both = jnp.dot(high, side[...], preferred_element_type=F32)
    rest = jnp.dot(low, side[:, 0:LANES], preferred_element_type=F32)
    return both[:, 0:LANES] + (both[:, LANES:] + rest)


def build_and_apply(mask, vectors, column, points, high, low, side, first_lane):
    across = vectors.T[SITE : SITE + SUMS, :] + points[:, first_lane : first_lane + NARROW]
    across_x, across_y, across_z = across[0:1, :], across[1:2, :], across[2:3, :]

    def rows16(step):
        rows = slice(step * 16, (step + 1) * 16)
        here_x, here_y, here_z = column[0, rows, :], column[1, rows, :], column[2, rows, :]
        keep = mask[step // 2 : step // 2 + 1, :]
        for tile in range(NARROW // LANES):
            lanes = slice(tile * LANES, (tile + 1) * LANES)
            dx = here_x - across_x[:, lanes]
            dy = here_y - across_y[:, lanes]
            dz = here_z - across_z[:, lanes]
            xx = dx * dx
            yy = dy * dy
            distance2 = xx + yy + dz * dz
            square = jnp.maximum(distance2, 1.0)
            inverse = lax.rsqrt(square)
            damping = 1.0 + jnp.tanh(1.25 * (square * inverse) - 3.0)
            inverse2 = inverse * inverse
            kept = keep[:, first_lane + tile * LANES : first_lane + (tile + 1) * LANES]
            weight = damping * (inverse2 * inverse2 * inverse) * kept
            radial = weight * distance2
            minus3 = -3.0 * weight
            along_x = minus3 * dx
            along_y = minus3 * dy
            entries = (
                radial + minus3 * xx,
                radial + minus3 * yy,
                along_x * dy,
                along_x * dz,
                along_y * dz,
            )
            for slot, entry in enumerate(entries):
                top = entry.astype(BF16)
                at = slice(slot * NARROW + tile * LANES, slot * NARROW + (tile + 1) * LANES)
                high[rows, at] = top
                low[rows, at] = (entry - top.astype(F32)).astype(BF16)

    outs = []
    for chunk in range(0, WIDE, CHUNK):
        for step in range(chunk // 16, (chunk + CHUNK) // 16):
            rows16(step)
        rows = slice(chunk, chunk + CHUNK)
        outs.append(product(high[rows, :], low[rows, :], side))
    return jnp.concatenate(outs, axis=0)


def first_own_kernel(mask, column, points, gathered, total, high, low, side):
    vectors = gathered[...].reshape(NARROW, LANES)
    right_side(vectors, side)
    total[...] = build_and_apply(mask, vectors, column, points, high, low, side, 0)


def first_other_kernel(mask, column, points, gathered, total, part_out, high, low, side):
    vectors = gathered[...].reshape(NARROW, LANES)
    right_side(vectors, side)
    out = build_and_apply(mask, vectors, column, points, high, low, side, NARROW)
    part_out[...] = (total[...] + out).reshape(GROUP, ATOMS, LANES)


def spare_sums(vectors):
    return jnp.where(lane_ids(ATOMS) < COMPS * RHS, 0.0, jnp.sum(vectors, axis=0))


def second_own_kernel(gathered, high, low, total, side):
    vectors = gathered[...]
    right_side(vectors.reshape(NARROW, LANES), side)
    out = product(high[...], low[...], side).reshape(GROUP, ATOMS, LANES) + spare_sums(vectors)[None]
    total[...] = out


def second_other_kernel(gathered, high, low, total, part_out, side):
    vectors = gathered[...]
    right_side(vectors.reshape(NARROW, LANES), side)
    out = product(high[...], low[...], side).reshape(GROUP, ATOMS, LANES) + spare_sums(vectors)[None]
    part_out[...] = total[...] + out


def shifted_kernel(parts, own, aux, out, work):
    coupled = jnp.sum(parts[...], axis=0)
    inside = lane_ids(ATOMS) < COMPS * RHS
    vector = jnp.where(inside, own[...], 0.0)
    mapped = aux[0:ATOMS, :] * vector + coupled
    sums = jnp.zeros((SUMS, LANES), F32)
    row = lax.broadcasted_iota(jnp.int32, (SUMS, LANES), 0)
    for slot, terms in enumerate((vector * vector, vector * mapped, mapped * mapped)):
        sums = jnp.where(row == slot, jnp.sum(terms, axis=0, keepdims=True), sums)
    sums = sum_components(sums)
    work[...] = jnp.zeros_like(work)
    work[SUM_ROW : SUM_ROW + SUMS, :] = pltpu.roll(sums, 4, 0)
    work[SUM_ROW + SUMS : SUM_ROW + 2 * SUMS, :] = pltpu.roll(sums, LANES - ATOMS, 1)
    payload = jnp.where(inside, mapped, work[...].T[0:ATOMS, :])
    for slot in range(HALF):
        out[slot] = payload


def second_kernel(gathered, high, low, part_out, side):
    vectors = gathered[...]
    right_side(vectors.reshape(WIDE, LANES), side)
    sums = jnp.where(lane_ids(ATOMS) < COMPS * RHS, 0.0, jnp.sum(vectors, axis=0))
    part_out[...] = product(high[...], low[...], side).reshape(GROUP, ATOMS, LANES) + sums[None]


def step_kernel(parts, own, shifted, aux, sums_out, state, work):
    total = jnp.sum(parts[...], axis=0)
    vector = own[...]
    mapped = shifted[0]
    twice = aux[0:ATOMS, :] * mapped + total
    work[...] = jnp.zeros_like(work)
    work[0:ATOMS, :] = total
    turned = work[...].T
    lane8 = lane_ids(SUMS)
    head = pltpu.roll(turned[SUM_ROW : SUM_ROW + SUMS, :], 4, 0)
    tail = pltpu.roll(turned[SUM_ROW + SUMS : SUM_ROW + 2 * SUMS, :], ATOMS, 1)
    sums = jnp.where(lane8 < ATOMS, head, jnp.where(lane8 < RHS, tail, 0.0))
    sums = sums + pltpu.roll(sums, RHS, 1) + pltpu.roll(sums, 2 * RHS, 1)
    bb, be, ee = sums[0:1, :], sums[1:2, :], sums[2:3, :]
    shift = aux[ATOMS : ATOMS + 1, :]
    bm = shift * bb + be
    step = bb / bm
    kept = be / bm
    beta = (bb * ee - be * be) / (bm * bm)
    residual = kept * vector - step * mapped
    direction = residual + beta * vector
    image = shift * direction + ((kept + beta) * mapped - step * twice)
    row = lax.broadcasted_iota(jnp.int32, (SUMS, LANES), 0)
    squares = jnp.sum(residual * residual, axis=0, keepdims=True)
    curvature = jnp.sum(direction * image, axis=0, keepdims=True)
    both = sum_components(jnp.where(row == 0, squares, jnp.where(row == 1, curvature, 0.0)))
    lane = lax.broadcasted_iota(jnp.int32, (1, LANES), 1)
    packed = jnp.where(lane < RHS, both[0:1, :], jnp.where(lane < 2 * RHS, both[1:2, :], 0.0))
    sums_out[...] = jnp.broadcast_to(packed, sums_out.shape)
    state[0] = step * vector
    state[1] = direction
    state[2] = residual
    state[3] = image


def pair_kernel(sums, swapped, out):
    out[...] = jnp.broadcast_to((sums[...] + swapped[...])[None], out.shape)


def finish_kernel(gathered, state, dipoles, residual):
    total = jnp.sum(gathered[...], axis=0)
    total = jnp.broadcast_to(jnp.sum(total, axis=0, keepdims=True), (SUMS, LANES))
    first, second, third = component_lanes(SUMS)
    up = pltpu.roll(total, RHS, 1)
    up2 = pltpu.roll(total, 2 * RHS, 1)
    down = pltpu.roll(total, LANES - RHS, 1)
    squares = jnp.where(first, total, jnp.where(second, up, up2))
    curvature = jnp.where(first, down, jnp.where(second, total, jnp.where(third, up, 1.0)))
    step = (squares / curvature)[0:1, :]
    for out, value in (
        (dipoles, state[0] + step * state[1]),
        (residual, state[2] - step * state[3]),
    ):
        for comp in range(COMPS):
            out[comp] = value[:, comp * RHS : (comp + 1) * RHS]


def shape(*dims, dtype=F32):
    return jax.ShapeDtypeStruct(dims, dtype)


def whole(*dims):
    return pl.BlockSpec(dims, lambda i: (0,) * len(dims))


def number(row, z, core):
    return row * GROUP + z * 2 + core


def trade(value, bits):
    return lax.ppermute(value, "device", [(here, here ^ bits) for here in range(GROUP * GROUP)])


def core_swap(value):
    return trade(value, 1)


def exchange(value, groups):
    return lax.all_to_all(value, "device", 0, 0, axis_index_groups=groups)


ROWS = [[number(row, z, core) for row in range(GROUP)] for z in range(HALF) for core in range(2)]
LINES = [[number(row, z, core) for z in range(HALF)] for row in range(GROUP) for core in range(2)]
CHIPS = [[number(row, z, core) for row in range(GROUP) for z in range(HALF)] for core in range(2)]
MIXED = [[number(row, z, 1) for z in range(HALF)] for row in range(GROUP)] + [
    [number(row, z, 0) for row in range(first, GROUP, 2)] for first in range(2) for z in range(HALF)
]


def local(external_field, jitter, species, alpha_table, block_cell, tile_map):
    me = lax.axis_index("device")
    ids = jnp.stack([me // GROUP, me % GROUP]).astype(jnp.int32)
    field = external_field.transpose(0, 2, 1)
    across_field = core_swap(field)
    shifts = [jnp.pad(jitter, ((0, 0), (0, LANES - ATOMS)))]
    shifts = shifts + [trade(jitter, bits) for bits in (1, GROUP, GROUP + 1)]
    cells = jnp.pad(block_cell.astype(F32)[None], ((0, SUMS - 1), (0, 0)))
    kinds = jnp.concatenate(
        [
            jnp.pad(species.astype(F32)[None], ((0, 3), (0, LANES - ATOMS))),
            jnp.pad(alpha_table.T, ((0, 0), (0, LANES - 12))),
        ]
    )
    vec, vector = pl.pallas_call(
        prepare_kernel,
        out_shape=(shape(HALF, 2 * ATOMS, LANES), shape(ATOMS, LANES)),
        in_specs=[SMEM] + [VMEM] * 6,
        out_specs=(VMEM, VMEM),
        scratch_shapes=[SQUARE, pltpu.VMEM((ATOMS, LANES), F32)],
        compiler_params=PARAMS,
        name="prepare",
    )(ids, *shifts, jnp.pad(field, ((0, 0), (0, 0), (0, LANES - RHS))), across_field)
    column_shape = shape(COMPS, WIDE, LANES)
    aux, mask, points, across = pl.pallas_call(
        side_kernel,
        out_shape=(shape(ATOMS + SUMS, LANES), shape(GROUP, WIDE), column_shape, shape(SUMS, WIDE)),
        in_specs=[SMEM, VMEM, VMEM, VMEM],
        out_specs=(VMEM, VMEM, VMEM, VMEM),
        scratch_shapes=[SQUARE],
        compiler_params=PARAMS,
        name="side",
    )(ids, kinds, cells, tile_map)
    mine, aux, mask, points, across = lax.optimization_barrier(
        (exchange(vec, MIXED), aux, mask, points, across)
    )
    half = shape(HALF, ATOMS, LANES)
    own, other, column = pl.pallas_call(
        pick_kernel,
        out_shape=(half, half, column_shape),
        in_specs=[SMEM, VMEM, VMEM, VMEM],
        out_specs=(VMEM, VMEM, VMEM),
        compiler_params=PARAMS,
        name="pick",
    )(ids, points, mine, core_swap(mine))
    side = pltpu.VMEM((PAIRS * NARROW, 2 * LANES), BF16)
    tile = shape(WIDE, PAIRS * NARROW, dtype=BF16)
    total, high0, low0 = pl.pallas_call(
        first_own_kernel,
        out_shape=(shape(WIDE, LANES), tile, tile),
        in_specs=[VMEM] * 4,
        out_specs=(VMEM, VMEM, VMEM),
        scratch_shapes=[side],
        compiler_params=PARAMS,
        name="first_own",
    )(mask, column, across, own)
    part, high1, low1 = pl.pallas_call(
        first_other_kernel,
        out_shape=(shape(GROUP, ATOMS, LANES), tile, tile),
        in_specs=[VMEM] * 5,
        out_specs=(VMEM, VMEM, VMEM),
        scratch_shapes=[side],
        compiler_params=PARAMS,
        name="first_other",
    )(mask, column, across, other, total)
    parts = exchange(part, ROWS)
    blocks = whole(GROUP, ATOMS, LANES)
    block = whole(1, ATOMS, LANES)
    shifted = pl.pallas_call(
        shifted_kernel,
        grid=(1,),
        out_shape=shape(HALF, ATOMS, LANES),
        in_specs=[blocks, whole(ATOMS, LANES), whole(ATOMS + SUMS, LANES)],
        out_specs=whole(HALF, ATOMS, LANES),
        scratch_shapes=[SQUARE],
        compiler_params=PARAMS,
        name="shifted",
    )(parts, vector, aux)
    own2 = exchange(shifted, LINES)
    other2 = core_swap(own2)
    total2 = pl.pallas_call(
        second_own_kernel,
        out_shape=shape(GROUP, ATOMS, LANES),
        in_specs=[VMEM] * 3,
        out_specs=VMEM,
        scratch_shapes=[side],
        compiler_params=PARAMS,
        name="second_own",
    )(own2, high0, low0)
    part2 = pl.pallas_call(
        second_other_kernel,
        out_shape=shape(GROUP, ATOMS, LANES),
        in_specs=[VMEM] * 4,
        out_specs=VMEM,
        scratch_shapes=[side],
        compiler_params=PARAMS,
        name="second_other",
    )(other2, high1, low1, total2)
    parts2 = exchange(part2, ROWS)
    sums, state = pl.pallas_call(
        step_kernel,
        grid=(1,),
        out_shape=(shape(SUMS, LANES), shape(4, ATOMS, LANES)),
        in_specs=[blocks, whole(ATOMS, LANES), block, whole(ATOMS + SUMS, LANES)],
        out_specs=(whole(SUMS, LANES), whole(4, ATOMS, LANES)),
        scratch_shapes=[SQUARE],
        compiler_params=PARAMS,
        name="step",
    )(parts2, vector, shifted, aux)
    pair = pl.pallas_call(
        pair_kernel,
        out_shape=shape(GROUP, SUMS, LANES),
        in_specs=[VMEM, VMEM],
        out_specs=VMEM,
        compiler_params=PARAMS,
        name="pair",
    )(sums, core_swap(sums))
    pair = pair.reshape(GROUP * HALF, 1, LANES)
    all_sums = exchange(pair, CHIPS).reshape(GROUP, SUMS, LANES)
    dipoles, residual = pl.pallas_call(
        finish_kernel,
        out_shape=(shape(COMPS, ATOMS, RHS), shape(COMPS, ATOMS, RHS)),
        in_specs=[VMEM, VMEM],
        out_specs=(VMEM, VMEM),
        compiler_params=PARAMS,
        name="finish",
    )(all_sums, state)
    return dipoles.transpose(0, 2, 1), residual.transpose(0, 2, 1)


def solution(mesh):
    flat = Mesh(mesh.devices.reshape(GROUP * GROUP), ("device",))
    every = "device"
    return jax.shard_map(
        local,
        mesh=flat,
        in_specs=(P(None, None, every), P(None, every), P(every), P(), P(), P()),
        out_specs=(P(None, None, every), P(None, None, every)),
        check_vma=False,
    )
```

```python
import jax
import jax.numpy as jnp
from jax import lax
from jax.experimental import pallas as pl
from jax.experimental.pallas import tpu as pltpu
from jax.sharding import Mesh, PartitionSpec as P

COMPS = 3
RHS = 36
ATOMS = 32
GROUP = 16
HALF = 8
LANES = 128
SUMS = 8
SITE = 120
SUM_ROW = 104
WIDE = GROUP * ATOMS
NARROW = HALF * ATOMS
CHUNK = 256
PAIRS = 5
SPACING = 2.0
F32 = jnp.float32
BF16 = jnp.bfloat16

VMEM = pl.BlockSpec(memory_space=pltpu.VMEM)
SMEM = pl.BlockSpec(memory_space=pltpu.SMEM)
SQUARE = pltpu.VMEM((LANES, LANES), F32)
PARAMS = pltpu.CompilerParams(vmem_limit_bytes=16 * 1024 * 1024)


def lane_ids(rows):
    return lax.broadcasted_iota(jnp.int32, (rows, LANES), 1)


def component_lanes(rows):
    lanes = lane_ids(rows)
    first = lanes < RHS
    second = (lanes >= RHS) & (lanes < 2 * RHS)
    third = (lanes >= 2 * RHS) & (lanes < COMPS * RHS)
    return first, second, third


def sum_components(value):
    first, second, third = component_lanes(SUMS)
    up = pltpu.roll(value, RHS, 1)
    up2 = pltpu.roll(value, 2 * RHS, 1)
    down = pltpu.roll(value, LANES - RHS, 1)
    down2 = pltpu.roll(value, LANES - 2 * RHS, 1)
    of_first = value + down + down2
    of_second = up + value + down
    of_third = up2 + up + value
    return jnp.where(first, of_first, jnp.where(second, of_second, jnp.where(third, of_third, 1.0)))


def prepare_kernel(jitter, across, beside, corner, field, partner, vec_out, own_out, work, wide):
    work[...] = jnp.zeros_like(work)
    for flip, near, far, vectors in ((0, jitter, beside, field), (1, across, corner, partner)):
        work[SITE : SITE + COMPS, 0:ATOMS] = near[:, 0:ATOMS]
        work[SITE + 4 : SITE + 4 + COMPS, 0:ATOMS] = far[...]
        wide[...] = work[...].T[0:ATOMS, :]
        for part in range(COMPS):
            wide[:, part * RHS : (part + 1) * RHS] = vectors[part, :, 0:RHS]
        turned = wide[...]
        if flip == 0:
            own_out[...] = turned
        for slot in range(HALF):
            vec_out[slot, flip * ATOMS : (flip + 1) * ATOMS, :] = turned


def pick_kernel(flags, points, mine, theirs, own, other, column):
    odd_core = flags[0:ATOMS, :] > 0.5
    odd_row = flags[ATOMS : 2 * ATOMS, :] > 0.5
    for slot in range(HALF):
        first, second = mine[slot, 0:ATOMS, :], mine[slot, ATOMS : 2 * ATOMS, :]
        third, fourth = theirs[slot, 0:ATOMS, :], theirs[slot, ATOMS : 2 * ATOMS, :]
        own[slot] = jnp.where(odd_core, first, fourth)
        other[slot] = jnp.where(odd_core, second, third)
        rows = jnp.where(odd_core, fourth, first)
        beside = pltpu.roll(rows, LANES - 4, 1)
        for block, sites in (
            (2 * slot, jnp.where(odd_row, beside, rows)),
            (2 * slot + 1, jnp.where(odd_row, rows, beside)),
        ):
            place = slice(block * ATOMS, (block + 1) * ATOMS)
            for comp in range(COMPS):
                column[comp, place, :] = points[comp, place, :] + sites[:, SITE + comp : SITE + comp + 1]


def lattice(comp, atom, cell):
    if isinstance(comp, int):
        inner = (atom >> 3, (atom >> 1) & 3, atom & 1)[comp]
        corner = ((cell >> 5) * 4, ((cell >> 2) & 7) * 4, (cell & 3) * 2)[comp]
        return (corner + inner).astype(F32) * SPACING
    inner = jnp.where(comp == 0, atom >> 3, jnp.where(comp == 1, (atom >> 1) & 3, atom & 1))
    corner = jnp.where(comp == 0, (cell >> 5) * 4, jnp.where(comp == 1, ((cell >> 2) & 7) * 4, (cell & 3) * 2))
    return (corner + inner).astype(F32) * SPACING


def side_kernel(ids, species, cells, tile_map, aux_out, mask_out, points, across, flags, work):
    alpha = species[4:SUMS, :]
    lane = lax.broadcasted_iota(jnp.int32, (4, LANES), 1)
    rhs_lane = jnp.where(lane >= 2 * RHS, lane - 2 * RHS, jnp.where(lane >= RHS, lane - RHS, lane))
    table = jnp.ones((4, LANES), F32)
    for freq in range(12):
        table = jnp.where(
            (rhs_lane >= 3 * freq) & (rhs_lane < 3 * freq + 3),
            jnp.broadcast_to(alpha[:, freq : freq + 1], (4, LANES)),
            table,
        )
    inverse = 1.0 / table
    shift = 0.25 * ((inverse[0:1] + inverse[1:2]) + (inverse[2:3] + inverse[3:4]))
    work[0:SUMS, :] = species[...]
    kinds = jnp.broadcast_to(work[...].T[0:ATOMS, 0:1], (ATOMS, LANES))
    diag = jnp.zeros((ATOMS, LANES), F32)
    for kind in range(4):
        diag = jnp.where(kinds == float(kind), inverse[kind : kind + 1] - shift, diag)
    aux_out[0:ATOMS, :] = diag
    aux_out[ATOMS : ATOMS + SUMS, :] = jnp.broadcast_to(shift, (SUMS, LANES))

    blocks = GROUP * GROUP
    active = jnp.where(tile_map[...] != 0, 1.0, 0.0).astype(BF16)
    place = lax.broadcasted_iota(jnp.int32, (GROUP, blocks), 1)
    wanted = lax.broadcasted_iota(jnp.int32, (GROUP, blocks), 0) * GROUP + ids[1]
    pick = jnp.where(place == wanted, 1.0, 0.0).astype(BF16)
    lines = jnp.dot(pick, active, preferred_element_type=F32).astype(BF16)
    slot = lax.broadcasted_iota(jnp.int32, (blocks, WIDE), 1) // ATOMS
    wanted = ids[0] * GROUP + (slot % HALF) * 2 + ((ids[1] % 2) ^ (slot // HALF))
    place = lax.broadcasted_iota(jnp.int32, (blocks, WIDE), 0)
    spread = jnp.where(place == wanted, 1.0, 0.0).astype(BF16)
    mask_out[...] = 0.5 * jnp.dot(lines, spread, preferred_element_type=F32)

    cell = jnp.dot(cells[...].astype(BF16), spread, preferred_element_type=F32)[0:1, :].astype(jnp.int32)
    comp = lax.broadcasted_iota(jnp.int32, (SUMS, WIDE), 0)
    atom = lax.broadcasted_iota(jnp.int32, (SUMS, WIDE), 1) & (ATOMS - 1)
    across[...] = lattice(comp, atom, cell)
    place = lax.broadcasted_iota(jnp.int32, (WIDE, blocks), 1)
    row = lax.broadcasted_iota(jnp.int32, (WIDE, blocks), 0)
    wanted = (row // ATOMS) * GROUP + ids[1]
    cell = jnp.sum(jnp.where(place == wanted, cells[0:1, :], 0.0), axis=1, keepdims=True).astype(jnp.int32)
    atom = lax.broadcasted_iota(jnp.int32, (WIDE, LANES), 0) & (ATOMS - 1)
    for comp in range(COMPS):
        points[comp] = lattice(comp, atom, cell)
    flags[0:ATOMS, :] = jnp.full((ATOMS, LANES), ids[1] % 2, jnp.int32).astype(F32)
    flags[ATOMS : 2 * ATOMS, :] = jnp.full((ATOMS, LANES), ids[0] % 2, jnp.int32).astype(F32)


def right_side(vectors, side):
    first, second, third = component_lanes(NARROW)
    zero = jnp.zeros_like(vectors)
    up = pltpu.roll(vectors, RHS, 1)
    up2 = pltpu.roll(vectors, 2 * RHS, 1)
    down = pltpu.roll(vectors, LANES - RHS, 1)
    down2 = pltpu.roll(vectors, LANES - 2 * RHS, 1)
    parts = (
        jnp.where(first, vectors, jnp.where(third, -vectors, zero)),
        jnp.where(second, vectors, jnp.where(third, -vectors, zero)),
        jnp.where(first, down, jnp.where(second, up, zero)),
        jnp.where(first, down2, jnp.where(third, up2, zero)),
        jnp.where(second, down, jnp.where(third, up, zero)),
    )
    for slot, part in enumerate(parts):
        high = part.astype(BF16)
        low = (part - high.astype(F32)).astype(BF16)
        side[slot * NARROW : (slot + 1) * NARROW, 0:LANES] = high
        side[slot * NARROW : (slot + 1) * NARROW, LANES : 2 * LANES] = low


def product(high, low, side):
    both = jnp.dot(high, side[...], preferred_element_type=F32)
    rest = jnp.dot(low, side[:, 0:LANES], preferred_element_type=F32)
    return both[:, 0:LANES] + (both[:, LANES:] + rest)


def build_and_apply(mask, vectors, column, points, high, low, side, first_lane):
    across = vectors.T[SITE : SITE + SUMS, :] + points[:, first_lane : first_lane + NARROW]
    across_x, across_y, across_z = across[0:1, :], across[1:2, :], across[2:3, :]

    def rows16(step):
        rows = slice(step * 16, (step + 1) * 16)
        here_x, here_y, here_z = column[0, rows, :], column[1, rows, :], column[2, rows, :]
        keep = mask[step // 2 : step // 2 + 1, :]
        for tile in range(NARROW // LANES):
            lanes = slice(tile * LANES, (tile + 1) * LANES)
            dx = here_x - across_x[:, lanes]
            dy = here_y - across_y[:, lanes]
            dz = here_z - across_z[:, lanes]
            xx = dx * dx
            yy = dy * dy
            distance2 = xx + yy + dz * dz
            square = jnp.maximum(distance2, 1.0)
            inverse = lax.rsqrt(square)
            damping = 1.0 + jnp.tanh(1.25 * (square * inverse) - 3.0)
            inverse2 = inverse * inverse
            kept = keep[:, first_lane + tile * LANES : first_lane + (tile + 1) * LANES]
            weight = damping * (inverse2 * inverse2 * inverse) * kept
            radial = weight * distance2
            minus3 = -3.0 * weight
            along_x = minus3 * dx
            along_y = minus3 * dy
            entries = (
                radial + minus3 * xx,
                radial + minus3 * yy,
                along_x * dy,
                along_x * dz,
                along_y * dz,
            )
            for slot, entry in enumerate(entries):
                top = entry.astype(BF16)
                at = slice(slot * NARROW + tile * LANES, slot * NARROW + (tile + 1) * LANES)
                high[rows, at] = top
                low[rows, at] = (entry - top.astype(F32)).astype(BF16)

    outs = []
    for chunk in range(0, WIDE, CHUNK):
        for step in range(chunk // 16, (chunk + CHUNK) // 16):
            rows16(step)
        rows = slice(chunk, chunk + CHUNK)
        outs.append(product(high[rows, :], low[rows, :], side))
    return jnp.concatenate(outs, axis=0)


def first_own_kernel(mask, column, points, gathered, total, high, low, side):
    vectors = gathered[...].reshape(NARROW, LANES)
    right_side(vectors, side)
    total[...] = build_and_apply(mask, vectors, column, points, high, low, side, 0)


def first_other_kernel(mask, column, points, gathered, total, part_out, high, low, side):
    vectors = gathered[...].reshape(NARROW, LANES)
    right_side(vectors, side)
    out = build_and_apply(mask, vectors, column, points, high, low, side, NARROW)
    part_out[...] = (total[...] + out).reshape(GROUP, ATOMS, LANES)


def spare_sums(vectors):
    return jnp.where(lane_ids(ATOMS) < COMPS * RHS, 0.0, jnp.sum(vectors, axis=0))


def second_own_kernel(gathered, high, low, total, side):
    vectors = gathered[...]
    right_side(vectors.reshape(NARROW, LANES), side)
    out = product(high[...], low[...], side).reshape(GROUP, ATOMS, LANES) + spare_sums(vectors)[None]
    total[...] = out


def second_other_kernel(gathered, high, low, total, part_out, side):
    vectors = gathered[...]
    right_side(vectors.reshape(NARROW, LANES), side)
    out = product(high[...], low[...], side).reshape(GROUP, ATOMS, LANES) + spare_sums(vectors)[None]
    part_out[...] = total[...] + out


def shifted_kernel(parts, own, aux, out, work):
    coupled = jnp.sum(parts[...], axis=0)
    inside = lane_ids(ATOMS) < COMPS * RHS
    vector = jnp.where(inside, own[...], 0.0)
    mapped = aux[0:ATOMS, :] * vector + coupled
    sums = jnp.zeros((SUMS, LANES), F32)
    row = lax.broadcasted_iota(jnp.int32, (SUMS, LANES), 0)
    for slot, terms in enumerate((vector * vector, vector * mapped, mapped * mapped)):
        sums = jnp.where(row == slot, jnp.sum(terms, axis=0, keepdims=True), sums)
    sums = sum_components(sums)
    work[...] = jnp.zeros_like(work)
    work[SUM_ROW : SUM_ROW + SUMS, :] = pltpu.roll(sums, 4, 0)
    work[SUM_ROW + SUMS : SUM_ROW + 2 * SUMS, :] = pltpu.roll(sums, LANES - ATOMS, 1)
    payload = jnp.where(inside, mapped, work[...].T[0:ATOMS, :])
    for slot in range(HALF):
        out[slot] = payload


def second_kernel(gathered, high, low, part_out, side):
    vectors = gathered[...]
    right_side(vectors.reshape(WIDE, LANES), side)
    sums = jnp.where(lane_ids(ATOMS) < COMPS * RHS, 0.0, jnp.sum(vectors, axis=0))
    part_out[...] = product(high[...], low[...], side).reshape(GROUP, ATOMS, LANES) + sums[None]


def step_kernel(parts, own, shifted, aux, sums_out, state, work):
    total = jnp.sum(parts[...], axis=0)
    vector = own[...]
    mapped = shifted[0]
    twice = aux[0:ATOMS, :] * mapped + total
    work[...] = jnp.zeros_like(work)
    work[0:ATOMS, :] = total
    turned = work[...].T
    lane8 = lane_ids(SUMS)
    head = pltpu.roll(turned[SUM_ROW : SUM_ROW + SUMS, :], 4, 0)
    tail = pltpu.roll(turned[SUM_ROW + SUMS : SUM_ROW + 2 * SUMS, :], ATOMS, 1)
    sums = jnp.where(lane8 < ATOMS, head, jnp.where(lane8 < RHS, tail, 0.0))
    sums = sums + pltpu.roll(sums, RHS, 1) + pltpu.roll(sums, 2 * RHS, 1)
    bb, be, ee = sums[0:1, :], sums[1:2, :], sums[2:3, :]
    shift = aux[ATOMS : ATOMS + 1, :]
    bm = shift * bb + be
    step = bb / bm
    kept = be / bm
    beta = (bb * ee - be * be) / (bm * bm)
    residual = kept * vector - step * mapped
    direction = residual + beta * vector
    image = shift * direction + ((kept + beta) * mapped - step * twice)
    row = lax.broadcasted_iota(jnp.int32, (SUMS, LANES), 0)
    squares = jnp.sum(residual * residual, axis=0, keepdims=True)
    curvature = jnp.sum(direction * image, axis=0, keepdims=True)
    both = sum_components(jnp.where(row == 0, squares, jnp.where(row == 1, curvature, 0.0)))
    lane = lax.broadcasted_iota(jnp.int32, (1, LANES), 1)
    packed = jnp.where(lane < RHS, both[0:1, :], jnp.where(lane < 2 * RHS, both[1:2, :], 0.0))
    sums_out[...] = jnp.broadcast_to(packed, sums_out.shape)
    state[0] = step * vector
    state[1] = direction
    state[2] = residual
    state[3] = image


def pair_kernel(sums, swapped, out):
    out[...] = jnp.broadcast_to((sums[...] + swapped[...])[None], out.shape)


def finish_kernel(gathered, state, dipoles, residual):
    total = jnp.sum(gathered[...], axis=0)
    total = jnp.broadcast_to(jnp.sum(total, axis=0, keepdims=True), (SUMS, LANES))
    first, second, third = component_lanes(SUMS)
    up = pltpu.roll(total, RHS, 1)
    up2 = pltpu.roll(total, 2 * RHS, 1)
    down = pltpu.roll(total, LANES - RHS, 1)
    squares = jnp.where(first, total, jnp.where(second, up, up2))
    curvature = jnp.where(first, down, jnp.where(second, total, jnp.where(third, up, 1.0)))
    step = (squares / curvature)[0:1, :]
    for out, value in (
        (dipoles, state[0] + step * state[1]),
        (residual, state[2] - step * state[3]),
    ):
        for comp in range(COMPS):
            out[comp] = value[:, comp * RHS : (comp + 1) * RHS]


def shape(*dims, dtype=F32):
    return jax.ShapeDtypeStruct(dims, dtype)


def whole(*dims):
    return pl.BlockSpec(dims, lambda i: (0,) * len(dims))


def number(row, z, core):
    return row * GROUP + z * 2 + core


def trade(value, bits):
    return lax.ppermute(value, "device", [(here, here ^ bits) for here in range(GROUP * GROUP)])


def core_swap(value):
    return trade(value, 1)


def exchange(value, groups):
    return lax.all_to_all(value, "device", 0, 0, axis_index_groups=groups)


ROWS = [[number(row, z, core) for row in range(GROUP)] for z in range(HALF) for core in range(2)]
LINES = [[number(row, z, core) for z in range(HALF)] for row in range(GROUP) for core in range(2)]
CHIPS = [[number(row, z, core) for row in range(GROUP) for z in range(HALF)] for core in range(2)]
MIXED = [[number(row, z, 1) for z in range(HALF)] for row in range(GROUP)] + [
    [number(row, z, 0) for row in range(first, GROUP, 2)] for first in range(2) for z in range(HALF)
]


def local(external_field, jitter, species, alpha_table, block_cell, tile_map):
    me = lax.axis_index("device")
    ids = jnp.stack([me // GROUP, me % GROUP]).astype(jnp.int32)
    field = external_field.transpose(0, 2, 1)
    across_field = core_swap(field)
    shifts = [jnp.pad(jitter, ((0, 0), (0, LANES - ATOMS)))]
    shifts = shifts + [trade(jitter, bits) for bits in (1, GROUP, GROUP + 1)]
    cells = jnp.pad(block_cell.astype(F32)[None], ((0, SUMS - 1), (0, 0)))
    kinds = jnp.concatenate(
        [
            jnp.pad(species.astype(F32)[None], ((0, 3), (0, LANES - ATOMS))),
            jnp.pad(alpha_table.T, ((0, 0), (0, LANES - 12))),
        ]
    )
    vec, vector = pl.pallas_call(
        prepare_kernel,
        out_shape=(shape(HALF, 2 * ATOMS, LANES), shape(ATOMS, LANES)),
        in_specs=[VMEM] * 6,
        out_specs=(VMEM, VMEM),
        scratch_shapes=[SQUARE, pltpu.VMEM((ATOMS, LANES), F32)],
        compiler_params=PARAMS,
        name="prepare",
    )(*shifts, jnp.pad(field, ((0, 0), (0, 0), (0, LANES - RHS))), across_field)
    column_shape = shape(COMPS, WIDE, LANES)
    aux, mask, points, across, flags = pl.pallas_call(
        side_kernel,
        out_shape=(shape(ATOMS + SUMS, LANES), shape(GROUP, WIDE), column_shape, shape(SUMS, WIDE), shape(2 * ATOMS, LANES)),
        in_specs=[SMEM, VMEM, VMEM, VMEM],
        out_specs=(VMEM,) * 5,
        scratch_shapes=[SQUARE],
        compiler_params=PARAMS,
        name="side",
    )(ids, kinds, cells, tile_map)
    mine, aux, mask, points, across, flags = lax.optimization_barrier(
        (exchange(vec, MIXED), aux, mask, points, across, flags)
    )
    half = shape(HALF, ATOMS, LANES)
    own, other, column = pl.pallas_call(
        pick_kernel,
        out_shape=(half, half, column_shape),
        in_specs=[VMEM, VMEM, VMEM, VMEM],
        out_specs=(VMEM, VMEM, VMEM),
        compiler_params=PARAMS,
        name="pick",
    )(flags, points, mine, core_swap(mine))
    side = pltpu.VMEM((PAIRS * NARROW, 2 * LANES), BF16)
    tile = shape(WIDE, PAIRS * NARROW, dtype=BF16)
    total, high0, low0 = pl.pallas_call(
        first_own_kernel,
        out_shape=(shape(WIDE, LANES), tile, tile),
        in_specs=[VMEM] * 4,
        out_specs=(VMEM, VMEM, VMEM),
        scratch_shapes=[side],
        compiler_params=PARAMS,
        name="first_own",
    )(mask, column, across, own)
    part, high1, low1 = pl.pallas_call(
        first_other_kernel,
        out_shape=(shape(GROUP, ATOMS, LANES), tile, tile),
        in_specs=[VMEM] * 5,
        out_specs=(VMEM, VMEM, VMEM),
        scratch_shapes=[side],
        compiler_params=PARAMS,
        name="first_other",
    )(mask, column, across, other, total)
    parts = exchange(part, ROWS)
    blocks = whole(GROUP, ATOMS, LANES)
    block = whole(1, ATOMS, LANES)
    shifted = pl.pallas_call(
        shifted_kernel,
        grid=(1,),
        out_shape=shape(HALF, ATOMS, LANES),
        in_specs=[blocks, whole(ATOMS, LANES), whole(ATOMS + SUMS, LANES)],
        out_specs=whole(HALF, ATOMS, LANES),
        scratch_shapes=[SQUARE],
        compiler_params=PARAMS,
        name="shifted",
    )(parts, vector, aux)
    own2 = exchange(shifted, LINES)
    other2 = core_swap(own2)
    total2 = pl.pallas_call(
        second_own_kernel,
        out_shape=shape(GROUP, ATOMS, LANES),
        in_specs=[VMEM] * 3,
        out_specs=VMEM,
        scratch_shapes=[side],
        compiler_params=PARAMS,
        name="second_own",
    )(own2, high0, low0)
    part2 = pl.pallas_call(
        second_other_kernel,
        out_shape=shape(GROUP, ATOMS, LANES),
        in_specs=[VMEM] * 4,
        out_specs=VMEM,
        scratch_shapes=[side],
        compiler_params=PARAMS,
        name="second_other",
    )(other2, high1, low1, total2)
    parts2 = exchange(part2, ROWS)
    sums, state = pl.pallas_call(
        step_kernel,
        grid=(1,),
        out_shape=(shape(SUMS, LANES), shape(4, ATOMS, LANES)),
        in_specs=[blocks, whole(ATOMS, LANES), block, whole(ATOMS + SUMS, LANES)],
        out_specs=(whole(SUMS, LANES), whole(4, ATOMS, LANES)),
        scratch_shapes=[SQUARE],
        compiler_params=PARAMS,
        name="step",
    )(parts2, vector, shifted, aux)
    pair = pl.pallas_call(
        pair_kernel,
        out_shape=shape(GROUP, SUMS, LANES),
        in_specs=[VMEM, VMEM],
        out_specs=VMEM,
        compiler_params=PARAMS,
        name="pair",
    )(sums, core_swap(sums))
    pair = pair.reshape(GROUP * HALF, 1, LANES)
    all_sums = exchange(pair, CHIPS).reshape(GROUP, SUMS, LANES)
    dipoles, residual = pl.pallas_call(
        finish_kernel,
        out_shape=(shape(COMPS, ATOMS, RHS), shape(COMPS, ATOMS, RHS)),
        in_specs=[VMEM, VMEM],
        out_specs=(VMEM, VMEM),
        compiler_params=PARAMS,
        name="finish",
    )(all_sums, state)
    return dipoles.transpose(0, 2, 1), residual.transpose(0, 2, 1)


def solution(mesh):
    flat = Mesh(mesh.devices.reshape(GROUP * GROUP), ("device",))
    every = "device"
    return jax.shard_map(
        local,
        mesh=flat,
        in_specs=(P(None, None, every), P(None, every), P(every), P(), P(), P()),
        out_specs=(P(None, None, every), P(None, None, every)),
        check_vma=False,
    )
```

```python
import jax
import jax.numpy as jnp
from jax import lax
from jax.experimental import pallas as pl
from jax.experimental.pallas import tpu as pltpu
from jax.sharding import Mesh, PartitionSpec as P

COMPS = 3
RHS = 36
ATOMS = 32
GROUP = 16
HALF = 8
LANES = 128
SUMS = 8
SITE = 120
SUM_ROW = 104
WIDE = GROUP * ATOMS
NARROW = HALF * ATOMS
CHUNK = 256
PAIRS = 5
SPACING = 2.0
F32 = jnp.float32
BF16 = jnp.bfloat16

VMEM = pl.BlockSpec(memory_space=pltpu.VMEM)
SMEM = pl.BlockSpec(memory_space=pltpu.SMEM)
SQUARE = pltpu.VMEM((LANES, LANES), F32)
PARAMS = pltpu.CompilerParams(vmem_limit_bytes=16 * 1024 * 1024)


def lane_ids(rows):
    return lax.broadcasted_iota(jnp.int32, (rows, LANES), 1)


def component_lanes(rows):
    lanes = lane_ids(rows)
    first = lanes < RHS
    second = (lanes >= RHS) & (lanes < 2 * RHS)
    third = (lanes >= 2 * RHS) & (lanes < COMPS * RHS)
    return first, second, third


def sum_components(value):
    first, second, third = component_lanes(SUMS)
    up = pltpu.roll(value, RHS, 1)
    up2 = pltpu.roll(value, 2 * RHS, 1)
    down = pltpu.roll(value, LANES - RHS, 1)
    down2 = pltpu.roll(value, LANES - 2 * RHS, 1)
    of_first = value + down + down2
    of_second = up + value + down
    of_third = up2 + up + value
    return jnp.where(first, of_first, jnp.where(second, of_second, jnp.where(third, of_third, 1.0)))


def prepare_kernel(jitter, across, beside, corner, field, partner, vec_out, own_out, work, wide):
    work[...] = jnp.zeros_like(work)
    for flip, near, far, vectors in ((0, jitter, beside, field), (1, across, corner, partner)):
        work[SITE : SITE + COMPS, 0:ATOMS] = near[:, 0:ATOMS]
        work[SITE + 4 : SITE + 4 + COMPS, 0:ATOMS] = far[...]
        wide[...] = work[...].T[0:ATOMS, :]
        for part in range(COMPS):
            wide[:, part * RHS : (part + 1) * RHS] = vectors[part, :, 0:RHS]
        turned = wide[...]
        if flip == 0:
            own_out[...] = turned
        for slot in range(HALF):
            vec_out[slot, flip * ATOMS : (flip + 1) * ATOMS, :] = turned


def lattice(comp, atom, cell):
    if isinstance(comp, int):
        inner = (atom >> 3, (atom >> 1) & 3, atom & 1)[comp]
        corner = ((cell >> 5) * 4, ((cell >> 2) & 7) * 4, (cell & 3) * 2)[comp]
        return (corner + inner).astype(F32) * SPACING
    inner = jnp.where(comp == 0, atom >> 3, jnp.where(comp == 1, (atom >> 1) & 3, atom & 1))
    corner = jnp.where(comp == 0, (cell >> 5) * 4, jnp.where(comp == 1, ((cell >> 2) & 7) * 4, (cell & 3) * 2))
    return (corner + inner).astype(F32) * SPACING


def side_kernel(ids, species, cells, tile_map, aux_out, mask_out, points, across, flags, work):
    alpha = species[4:SUMS, :]
    lane = lax.broadcasted_iota(jnp.int32, (4, LANES), 1)
    rhs_lane = jnp.where(lane >= 2 * RHS, lane - 2 * RHS, jnp.where(lane >= RHS, lane - RHS, lane))
    table = jnp.ones((4, LANES), F32)
    for freq in range(12):
        table = jnp.where(
            (rhs_lane >= 3 * freq) & (rhs_lane < 3 * freq + 3),
            jnp.broadcast_to(alpha[:, freq : freq + 1], (4, LANES)),
            table,
        )
    inverse = 1.0 / table
    shift = 0.25 * ((inverse[0:1] + inverse[1:2]) + (inverse[2:3] + inverse[3:4]))
    work[0:SUMS, :] = species[...]
    kinds = jnp.broadcast_to(work[...].T[0:ATOMS, 0:1], (ATOMS, LANES))
    diag = jnp.zeros((ATOMS, LANES), F32)
    for kind in range(4):
        diag = jnp.where(kinds == float(kind), inverse[kind : kind + 1] - shift, diag)
    aux_out[0:ATOMS, :] = diag
    aux_out[ATOMS : ATOMS + SUMS, :] = jnp.broadcast_to(shift, (SUMS, LANES))

    blocks = GROUP * GROUP
    active = jnp.where(tile_map[...] != 0, 1.0, 0.0).astype(BF16)
    place = lax.broadcasted_iota(jnp.int32, (GROUP, blocks), 1)
    wanted = lax.broadcasted_iota(jnp.int32, (GROUP, blocks), 0) * GROUP + ids[1]
    pick = jnp.where(place == wanted, 1.0, 0.0).astype(BF16)
    lines = jnp.dot(pick, active, preferred_element_type=F32).astype(BF16)
    slot = lax.broadcasted_iota(jnp.int32, (blocks, WIDE), 1) // ATOMS
    wanted = ids[0] * GROUP + (slot % HALF) * 2 + ((ids[1] % 2) ^ (slot // HALF))
    place = lax.broadcasted_iota(jnp.int32, (blocks, WIDE), 0)
    spread = jnp.where(place == wanted, 1.0, 0.0).astype(BF16)
    mask_out[...] = 0.5 * jnp.dot(lines, spread, preferred_element_type=F32)

    cell = jnp.dot(cells[...].astype(BF16), spread, preferred_element_type=F32)[0:1, :].astype(jnp.int32)
    comp = lax.broadcasted_iota(jnp.int32, (SUMS, WIDE), 0)
    atom = lax.broadcasted_iota(jnp.int32, (SUMS, WIDE), 1) & (ATOMS - 1)
    across[...] = lattice(comp, atom, cell)
    place = lax.broadcasted_iota(jnp.int32, (WIDE, blocks), 1)
    row = lax.broadcasted_iota(jnp.int32, (WIDE, blocks), 0)
    wanted = (row // ATOMS) * GROUP + ids[1]
    cell = jnp.sum(jnp.where(place == wanted, cells[0:1, :], 0.0), axis=1, keepdims=True).astype(jnp.int32)
    atom = lax.broadcasted_iota(jnp.int32, (WIDE, LANES), 0) & (ATOMS - 1)
    for comp in range(COMPS):
        points[comp] = lattice(comp, atom, cell)
    flags[0:ATOMS, :] = jnp.full((ATOMS, LANES), ids[1] % 2, jnp.int32).astype(F32)
    flags[ATOMS : 2 * ATOMS, :] = jnp.full((ATOMS, LANES), ids[0] % 2, jnp.int32).astype(F32)


def right_side(vectors, side):
    first, second, third = component_lanes(NARROW)
    zero = jnp.zeros_like(vectors)
    up = pltpu.roll(vectors, RHS, 1)
    up2 = pltpu.roll(vectors, 2 * RHS, 1)
    down = pltpu.roll(vectors, LANES - RHS, 1)
    down2 = pltpu.roll(vectors, LANES - 2 * RHS, 1)
    parts = (
        jnp.where(first, vectors, jnp.where(third, -vectors, zero)),
        jnp.where(second, vectors, jnp.where(third, -vectors, zero)),
        jnp.where(first, down, jnp.where(second, up, zero)),
        jnp.where(first, down2, jnp.where(third, up2, zero)),
        jnp.where(second, down, jnp.where(third, up, zero)),
    )
    for slot, part in enumerate(parts):
        high = part.astype(BF16)
        low = (part - high.astype(F32)).astype(BF16)
        side[slot * NARROW : (slot + 1) * NARROW, 0:LANES] = high
        side[slot * NARROW : (slot + 1) * NARROW, LANES : 2 * LANES] = low


def product(high, low, side):
    both = jnp.dot(high, side[...], preferred_element_type=F32)
    rest = jnp.dot(low, side[:, 0:LANES], preferred_element_type=F32)
    return both[:, 0:LANES] + (both[:, LANES:] + rest)


def build_and_apply(mask, vectors, column, points, high, low, side, first_lane):
    across = vectors.T[SITE : SITE + SUMS, :] + points[:, first_lane : first_lane + NARROW]
    across_x, across_y, across_z = across[0:1, :], across[1:2, :], across[2:3, :]

    def rows16(step):
        rows = slice(step * 16, (step + 1) * 16)
        here_x, here_y, here_z = column[0, rows, :], column[1, rows, :], column[2, rows, :]
        keep = mask[step // 2 : step // 2 + 1, :]
        for tile in range(NARROW // LANES):
            lanes = slice(tile * LANES, (tile + 1) * LANES)
            dx = here_x - across_x[:, lanes]
            dy = here_y - across_y[:, lanes]
            dz = here_z - across_z[:, lanes]
            xx = dx * dx
            yy = dy * dy
            distance2 = xx + yy + dz * dz
            square = jnp.maximum(distance2, 1.0)
            inverse = lax.rsqrt(square)
            damping = 1.0 + jnp.tanh(1.25 * (square * inverse) - 3.0)
            inverse2 = inverse * inverse
            kept = keep[:, first_lane + tile * LANES : first_lane + (tile + 1) * LANES]
            weight = damping * (inverse2 * inverse2 * inverse) * kept
            radial = weight * distance2
            minus3 = -3.0 * weight
            along_x = minus3 * dx
            along_y = minus3 * dy
            entries = (
                radial + minus3 * xx,
                radial + minus3 * yy,
                along_x * dy,
                along_x * dz,
                along_y * dz,
            )
            for slot, entry in enumerate(entries):
                top = entry.astype(BF16)
                at = slice(slot * NARROW + tile * LANES, slot * NARROW + (tile + 1) * LANES)
                high[rows, at] = top
                low[rows, at] = (entry - top.astype(F32)).astype(BF16)

    outs = []
    for chunk in range(0, WIDE, CHUNK):
        for step in range(chunk // 16, (chunk + CHUNK) // 16):
            rows16(step)
        rows = slice(chunk, chunk + CHUNK)
        outs.append(product(high[rows, :], low[rows, :], side))
    return jnp.concatenate(outs, axis=0)


def first_kernel(
    flags, points, mask, across, mine, theirs,
    part_out, high0, low0, high1, low1, own, other, column, side0, side1
):
    odd_core = flags[0:ATOMS, :] > 0.5
    odd_row = flags[ATOMS : 2 * ATOMS, :] > 0.5
    for slot in range(HALF):
        first, second = mine[slot, 0:ATOMS, :], mine[slot, ATOMS : 2 * ATOMS, :]
        third, fourth = theirs[slot, 0:ATOMS, :], theirs[slot, ATOMS : 2 * ATOMS, :]
        own[slot] = jnp.where(odd_core, first, fourth)
        other[slot] = jnp.where(odd_core, second, third)
        rows = jnp.where(odd_core, fourth, first)
        beside = pltpu.roll(rows, LANES - 4, 1)
        for block, sites in (
            (2 * slot, jnp.where(odd_row, beside, rows)),
            (2 * slot + 1, jnp.where(odd_row, rows, beside)),
        ):
            place = slice(block * ATOMS, (block + 1) * ATOMS)
            for comp in range(COMPS):
                column[comp, place, :] = points[comp, place, :] + sites[:, SITE + comp : SITE + comp + 1]

    total = jnp.zeros((WIDE, LANES), F32)
    halves = ((own, high0, low0, side0), (other, high1, low1, side1))
    for half, (gathered, high, low, right) in enumerate(halves):
        vectors = gathered[...].reshape(NARROW, LANES)
        right_side(vectors, right)
        total = total + build_and_apply(mask, vectors, column, across, high, low, right, half * NARROW)
    part_out[...] = total.reshape(GROUP, ATOMS, LANES)


def spare_sums(vectors):
    return jnp.where(lane_ids(ATOMS) < COMPS * RHS, 0.0, jnp.sum(vectors, axis=0))


def second_own_kernel(gathered, high, low, total, side):
    vectors = gathered[...]
    right_side(vectors.reshape(NARROW, LANES), side)
    out = product(high[...], low[...], side).reshape(GROUP, ATOMS, LANES) + spare_sums(vectors)[None]
    total[...] = out


def second_other_kernel(gathered, high, low, total, part_out, side):
    vectors = gathered[...]
    right_side(vectors.reshape(NARROW, LANES), side)
    out = product(high[...], low[...], side).reshape(GROUP, ATOMS, LANES) + spare_sums(vectors)[None]
    part_out[...] = total[...] + out


def shifted_kernel(parts, own, aux, out, work):
    coupled = jnp.sum(parts[...], axis=0)
    inside = lane_ids(ATOMS) < COMPS * RHS
    vector = jnp.where(inside, own[...], 0.0)
    mapped = aux[0:ATOMS, :] * vector + coupled
    sums = jnp.zeros((SUMS, LANES), F32)
    row = lax.broadcasted_iota(jnp.int32, (SUMS, LANES), 0)
    for slot, terms in enumerate((vector * vector, vector * mapped, mapped * mapped)):
        sums = jnp.where(row == slot, jnp.sum(terms, axis=0, keepdims=True), sums)
    sums = sum_components(sums)
    work[...] = jnp.zeros_like(work)
    work[SUM_ROW : SUM_ROW + SUMS, :] = pltpu.roll(sums, 4, 0)
    work[SUM_ROW + SUMS : SUM_ROW + 2 * SUMS, :] = pltpu.roll(sums, LANES - ATOMS, 1)
    payload = jnp.where(inside, mapped, work[...].T[0:ATOMS, :])
    for slot in range(HALF):
        out[slot] = payload


def second_kernel(gathered, high, low, part_out, side):
    vectors = gathered[...]
    right_side(vectors.reshape(WIDE, LANES), side)
    sums = jnp.where(lane_ids(ATOMS) < COMPS * RHS, 0.0, jnp.sum(vectors, axis=0))
    part_out[...] = product(high[...], low[...], side).reshape(GROUP, ATOMS, LANES) + sums[None]


def step_kernel(parts, own, shifted, aux, sums_out, state, work):
    total = jnp.sum(parts[...], axis=0)
    vector = own[...]
    mapped = shifted[0]
    twice = aux[0:ATOMS, :] * mapped + total
    work[...] = jnp.zeros_like(work)
    work[0:ATOMS, :] = total
    turned = work[...].T
    lane8 = lane_ids(SUMS)
    head = pltpu.roll(turned[SUM_ROW : SUM_ROW + SUMS, :], 4, 0)
    tail = pltpu.roll(turned[SUM_ROW + SUMS : SUM_ROW + 2 * SUMS, :], ATOMS, 1)
    sums = jnp.where(lane8 < ATOMS, head, jnp.where(lane8 < RHS, tail, 0.0))
    sums = sums + pltpu.roll(sums, RHS, 1) + pltpu.roll(sums, 2 * RHS, 1)
    bb, be, ee = sums[0:1, :], sums[1:2, :], sums[2:3, :]
    shift = aux[ATOMS : ATOMS + 1, :]
    bm = shift * bb + be
    step = bb / bm
    kept = be / bm
    beta = (bb * ee - be * be) / (bm * bm)
    residual = kept * vector - step * mapped
    direction = residual + beta * vector
    image = shift * direction + ((kept + beta) * mapped - step * twice)
    row = lax.broadcasted_iota(jnp.int32, (SUMS, LANES), 0)
    squares = jnp.sum(residual * residual, axis=0, keepdims=True)
    curvature = jnp.sum(direction * image, axis=0, keepdims=True)
    both = sum_components(jnp.where(row == 0, squares, jnp.where(row == 1, curvature, 0.0)))
    lane = lax.broadcasted_iota(jnp.int32, (1, LANES), 1)
    packed = jnp.where(lane < RHS, both[0:1, :], jnp.where(lane < 2 * RHS, both[1:2, :], 0.0))
    sums_out[...] = jnp.broadcast_to(packed, sums_out.shape)
    state[0] = step * vector
    state[1] = direction
    state[2] = residual
    state[3] = image


def pair_kernel(sums, swapped, out):
    out[...] = jnp.broadcast_to((sums[...] + swapped[...])[None], out.shape)


def finish_kernel(gathered, state, dipoles, residual):
    total = jnp.sum(gathered[...], axis=0)
    total = jnp.broadcast_to(jnp.sum(total, axis=0, keepdims=True), (SUMS, LANES))
    first, second, third = component_lanes(SUMS)
    up = pltpu.roll(total, RHS, 1)
    up2 = pltpu.roll(total, 2 * RHS, 1)
    down = pltpu.roll(total, LANES - RHS, 1)
    squares = jnp.where(first, total, jnp.where(second, up, up2))
    curvature = jnp.where(first, down, jnp.where(second, total, jnp.where(third, up, 1.0)))
    step = (squares / curvature)[0:1, :]
    for out, value in (
        (dipoles, state[0] + step * state[1]),
        (residual, state[2] - step * state[3]),
    ):
        for comp in range(COMPS):
            out[comp] = value[:, comp * RHS : (comp + 1) * RHS]


def shape(*dims, dtype=F32):
    return jax.ShapeDtypeStruct(dims, dtype)


def whole(*dims):
    return pl.BlockSpec(dims, lambda i: (0,) * len(dims))


def number(row, z, core):
    return row * GROUP + z * 2 + core


def trade(value, bits):
    return lax.ppermute(value, "device", [(here, here ^ bits) for here in range(GROUP * GROUP)])


def core_swap(value):
    return trade(value, 1)


def exchange(value, groups):
    return lax.all_to_all(value, "device", 0, 0, axis_index_groups=groups)


ROWS = [[number(row, z, core) for row in range(GROUP)] for z in range(HALF) for core in range(2)]
LINES = [[number(row, z, core) for z in range(HALF)] for row in range(GROUP) for core in range(2)]
CHIPS = [[number(row, z, core) for row in range(GROUP) for z in range(HALF)] for core in range(2)]
MIXED = [[number(row, z, 1) for z in range(HALF)] for row in range(GROUP)] + [
    [number(row, z, 0) for row in range(first, GROUP, 2)] for first in range(2) for z in range(HALF)
]


def local(external_field, jitter, species, alpha_table, block_cell, tile_map):
    me = lax.axis_index("device")
    ids = jnp.stack([me // GROUP, me % GROUP]).astype(jnp.int32)
    field = external_field.transpose(0, 2, 1)
    across_field = core_swap(field)
    shifts = [jnp.pad(jitter, ((0, 0), (0, LANES - ATOMS)))]
    shifts = shifts + [trade(jitter, bits) for bits in (1, GROUP, GROUP + 1)]
    cells = jnp.pad(block_cell.astype(F32)[None], ((0, SUMS - 1), (0, 0)))
    kinds = jnp.concatenate(
        [
            jnp.pad(species.astype(F32)[None], ((0, 3), (0, LANES - ATOMS))),
            jnp.pad(alpha_table.T, ((0, 0), (0, LANES - 12))),
        ]
    )
    vec, vector = pl.pallas_call(
        prepare_kernel,
        out_shape=(shape(HALF, 2 * ATOMS, LANES), shape(ATOMS, LANES)),
        in_specs=[VMEM] * 6,
        out_specs=(VMEM, VMEM),
        scratch_shapes=[SQUARE, pltpu.VMEM((ATOMS, LANES), F32)],
        compiler_params=PARAMS,
        name="prepare",
    )(*shifts, jnp.pad(field, ((0, 0), (0, 0), (0, LANES - RHS))), across_field)
    column_shape = shape(COMPS, WIDE, LANES)
    aux, mask, points, across, flags = pl.pallas_call(
        side_kernel,
        out_shape=(shape(ATOMS + SUMS, LANES), shape(GROUP, WIDE), column_shape, shape(SUMS, WIDE), shape(2 * ATOMS, LANES)),
        in_specs=[SMEM, VMEM, VMEM, VMEM],
        out_specs=(VMEM,) * 5,
        scratch_shapes=[SQUARE],
        compiler_params=PARAMS,
        name="side",
    )(ids, kinds, cells, tile_map)
    mine, aux, mask, points, across, flags = lax.optimization_barrier(
        (exchange(vec, MIXED), aux, mask, points, across, flags)
    )
    side = pltpu.VMEM((PAIRS * NARROW, 2 * LANES), BF16)
    half = pltpu.VMEM((HALF, ATOMS, LANES), F32)
    tile = shape(WIDE, PAIRS * NARROW, dtype=BF16)
    part, high0, low0, high1, low1 = pl.pallas_call(
        first_kernel,
        out_shape=(shape(GROUP, ATOMS, LANES), tile, tile, tile, tile),
        in_specs=[VMEM] * 6,
        out_specs=(VMEM,) * 5,
        scratch_shapes=[half, half, pltpu.VMEM((COMPS, WIDE, LANES), F32), side, side],
        compiler_params=PARAMS,
        name="first",
    )(flags, points, mask, across, mine, core_swap(mine))
    parts = exchange(part, ROWS)
    blocks = whole(GROUP, ATOMS, LANES)
    block = whole(1, ATOMS, LANES)
    shifted = pl.pallas_call(
        shifted_kernel,
        grid=(1,),
        out_shape=shape(HALF, ATOMS, LANES),
        in_specs=[blocks, whole(ATOMS, LANES), whole(ATOMS + SUMS, LANES)],
        out_specs=whole(HALF, ATOMS, LANES),
        scratch_shapes=[SQUARE],
        compiler_params=PARAMS,
        name="shifted",
    )(parts, vector, aux)
    own2 = exchange(shifted, LINES)
    other2 = core_swap(own2)
    total2 = pl.pallas_call(
        second_own_kernel,
        out_shape=shape(GROUP, ATOMS, LANES),
        in_specs=[VMEM] * 3,
        out_specs=VMEM,
        scratch_shapes=[side],
        compiler_params=PARAMS,
        name="second_own",
    )(own2, high0, low0)
    part2 = pl.pallas_call(
        second_other_kernel,
        out_shape=shape(GROUP, ATOMS, LANES),
        in_specs=[VMEM] * 4,
        out_specs=VMEM,
        scratch_shapes=[side],
        compiler_params=PARAMS,
        name="second_other",
    )(other2, high1, low1, total2)
    parts2 = exchange(part2, ROWS)
    sums, state = pl.pallas_call(
        step_kernel,
        grid=(1,),
        out_shape=(shape(SUMS, LANES), shape(4, ATOMS, LANES)),
        in_specs=[blocks, whole(ATOMS, LANES), block, whole(ATOMS + SUMS, LANES)],
        out_specs=(whole(SUMS, LANES), whole(4, ATOMS, LANES)),
        scratch_shapes=[SQUARE],
        compiler_params=PARAMS,
        name="step",
    )(parts2, vector, shifted, aux)
    pair = pl.pallas_call(
        pair_kernel,
        out_shape=shape(GROUP, SUMS, LANES),
        in_specs=[VMEM, VMEM],
        out_specs=VMEM,
        compiler_params=PARAMS,
        name="pair",
    )(sums, core_swap(sums))
    pair = pair.reshape(GROUP * HALF, 1, LANES)
    all_sums = exchange(pair, CHIPS).reshape(GROUP, SUMS, LANES)
    dipoles, residual = pl.pallas_call(
        finish_kernel,
        out_shape=(shape(COMPS, ATOMS, RHS), shape(COMPS, ATOMS, RHS)),
        in_specs=[VMEM, VMEM],
        out_specs=(VMEM, VMEM),
        compiler_params=PARAMS,
        name="finish",
    )(all_sums, state)
    return dipoles.transpose(0, 2, 1), residual.transpose(0, 2, 1)


def solution(mesh):
    flat = Mesh(mesh.devices.reshape(GROUP * GROUP), ("device",))
    every = "device"
    return jax.shard_map(
        local,
        mesh=flat,
        in_specs=(P(None, None, every), P(None, every), P(every), P(), P(), P()),
        out_specs=(P(None, None, every), P(None, None, every)),
        check_vma=False,
    )
```

```python
import jax
import jax.numpy as jnp
from jax import lax
from jax.experimental import pallas as pl
from jax.experimental.pallas import tpu as pltpu
from jax.sharding import Mesh, PartitionSpec as P

COMPS = 3
RHS = 36
ATOMS = 32
GROUP = 16
HALF = 8
LANES = 128
SUMS = 8
SITE = 120
SUM_ROW = 104
WIDE = GROUP * ATOMS
NARROW = HALF * ATOMS
CHUNK = 128
PAIRS = 5
SPACING = 2.0
F32 = jnp.float32
BF16 = jnp.bfloat16

VMEM = pl.BlockSpec(memory_space=pltpu.VMEM)
SMEM = pl.BlockSpec(memory_space=pltpu.SMEM)
SQUARE = pltpu.VMEM((LANES, LANES), F32)
PARAMS = pltpu.CompilerParams(vmem_limit_bytes=16 * 1024 * 1024)


def lane_ids(rows):
    return lax.broadcasted_iota(jnp.int32, (rows, LANES), 1)


def component_lanes(rows):
    lanes = lane_ids(rows)
    first = lanes < RHS
    second = (lanes >= RHS) & (lanes < 2 * RHS)
    third = (lanes >= 2 * RHS) & (lanes < COMPS * RHS)
    return first, second, third


def sum_components(value):
    first, second, third = component_lanes(SUMS)
    up = pltpu.roll(value, RHS, 1)
    up2 = pltpu.roll(value, 2 * RHS, 1)
    down = pltpu.roll(value, LANES - RHS, 1)
    down2 = pltpu.roll(value, LANES - 2 * RHS, 1)
    of_first = value + down + down2
    of_second = up + value + down
    of_third = up2 + up + value
    return jnp.where(first, of_first, jnp.where(second, of_second, jnp.where(third, of_third, 1.0)))


def prepare_kernel(jitter, across, beside, corner, field, partner, vec_out, own_out, work, wide):
    work[...] = jnp.zeros_like(work)
    for flip, near, far, vectors in ((0, jitter, beside, field), (1, across, corner, partner)):
        work[SITE : SITE + COMPS, 0:ATOMS] = near[:, 0:ATOMS]
        work[SITE + 4 : SITE + 4 + COMPS, 0:ATOMS] = far[...]
        wide[...] = work[...].T[0:ATOMS, :]
        for part in range(COMPS):
            wide[:, part * RHS : (part + 1) * RHS] = vectors[part, :, 0:RHS]
        turned = wide[...]
        if flip == 0:
            own_out[...] = turned
        for slot in range(HALF):
            vec_out[slot, flip * ATOMS : (flip + 1) * ATOMS, :] = turned


def lattice(comp, atom, cell):
    if isinstance(comp, int):
        inner = (atom >> 3, (atom >> 1) & 3, atom & 1)[comp]
        corner = ((cell >> 5) * 4, ((cell >> 2) & 7) * 4, (cell & 3) * 2)[comp]
        return (corner + inner).astype(F32) * SPACING
    inner = jnp.where(comp == 0, atom >> 3, jnp.where(comp == 1, (atom >> 1) & 3, atom & 1))
    corner = jnp.where(comp == 0, (cell >> 5) * 4, jnp.where(comp == 1, ((cell >> 2) & 7) * 4, (cell & 3) * 2))
    return (corner + inner).astype(F32) * SPACING


def side_kernel(ids, species, cells, tile_map, aux_out, mask_out, points, across, flags, work):
    alpha = species[4:SUMS, :]
    lane = lax.broadcasted_iota(jnp.int32, (4, LANES), 1)
    rhs_lane = jnp.where(lane >= 2 * RHS, lane - 2 * RHS, jnp.where(lane >= RHS, lane - RHS, lane))
    table = jnp.ones((4, LANES), F32)
    for freq in range(12):
        table = jnp.where(
            (rhs_lane >= 3 * freq) & (rhs_lane < 3 * freq + 3),
            jnp.broadcast_to(alpha[:, freq : freq + 1], (4, LANES)),
            table,
        )
    inverse = 1.0 / table
    shift = 0.25 * ((inverse[0:1] + inverse[1:2]) + (inverse[2:3] + inverse[3:4]))
    work[0:SUMS, :] = species[...]
    kinds = jnp.broadcast_to(work[...].T[0:ATOMS, 0:1], (ATOMS, LANES))
    diag = jnp.zeros((ATOMS, LANES), F32)
    for kind in range(4):
        diag = jnp.where(kinds == float(kind), inverse[kind : kind + 1] - shift, diag)
    aux_out[0:ATOMS, :] = diag
    aux_out[ATOMS : ATOMS + SUMS, :] = jnp.broadcast_to(shift, (SUMS, LANES))

    blocks = GROUP * GROUP
    active = jnp.where(tile_map[...] != 0, 1.0, 0.0).astype(BF16)
    place = lax.broadcasted_iota(jnp.int32, (GROUP, blocks), 1)
    wanted = lax.broadcasted_iota(jnp.int32, (GROUP, blocks), 0) * GROUP + ids[1]
    pick = jnp.where(place == wanted, 1.0, 0.0).astype(BF16)
    lines = jnp.dot(pick, active, preferred_element_type=F32).astype(BF16)
    slot = lax.broadcasted_iota(jnp.int32, (blocks, WIDE), 1) // ATOMS
    wanted = ids[0] * GROUP + (slot % HALF) * 2 + ((ids[1] % 2) ^ (slot // HALF))
    place = lax.broadcasted_iota(jnp.int32, (blocks, WIDE), 0)
    spread = jnp.where(place == wanted, 1.0, 0.0).astype(BF16)
    mask_out[...] = 0.5 * jnp.dot(lines, spread, preferred_element_type=F32)

    cell = jnp.dot(cells[...].astype(BF16), spread, preferred_element_type=F32)[0:1, :].astype(jnp.int32)
    comp = lax.broadcasted_iota(jnp.int32, (SUMS, WIDE), 0)
    atom = lax.broadcasted_iota(jnp.int32, (SUMS, WIDE), 1) & (ATOMS - 1)
    across[...] = lattice(comp, atom, cell)
    place = lax.broadcasted_iota(jnp.int32, (WIDE, blocks), 1)
    row = lax.broadcasted_iota(jnp.int32, (WIDE, blocks), 0)
    wanted = (row // ATOMS) * GROUP + ids[1]
    cell = jnp.sum(jnp.where(place == wanted, cells[0:1, :], 0.0), axis=1, keepdims=True).astype(jnp.int32)
    atom = lax.broadcasted_iota(jnp.int32, (WIDE, LANES), 0) & (ATOMS - 1)
    for comp in range(COMPS):
        points[comp] = lattice(comp, atom, cell)
    flags[0:ATOMS, :] = jnp.full((ATOMS, LANES), ids[1] % 2, jnp.int32).astype(F32)
    flags[ATOMS : 2 * ATOMS, :] = jnp.full((ATOMS, LANES), ids[0] % 2, jnp.int32).astype(F32)


def right_side(vectors, side):
    first, second, third = component_lanes(NARROW)
    zero = jnp.zeros_like(vectors)
    up = pltpu.roll(vectors, RHS, 1)
    up2 = pltpu.roll(vectors, 2 * RHS, 1)
    down = pltpu.roll(vectors, LANES - RHS, 1)
    down2 = pltpu.roll(vectors, LANES - 2 * RHS, 1)
    parts = (
        jnp.where(first, vectors, jnp.where(third, -vectors, zero)),
        jnp.where(second, vectors, jnp.where(third, -vectors, zero)),
        jnp.where(first, down, jnp.where(second, up, zero)),
        jnp.where(first, down2, jnp.where(third, up2, zero)),
        jnp.where(second, down, jnp.where(third, up, zero)),
    )
    for slot, part in enumerate(parts):
        high = part.astype(BF16)
        low = (part - high.astype(F32)).astype(BF16)
        side[slot * NARROW : (slot + 1) * NARROW, 0:LANES] = high
        side[slot * NARROW : (slot + 1) * NARROW, LANES : 2 * LANES] = low


def product(high, low, side):
    both = jnp.dot(high, side[...], preferred_element_type=F32)
    rest = jnp.dot(low, side[:, 0:LANES], preferred_element_type=F32)
    return both[:, 0:LANES] + (both[:, LANES:] + rest)


def build_and_apply(mask, vectors, column, points, high, low, side, first_lane):
    across = vectors.T[SITE : SITE + SUMS, :] + points[:, first_lane : first_lane + NARROW]
    across_x, across_y, across_z = across[0:1, :], across[1:2, :], across[2:3, :]

    def rows16(step):
        rows = slice(step * 16, (step + 1) * 16)
        here_x, here_y, here_z = column[0, rows, :], column[1, rows, :], column[2, rows, :]
        keep = mask[step // 2 : step // 2 + 1, :]
        for tile in range(NARROW // LANES):
            lanes = slice(tile * LANES, (tile + 1) * LANES)
            dx = here_x - across_x[:, lanes]
            dy = here_y - across_y[:, lanes]
            dz = here_z - across_z[:, lanes]
            xx = dx * dx
            yy = dy * dy
            distance2 = xx + yy + dz * dz
            square = jnp.maximum(distance2, 1.0)
            inverse = lax.rsqrt(square)
            damping = 1.0 + jnp.tanh(1.25 * (square * inverse) - 3.0)
            inverse2 = inverse * inverse
            kept = keep[:, first_lane + tile * LANES : first_lane + (tile + 1) * LANES]
            weight = damping * (inverse2 * inverse2 * inverse) * kept
            radial = weight * distance2
            minus3 = -3.0 * weight
            along_x = minus3 * dx
            along_y = minus3 * dy
            entries = (
                radial + minus3 * xx,
                radial + minus3 * yy,
                along_x * dy,
                along_x * dz,
                along_y * dz,
            )
            for slot, entry in enumerate(entries):
                top = entry.astype(BF16)
                at = slice(slot * NARROW + tile * LANES, slot * NARROW + (tile + 1) * LANES)
                high[rows, at] = top
                low[rows, at] = (entry - top.astype(F32)).astype(BF16)

    outs = []
    for chunk in range(0, WIDE, CHUNK):
        for step in range(chunk // 16, (chunk + CHUNK) // 16):
            rows16(step)
        rows = slice(chunk, chunk + CHUNK)
        outs.append(product(high[rows, :], low[rows, :], side))
    return jnp.concatenate(outs, axis=0)


def first_kernel(
    flags, points, mask, across, mine, theirs,
    part_out, high0, low0, high1, low1, own, other, column, side0, side1
):
    odd_core = flags[0:ATOMS, :] > 0.5
    odd_row = flags[ATOMS : 2 * ATOMS, :] > 0.5
    for slot in range(HALF):
        first, second = mine[slot, 0:ATOMS, :], mine[slot, ATOMS : 2 * ATOMS, :]
        third, fourth = theirs[slot, 0:ATOMS, :], theirs[slot, ATOMS : 2 * ATOMS, :]
        own[slot] = jnp.where(odd_core, first, fourth)
        other[slot] = jnp.where(odd_core, second, third)
        rows = jnp.where(odd_core, fourth, first)
        beside = pltpu.roll(rows, LANES - 4, 1)
        for block, sites in (
            (2 * slot, jnp.where(odd_row, beside, rows)),
            (2 * slot + 1, jnp.where(odd_row, rows, beside)),
        ):
            place = slice(block * ATOMS, (block + 1) * ATOMS)
            for comp in range(COMPS):
                column[comp, place, :] = points[comp, place, :] + sites[:, SITE + comp : SITE + comp + 1]

    total = jnp.zeros((WIDE, LANES), F32)
    halves = ((own, high0, low0, side0), (other, high1, low1, side1))
    for half, (gathered, high, low, right) in enumerate(halves):
        vectors = gathered[...].reshape(NARROW, LANES)
        right_side(vectors, right)
        total = total + build_and_apply(mask, vectors, column, across, high, low, right, half * NARROW)
    part_out[...] = total.reshape(GROUP, ATOMS, LANES)


def spare_sums(vectors):
    return jnp.where(lane_ids(ATOMS) < COMPS * RHS, 0.0, jnp.sum(vectors, axis=0))


def second_own_kernel(gathered, high, low, total, side):
    vectors = gathered[...]
    right_side(vectors.reshape(NARROW, LANES), side)
    out = product(high[...], low[...], side).reshape(GROUP, ATOMS, LANES) + spare_sums(vectors)[None]
    total[...] = out


def second_other_kernel(gathered, high, low, total, part_out, side):
    vectors = gathered[...]
    right_side(vectors.reshape(NARROW, LANES), side)
    out = product(high[...], low[...], side).reshape(GROUP, ATOMS, LANES) + spare_sums(vectors)[None]
    part_out[...] = total[...] + out


def shifted_kernel(parts, own, aux, out, work):
    coupled = jnp.sum(parts[...], axis=0)
    inside = lane_ids(ATOMS) < COMPS * RHS
    vector = jnp.where(inside, own[...], 0.0)
    mapped = aux[0:ATOMS, :] * vector + coupled
    sums = jnp.zeros((SUMS, LANES), F32)
    row = lax.broadcasted_iota(jnp.int32, (SUMS, LANES), 0)
    for slot, terms in enumerate((vector * vector, vector * mapped, mapped * mapped)):
        sums = jnp.where(row == slot, jnp.sum(terms, axis=0, keepdims=True), sums)
    sums = sum_components(sums)
    work[...] = jnp.zeros_like(work)
    work[SUM_ROW : SUM_ROW + SUMS, :] = pltpu.roll(sums, 4, 0)
    work[SUM_ROW + SUMS : SUM_ROW + 2 * SUMS, :] = pltpu.roll(sums, LANES - ATOMS, 1)
    payload = jnp.where(inside, mapped, work[...].T[0:ATOMS, :])
    for slot in range(HALF):
        out[slot] = payload


def second_kernel(gathered, high, low, part_out, side):
    vectors = gathered[...]
    right_side(vectors.reshape(WIDE, LANES), side)
    sums = jnp.where(lane_ids(ATOMS) < COMPS * RHS, 0.0, jnp.sum(vectors, axis=0))
    part_out[...] = product(high[...], low[...], side).reshape(GROUP, ATOMS, LANES) + sums[None]


def step_kernel(parts, own, shifted, aux, sums_out, state, work):
    total = jnp.sum(parts[...], axis=0)
    vector = own[...]
    mapped = shifted[0]
    twice = aux[0:ATOMS, :] * mapped + total
    work[...] = jnp.zeros_like(work)
    work[0:ATOMS, :] = total
    turned = work[...].T
    lane8 = lane_ids(SUMS)
    head = pltpu.roll(turned[SUM_ROW : SUM_ROW + SUMS, :], 4, 0)
    tail = pltpu.roll(turned[SUM_ROW + SUMS : SUM_ROW + 2 * SUMS, :], ATOMS, 1)
    sums = jnp.where(lane8 < ATOMS, head, jnp.where(lane8 < RHS, tail, 0.0))
    sums = sums + pltpu.roll(sums, RHS, 1) + pltpu.roll(sums, 2 * RHS, 1)
    bb, be, ee = sums[0:1, :], sums[1:2, :], sums[2:3, :]
    shift = aux[ATOMS : ATOMS + 1, :]
    bm = shift * bb + be
    step = bb / bm
    kept = be / bm
    beta = (bb * ee - be * be) / (bm * bm)
    residual = kept * vector - step * mapped
    direction = residual + beta * vector
    image = shift * direction + ((kept + beta) * mapped - step * twice)
    row = lax.broadcasted_iota(jnp.int32, (SUMS, LANES), 0)
    squares = jnp.sum(residual * residual, axis=0, keepdims=True)
    curvature = jnp.sum(direction * image, axis=0, keepdims=True)
    both = sum_components(jnp.where(row == 0, squares, jnp.where(row == 1, curvature, 0.0)))
    lane = lax.broadcasted_iota(jnp.int32, (1, LANES), 1)
    packed = jnp.where(lane < RHS, both[0:1, :], jnp.where(lane < 2 * RHS, both[1:2, :], 0.0))
    sums_out[...] = jnp.broadcast_to(packed, sums_out.shape)
    state[0] = step * vector
    state[1] = direction
    state[2] = residual
    state[3] = image


def pair_kernel(sums, swapped, out):
    out[...] = jnp.broadcast_to((sums[...] + swapped[...])[None], out.shape)


def finish_kernel(gathered, state, dipoles, residual):
    total = jnp.sum(gathered[...], axis=0)
    total = jnp.broadcast_to(jnp.sum(total, axis=0, keepdims=True), (SUMS, LANES))
    first, second, third = component_lanes(SUMS)
    up = pltpu.roll(total, RHS, 1)
    up2 = pltpu.roll(total, 2 * RHS, 1)
    down = pltpu.roll(total, LANES - RHS, 1)
    squares = jnp.where(first, total, jnp.where(second, up, up2))
    curvature = jnp.where(first, down, jnp.where(second, total, jnp.where(third, up, 1.0)))
    step = (squares / curvature)[0:1, :]
    for out, value in (
        (dipoles, state[0] + step * state[1]),
        (residual, state[2] - step * state[3]),
    ):
        for comp in range(COMPS):
            out[comp] = value[:, comp * RHS : (comp + 1) * RHS]


def shape(*dims, dtype=F32):
    return jax.ShapeDtypeStruct(dims, dtype)


def whole(*dims):
    return pl.BlockSpec(dims, lambda i: (0,) * len(dims))


def number(row, z, core):
    return row * GROUP + z * 2 + core


def trade(value, bits):
    return lax.ppermute(value, "device", [(here, here ^ bits) for here in range(GROUP * GROUP)])


def core_swap(value):
    return trade(value, 1)


def exchange(value, groups):
    return lax.all_to_all(value, "device", 0, 0, axis_index_groups=groups)


ROWS = [[number(row, z, core) for row in range(GROUP)] for z in range(HALF) for core in range(2)]
LINES = [[number(row, z, core) for z in range(HALF)] for row in range(GROUP) for core in range(2)]
CHIPS = [[number(row, z, core) for row in range(GROUP) for z in range(HALF)] for core in range(2)]
MIXED = [[number(row, z, 1) for z in range(HALF)] for row in range(GROUP)] + [
    [number(row, z, 0) for row in range(first, GROUP, 2)] for first in range(2) for z in range(HALF)
]


def local(external_field, jitter, species, alpha_table, block_cell, tile_map):
    me = lax.axis_index("device")
    ids = jnp.stack([me // GROUP, me % GROUP]).astype(jnp.int32)
    field = external_field.transpose(0, 2, 1)
    across_field = core_swap(field)
    shifts = [jnp.pad(jitter, ((0, 0), (0, LANES - ATOMS)))]
    shifts = shifts + [trade(jitter, bits) for bits in (1, GROUP, GROUP + 1)]
    cells = jnp.pad(block_cell.astype(F32)[None], ((0, SUMS - 1), (0, 0)))
    kinds = jnp.concatenate(
        [
            jnp.pad(species.astype(F32)[None], ((0, 3), (0, LANES - ATOMS))),
            jnp.pad(alpha_table.T, ((0, 0), (0, LANES - 12))),
        ]
    )
    vec, vector = pl.pallas_call(
        prepare_kernel,
        out_shape=(shape(HALF, 2 * ATOMS, LANES), shape(ATOMS, LANES)),
        in_specs=[VMEM] * 6,
        out_specs=(VMEM, VMEM),
        scratch_shapes=[SQUARE, pltpu.VMEM((ATOMS, LANES), F32)],
        compiler_params=PARAMS,
        name="prepare",
    )(*shifts, jnp.pad(field, ((0, 0), (0, 0), (0, LANES - RHS))), across_field)
    column_shape = shape(COMPS, WIDE, LANES)
    aux, mask, points, across, flags = pl.pallas_call(
        side_kernel,
        out_shape=(shape(ATOMS + SUMS, LANES), shape(GROUP, WIDE), column_shape, shape(SUMS, WIDE), shape(2 * ATOMS, LANES)),
        in_specs=[SMEM, VMEM, VMEM, VMEM],
        out_specs=(VMEM,) * 5,
        scratch_shapes=[SQUARE],
        compiler_params=PARAMS,
        name="side",
    )(ids, kinds, cells, tile_map)
    mine, aux, mask, points, across, flags = lax.optimization_barrier(
        (exchange(vec, MIXED), aux, mask, points, across, flags)
    )
    side = pltpu.VMEM((PAIRS * NARROW, 2 * LANES), BF16)
    half = pltpu.VMEM((HALF, ATOMS, LANES), F32)
    tile = shape(WIDE, PAIRS * NARROW, dtype=BF16)
    part, high0, low0, high1, low1 = pl.pallas_call(
        first_kernel,
        out_shape=(shape(GROUP, ATOMS, LANES), tile, tile, tile, tile),
        in_specs=[VMEM] * 6,
        out_specs=(VMEM,) * 5,
        scratch_shapes=[half, half, pltpu.VMEM((COMPS, WIDE, LANES), F32), side, side],
        compiler_params=PARAMS,
        name="first",
    )(flags, points, mask, across, mine, core_swap(mine))
    parts = exchange(part, ROWS)
    blocks = whole(GROUP, ATOMS, LANES)
    block = whole(1, ATOMS, LANES)
    shifted = pl.pallas_call(
        shifted_kernel,
        grid=(1,),
        out_shape=shape(HALF, ATOMS, LANES),
        in_specs=[blocks, whole(ATOMS, LANES), whole(ATOMS + SUMS, LANES)],
        out_specs=whole(HALF, ATOMS, LANES),
        scratch_shapes=[SQUARE],
        compiler_params=PARAMS,
        name="shifted",
    )(parts, vector, aux)
    own2 = exchange(shifted, LINES)
    other2 = core_swap(own2)
    total2 = pl.pallas_call(
        second_own_kernel,
        out_shape=shape(GROUP, ATOMS, LANES),
        in_specs=[VMEM] * 3,
        out_specs=VMEM,
        scratch_shapes=[side],
        compiler_params=PARAMS,
        name="second_own",
    )(own2, high0, low0)
    part2 = pl.pallas_call(
        second_other_kernel,
        out_shape=shape(GROUP, ATOMS, LANES),
        in_specs=[VMEM] * 4,
        out_specs=VMEM,
        scratch_shapes=[side],
        compiler_params=PARAMS,
        name="second_other",
    )(other2, high1, low1, total2)
    parts2 = exchange(part2, ROWS)
    sums, state = pl.pallas_call(
        step_kernel,
        grid=(1,),
        out_shape=(shape(SUMS, LANES), shape(4, ATOMS, LANES)),
        in_specs=[blocks, whole(ATOMS, LANES), block, whole(ATOMS + SUMS, LANES)],
        out_specs=(whole(SUMS, LANES), whole(4, ATOMS, LANES)),
        scratch_shapes=[SQUARE],
        compiler_params=PARAMS,
        name="step",
    )(parts2, vector, shifted, aux)
    pair = pl.pallas_call(
        pair_kernel,
        out_shape=shape(GROUP, SUMS, LANES),
        in_specs=[VMEM, VMEM],
        out_specs=VMEM,
        compiler_params=PARAMS,
        name="pair",
    )(sums, core_swap(sums))
    pair = pair.reshape(GROUP * HALF, 1, LANES)
    all_sums = exchange(pair, CHIPS).reshape(GROUP, SUMS, LANES)
    dipoles, residual = pl.pallas_call(
        finish_kernel,
        out_shape=(shape(COMPS, ATOMS, RHS), shape(COMPS, ATOMS, RHS)),
        in_specs=[VMEM, VMEM],
        out_specs=(VMEM, VMEM),
        compiler_params=PARAMS,
        name="finish",
    )(all_sums, state)
    return dipoles.transpose(0, 2, 1), residual.transpose(0, 2, 1)


def solution(mesh):
    flat = Mesh(mesh.devices.reshape(GROUP * GROUP), ("device",))
    every = "device"
    return jax.shard_map(
        local,
        mesh=flat,
        in_specs=(P(None, None, every), P(None, every), P(every), P(), P(), P()),
        out_specs=(P(None, None, every), P(None, None, every)),
        check_vma=False,
    )
```
